32 devices in a mesh: dp: 16 (over z, y, x), mp: 2 (over core).
Axes of the slice: x: 2, y: 2, z: 4, core: 2. Of those that a mesh axis runs over, the one named last changes fastest.
Arguments:
- tokens: bfloat16 [1536, 16, 1024], P('mp', 'dp'), may hold values from -6 to 6
- segment_ids: int32 [16, 1536], P('dp'), may hold values from 0 to 1, as said below
- keep_mask: int32 [16, 1536], P('dp'), may hold values from 0 to 1, as said below
- w_query: bfloat16 [1024, 1024], P(None, 'mp'), may hold values from -0.375 to 0.375
- w_key: bfloat16 [1024, 1024], P(None, 'mp'), may hold values from -0.1875 to 0.1875
- w_value: bfloat16 [1024, 1024], P(None, 'mp'), may hold values from -0.1875 to 0.1875
- w_out: bfloat16 [1024, 1024], P('mp'), may hold values from -1 to 1
- w_gate: bfloat16 [1024, 2816], P(None, 'mp'), may hold values from -0.1875 to 0.1875
- w_up: bfloat16 [1024, 2816], P(None, 'mp'), may hold values from -0.1875 to 0.1875
- w_down: bfloat16 [2816, 1024], P('mp'), may hold values from -0.109375 to 0.109375
- norm_attn: float32 [1024], replicated, may hold values from 0.25 to 1.75
- norm_ffn: float32 [1024], replicated, may hold values from 0.25 to 1.75
- cotangent: bfloat16 [1536, 16, 1024], P('mp', 'dp'), may hold values from -6 to 6
Outputs:
- result: bfloat16 [1536, 16, 1024], P('mp', 'dp')
- grad_tokens: bfloat16 [1536, 16, 1024], P('mp', 'dp')
- grad_w_query: float32 [1024, 1024], P(None, 'mp')
- grad_w_key: float32 [1024, 1024], P(None, 'mp')
- grad_w_value: float32 [1024, 1024], P(None, 'mp')
- grad_w_out: float32 [1024, 1024], P('mp')
- grad_w_gate: float32 [1024, 2816], P(None, 'mp')
- grad_w_up: float32 [1024, 2816], P(None, 'mp')
- grad_w_down: float32 [2816, 1024], P('mp')
- grad_norm_attn: float32 [1024], replicated
- grad_norm_ffn: float32 [1024], replicated
The draws below stay inside these ranges and needn't reach their ends.
Inputs may be any that keep to these rules, and one draw needn't show every extreme that they name: `segment_ids`: each packed row holds one source row of 1152 tokens starting at token 0 or 384; the other 384 tokens are one source row with its own id, or padding that carries the long row's id. `keep_mask`: 0 exactly on the padding described for segment_ids.
All inputs are finite; a program needn't handle non-finite values.
Results may differ from the reference program's by a relative error of at most 0.019.
The reference program's roundings to bfloat16 on the way count: a program that leaves them out, or rounds other values in their place, can miss the bound.
Values may be sent and summed in bfloat16 or wider, within the bound.
No kernel may reach another device: no remote copies, remote signals or barrier semaphores. Data moves between devices by JAX's collectives and lax.ppermute only.
A program may use at most 256 MiB of HBM per device.

```python
import jax
import jax.numpy as jnp
from jax import lax

D = 1024
HEADS = 16
HDIM = 64
FF = 2816
SLOT = 384
PACK = 1536
ROWS = 16


def pack_layout(key):
    start_key, fill_key = jax.random.split(key)
    start_slot = jax.random.randint(start_key, (ROWS, 1), 0, 2)
    short_here = jax.random.randint(fill_key, (ROWS, 1), 0, 2)
    slot_index = (jnp.arange(PACK, dtype=jnp.int32) // SLOT)[None, :]
    in_long = (slot_index >= start_slot) & (slot_index < start_slot + 3)
    segment = jnp.where(in_long, start_slot, 1 - start_slot)
    keep_flag = jnp.where(in_long | (short_here > 0), 1, 0)
    segment = jnp.where(keep_flag > 0, segment, start_slot)
    return (segment.astype(jnp.int32), keep_flag.astype(jnp.int32))


def draw_segment_ids(key, part):
    return pack_layout(key)[0]


def draw_keep_mask(key, part):
    return pack_layout(key)[1]


def steps_of(own_key, dims, pieces, smallest, largest):
    loudness = 1.0
    for axis_at, parts in pieces:
        draws = jax.random.uniform(jax.random.fold_in(jax.random.fold_in(own_key, 6), axis_at), (parts,), jnp.float32, smallest / len(pieces), largest / len(pieces))
        loudness = loudness * jnp.repeat(jnp.exp(draws), dims[axis_at] // parts).reshape((-1,) + (1,) * (len(dims) - 1 - axis_at))
    return loudness


def centred(own_key, dims, width, limit, cuts=(), kind=jnp.bfloat16):
    result = width * jax.random.normal(own_key, dims, jnp.float32)
    if cuts:
        result = result * steps_of(own_key, dims, cuts, -0.22, 0.18)
    return jnp.clip(result, -limit, limit).astype(kind)


def setup_inputs(seed: int = 0) -> dict:
    splits = jax.random.split(jax.random.key(seed), 14)
    return {
        "tokens": centred(splits[0], (PACK, ROWS, D), 1.0, 6.0, ((0, 2), (1, 16))),
        "segment_ids": draw_segment_ids(jax.random.fold_in(splits[13], 71), 0),
        "keep_mask": draw_keep_mask(jax.random.fold_in(splits[13], 71), 0),
        "w_query": centred(splits[3], (D, HEADS * HDIM), (D // 4) ** -0.5, 0.375, ((1, 2),)),
        "w_key": centred(splits[4], (D, HEADS * HDIM), D ** -0.5, 0.1875, ((1, 2),)),
        "w_value": centred(splits[5], (D, HEADS * HDIM), D ** -0.5, 0.1875, ((1, 2),)),
        "w_out": centred(splits[6], (HEADS * HDIM, D), (HEADS * HDIM // 32) ** -0.5, 1.0, ((0, 2),)),
        "w_gate": centred(splits[7], (D, FF), D ** -0.5, 0.1875, ((1, 2),)),
        "w_up": centred(splits[8], (D, FF), D ** -0.5, 0.1875, ((1, 2),)),
        "w_down": centred(splits[9], (FF, D), FF ** -0.5, 0.109375, ((0, 2),)),
        "norm_attn": jnp.clip(1.0 + 0.15 * jax.random.normal(splits[10], (D,), jnp.float32), 0.25, 1.75),
        "norm_ffn": jnp.clip(1.0 + 0.15 * jax.random.normal(splits[11], (D,), jnp.float32), 0.25, 1.75),
        "cotangent": centred(splits[12], (PACK, ROWS, D), 1.0, 6.0, ((0, 2), (1, 16))),
    }


EPSILON = 1e-06
MASKED_SCORE = -1e+30

@jax.custom_vjp
def low(v):
    return lax.optimization_barrier(v.astype(jnp.bfloat16)).astype(jnp.float32)

@jax.custom_vjp
def low_back(v):
    return v

def low_keep(v):
    return (low(v), None)

def low_pass(kept, grad):
    return (grad,)

def back_keep(v):
    return (v, None)

def back_low(kept, grad):
    return (low(grad),)
low.defvjp(low_keep, low_pass)
low_back.defvjp(back_keep, back_low)

def round_both(value):
    return low(low_back(value))

def matmul_hi(form, left, right):
    return jnp.einsum(form, left, right, precision=lax.Precision.HIGHEST)

def normalize(value, gain):
    return value * lax.rsqrt(lax.optimization_barrier(jnp.mean(value * value, axis=-1, keepdims=True)) + EPSILON) * gain

def attend_block(query_block, key_heads, value_heads, seg_block, segments, keep_row):
    scores = low_back(matmul_hi('qhd,khd->hqk', query_block, key_heads) * HDIM ** (-0.5))
    allowed = (seg_block[:, None] == segments[None, :]) & (keep_row[None, :] > 0)
    scores = jnp.where(allowed[None], scores, MASKED_SCORE)
    highest = lax.optimization_barrier(jnp.max(scores, axis=-1, keepdims=True))
    raised = jnp.exp(scores - highest)
    probs = raised / lax.optimization_barrier(jnp.sum(raised, axis=-1, keepdims=True))
    return matmul_hi('hqk,khd->qhd', low(probs), value_heads)

def layer_row(residual, segments, keep_row, weights):
    w_query, w_key, w_value, w_out, w_gate, w_up, w_down, norm_attn, norm_ffn = weights
    attn_normed = low(normalize(residual, norm_attn))
    query = round_both(matmul_hi('ld,de->le', attn_normed, w_query))
    keys = round_both(matmul_hi('ld,de->le', attn_normed, w_key))
    values = round_both(matmul_hi('ld,de->le', attn_normed, w_value))
    block_len = min(512, PACK)
    block_count = PACK // block_len
    key_heads = keys.reshape(PACK, HEADS, HDIM)
    value_heads = values.reshape(PACK, HEADS, HDIM)
    query_blocks = query.reshape(block_count, block_len, HEADS, HDIM)
    seg_blocks = segments.reshape(block_count, block_len)
    block_fn = jax.checkpoint(attend_block)
    mixed = lax.map(lambda inputs: block_fn(inputs[0], key_heads, value_heads, inputs[1], segments, keep_row), (query_blocks, seg_blocks))
    mixed = round_both(mixed.reshape(PACK, HEADS * HDIM))
    hidden_state = residual + low_back(matmul_hi('le,ed->ld', mixed, w_out))
    ffn_normed = low(normalize(hidden_state, norm_ffn))
    gate_proj = low_back(matmul_hi('ld,df->lf', ffn_normed, w_gate))
    up_proj = low_back(matmul_hi('ld,df->lf', ffn_normed, w_up))
    activated = low(jax.nn.gelu(gate_proj, approximate=True) * up_proj)
    return hidden_state + low_back(matmul_hi('lf,fd->ld', activated, w_down))

def reference(tokens, segment_ids, keep_mask, w_query, w_key, w_value, w_out, w_gate, w_up, w_down, norm_attn, norm_ffn, cotangent):
    weights = (w_query.astype(jnp.float32), w_key.astype(jnp.float32), w_value.astype(jnp.float32), w_out.astype(jnp.float32), w_gate.astype(jnp.float32), w_up.astype(jnp.float32), w_down.astype(jnp.float32), norm_attn.astype(jnp.float32), norm_ffn.astype(jnp.float32))
    residuals = jnp.moveaxis(tokens.astype(jnp.float32), 1, 0)
    cotangents = jnp.moveaxis(cotangent.astype(jnp.float32), 1, 0)

    def row_step(summed, inputs):
        residual, segments, keep_row, grad_row = inputs

        def forward(value, params):
            return layer_row(value, segments, keep_row, params)
        output, pull = jax.vjp(forward, residual, weights)
        grad_input, grad_params = pull(grad_row)
        summed = jax.tree.map(jnp.add, summed, grad_params)
        return (summed, (output.astype(jnp.bfloat16), grad_input.astype(jnp.bfloat16)))
    initial = jax.tree.map(jnp.zeros_like, weights)
    summed, (outputs, grad_inputs) = lax.scan(row_step, initial, (residuals, segment_ids, keep_mask, cotangents))
    return (jnp.moveaxis(outputs, 0, 1), jnp.moveaxis(grad_inputs, 0, 1), summed[0], summed[1], summed[2], summed[3], summed[4], summed[5], summed[6], summed[7], summed[8])
```

```python
import functools

import jax
import jax.numpy as jnp
from jax import lax
from jax.experimental import pallas as pl
from jax.experimental.pallas import tpu as pltpu
from jax.sharding import PartitionSpec as P

HDIM = 64
EPSILON = 1e-06
LOG2E = 1.4426950408889634
BF = jnp.bfloat16
F32 = jnp.float32
VMEM_LIMIT = 58 * 1024 * 1024
NN = ((1,), (0,))
NT = ((1,), (1,))
FFN_CHUNKS = (384, 512, 512)


def dot(left, right, dims=NN):
    return lax.dot_general(left, right, (dims, ((), ())), preferred_element_type=F32)


def params():
    return pltpu.CompilerParams(vmem_limit_bytes=VMEM_LIMIT)


def cost(flops, moved):
    return pl.CostEstimate(flops=flops, bytes_accessed=moved, transcendentals=0)


def shape(dims, dtype):
    return jax.ShapeDtypeStruct(dims, dtype)


def qkv_kernel(tokens, gain, wq, wk, wv, *refs):
    projected, normed_t = refs[-2:]
    x = tokens[...].astype(F32)
    r = lax.rsqrt(jnp.mean(x * x, axis=-1, keepdims=True) + EPSILON)
    low = (x * r * gain[...]).astype(BF)
    width = wq.shape[1]
    for at, w in enumerate((wq, wk, wv)):
        projected[:, at * width : (at + 1) * width] = dot(low, w[...]).astype(BF)
    normed_t[...] = low.T


def project(tokens, gain, wq, wk, wv, half, before=None):
    rows, d = tokens.shape
    width = wq.shape[1]
    tile = rows // 2
    whole = lambda a: pl.BlockSpec(a.shape, lambda i: (0, 0))
    args = [tokens, gain, wq, wk, wv]
    specs = [pl.BlockSpec((tile, d), lambda i: (i, 0))] + [whole(a) for a in args[1:]]
    alias = {}
    if before is not None:
        args += list(before)
        specs += [pl.BlockSpec(memory_space=pl.ANY)] * 2
        alias = {5: 0, 6: 1}
    return pl.pallas_call(
        qkv_kernel,
        grid=(2,),
        in_specs=specs,
        out_specs=[
            pl.BlockSpec((tile, 3 * width), lambda i: (i + 2 * half, 0)),
            pl.BlockSpec((d, tile), lambda i: (0, i + 2 * half)),
        ],
        out_shape=[shape((2 * rows, 3 * width), BF), shape((d, 2 * rows), BF)],
        input_output_aliases=alias,
        compiler_params=params(),
        cost_estimate=cost(2 * rows * d * 3 * width, 8 * rows * d),
    )(*args)


def slot_rows(meta, logical, slot):
    return pl.ds(pl.multiple_of(meta[logical] * slot, slot), slot)


def two_heads(columns):
    slot = columns.shape[1]
    zero = jnp.zeros((HDIM, slot), BF)
    first = jnp.concatenate([columns[:HDIM], zero], 0)
    second = jnp.concatenate([zero, columns[HDIM:]], 0)
    return jnp.concatenate([first, second], 1)


def attend_kernel(meta, q_ref, k_ref, v_ref, o_ref, ot_ref, lse_ref, *, slot):
    scale = HDIM**-0.5 * LOG2E
    padded = meta[4]
    rows = lambda logical: slot_rows(meta, logical, slot)

    def attend(at, key_slots):
        q2 = two_heads(q_ref[rows(at), :].T)
        scores = [dot(k_ref[rows(j), :], q2) for j in key_slots]
        top = functools.reduce(
            jnp.maximum, [jnp.max(s, axis=0, keepdims=True) for s in scores]
        )
        one = jnp.ones((16, slot), BF)
        oa = jnp.zeros((HDIM + 16, slot), F32)
        ob = oa
        for j, s in zip(key_slots, scores):
            p = jnp.exp2((s - top) * scale).astype(BF)
            vt = v_ref[rows(j), :].T
            oa += dot(jnp.concatenate([vt[:HDIM], one], 0), p[:, :slot])
            ob += dot(jnp.concatenate([vt[HDIM:], one], 0), p[:, slot:])
        la, lb = oa[HDIM : HDIM + 1], ob[HDIM : HDIM + 1]
        ot = jnp.concatenate([oa[:HDIM] / la, ob[:HDIM] / lb], 0).astype(BF)
        ot_ref[:, rows(at)] = ot
        o_ref[rows(at), :] = ot.T
        lse = top * HDIM**-0.5 + jnp.log(jnp.concatenate([la, lb], 1))
        lse_ref[0, 0:1, rows(at)] = lse[:, :slot]
        lse_ref[0, 1:2, rows(at)] = lse[:, slot:]

    lax.fori_loop(0, 3 + padded, lambda i, c: (attend(i, (0, 1, 2)), c)[1], 0)

    @pl.when(padded == 0)
    def _():
        attend(3, (3,))


def attend(meta, qkv):
    seq, width = qkv.shape[0], qkv.shape[1] // 3
    pairs = width // 128
    column = lambda off: pl.BlockSpec((seq, 128), lambda p, m: (0, p + off))
    return pl.pallas_call(
        functools.partial(attend_kernel, slot=seq // 4),
        grid_spec=pltpu.PrefetchScalarGridSpec(
            num_scalar_prefetch=1,
            grid=(pairs,),
            in_specs=[column(0), column(pairs), column(2 * pairs)],
            out_specs=[
                column(0),
                pl.BlockSpec((128, seq), lambda p, m: (p, 0)),
                pl.BlockSpec((1, 2, seq), lambda p, m: (p, 0, 0)),
            ],
        ),
        out_shape=[shape((seq, width), BF), shape((width, seq), BF), shape((pairs, 2, seq), F32)],
        compiler_params=params(),
        cost_estimate=cost(20 * seq * seq * width, 5 * seq * width * 2),
    )(meta, qkv, qkv, qkv)


def attend_back_kernel(
    meta, q_ref, k_ref, v_ref, ot_ref, do_ref, lse_ref, dq_ref, dk_ref, dv_ref, dk_sum, dv_sum, *, slot
):
    scale = HDIM**-0.5 * LOG2E
    padded = meta[4]
    rows = lambda logical: slot_rows(meta, logical, slot)
    lane = lax.broadcasted_iota(jnp.int32, (slot, 128), 1)
    ones = jnp.ones((slot, 128), BF)

    def stacked(x):
        zero = jnp.zeros_like(x)
        return jnp.concatenate([jnp.where(lane < HDIM, x, zero), jnp.where(lane < HDIM, zero, x)], 0)

    def extended(columns, tail):
        high = tail.astype(BF).astype(F32)
        rest = tail - high
        middle = rest.astype(BF).astype(F32)
        extra = jnp.concatenate(
            [high, middle, rest - middle, jnp.zeros((125, 2 * slot), F32)], 0
        ).astype(BF)
        return jnp.concatenate([two_heads(columns), extra], 0)

    def attend(at, key_slots, first):
        q, do = q_ref[rows(at), :], do_ref[rows(at), :]
        do_t = do.T
        prod = do_t.astype(F32) * ot_ref[:, rows(at)].astype(F32)
        delta = jnp.concatenate(
            [jnp.sum(prod[:HDIM], 0, keepdims=True), jnp.sum(prod[HDIM:], 0, keepdims=True)], 1
        )
        lse = jnp.concatenate([lse_ref[0, 0:1, rows(at)], lse_ref[0, 1:2, rows(at)]], 1)
        q2 = extended(q.T, lse * -(HDIM**0.5))
        do2 = extended(do_t, -delta)
        qs, dos = stacked(q), stacked(do)
        dqa = jnp.zeros((HDIM, slot), F32)
        dqb = dqa
        for j in key_slots:
            k, v = k_ref[rows(j), :], v_ref[rows(j), :]
            p = jnp.exp2(dot(jnp.concatenate([k, ones], 1), q2) * scale)
            dp = dot(jnp.concatenate([v, ones], 1), do2)
            ds = (p * dp).astype(BF)
            dv = dot(p.astype(BF), dos)
            dk = dot(ds, qs)
            kt = k.T
            dqa += dot(kt[:HDIM], ds[:, :slot])
            dqb += dot(kt[HDIM:], ds[:, slot:])
            if first:
                dk_sum[rows(j), :] = dk
                dv_sum[rows(j), :] = dv
            else:
                dk_sum[rows(j), :] += dk
                dv_sum[rows(j), :] += dv
        dq_ref[rows(at), :] = (jnp.concatenate([dqa, dqb], 0) * HDIM**-0.5).astype(BF).T

    dk_sum[...] = jnp.zeros_like(dk_sum)
    dv_sum[...] = jnp.zeros_like(dv_sum)
    lax.fori_loop(0, 3 + padded, lambda i, c: (attend(i, (0, 1, 2), False), c)[1], 0)

    @pl.when(padded == 0)
    def _():
        attend(3, (3,), True)

    dk_ref[...] = (dk_sum[...] * HDIM**-0.5).astype(BF)
    dv_ref[...] = dv_sum[...].astype(BF)


def attend_back(meta, qkv, mixed_t, grad_mixed, lse):
    seq, width = qkv.shape[0], qkv.shape[1] // 3
    pairs = width // 128
    column = lambda off: pl.BlockSpec((seq, 128), lambda p, m: (0, p + off))
    return pl.pallas_call(
        functools.partial(attend_back_kernel, slot=seq // 4),
        grid_spec=pltpu.PrefetchScalarGridSpec(
            num_scalar_prefetch=1,
            grid=(pairs,),
            in_specs=[
                column(0),
                column(pairs),
                column(2 * pairs),
                pl.BlockSpec((128, seq), lambda p, m: (p, 0)),
                column(0),
                pl.BlockSpec((1, 2, seq), lambda p, m: (p, 0, 0)),
            ],
            out_specs=[column(0)] * 3,
            scratch_shapes=[pltpu.VMEM((seq, 128), F32)] * 2,
        ),
        out_shape=[shape((seq, width), BF)] * 3,
        compiler_params=params(),
        cost_estimate=cost(30 * seq * seq * width, 8 * seq * width * 2),
    )(meta, qkv, qkv, qkv, mixed_t, grad_mixed, lse)


def matmul_kernel(a, b, out, *, dims):
    out[...] = dot(a[...], b[...], dims).astype(out.dtype)


def matmul_rows(a, b, dims, dtype, tile=256):
    rows, depth = a.shape
    width = b.shape[1] if dims == NN else b.shape[0]
    return pl.pallas_call(
        functools.partial(matmul_kernel, dims=dims),
        grid=(rows // tile,),
        in_specs=[pl.BlockSpec((tile, depth), lambda i: (i, 0)), pl.BlockSpec(b.shape, lambda i: (0, 0))],
        out_specs=pl.BlockSpec((tile, width), lambda i: (i, 0)),
        out_shape=shape((rows, width), dtype),
        compiler_params=params(),
        cost_estimate=cost(2 * rows * depth * width, 2 * (rows * depth + depth * width + rows * width)),
    )(a, b)


def middle_kernel(own, other, mine, theirs, gain, hidden, normed, normed_t):
    tokens = jnp.where(pl.program_id(0) < pl.num_programs(0) // 2, own[...], other[...]).astype(F32)
    h = tokens + (mine[...].astype(F32) + theirs[...].astype(F32))
    r = lax.rsqrt(jnp.mean(h * h, axis=-1, keepdims=True) + EPSILON)
    low = (h * r * gain[...]).astype(BF)
    hidden[...] = h
    normed[...] = low
    normed_t[...] = low.T


def middle(own, other, mine, theirs, gain, tile=256):
    half, d = own.shape
    n = 2 * half // tile
    block = lambda f: pl.BlockSpec((tile, d), lambda i: (f(i), 0))
    return pl.pallas_call(
        middle_kernel,
        grid=(n,),
        in_specs=[
            block(lambda i: jnp.minimum(i, n // 2 - 1)),
            block(lambda i: jnp.maximum(i - n // 2, 0)),
            block(lambda i: i),
            block(lambda i: lax.rem(i + n // 2, n)),
            pl.BlockSpec((1, d), lambda i: (0, 0)),
        ],
        out_specs=[block(lambda i: i), block(lambda i: i), pl.BlockSpec((d, tile), lambda i: (0, i))],
        out_shape=[shape((2 * half, d), F32), shape((2 * half, d), BF), shape((d, 2 * half), BF)],
        compiler_params=params(),
        cost_estimate=cost(20 * half * d, 30 * half * d),
    )(own, other, mine, theirs, gain)


def gelu_parts(v):
    c = 0.7978845608028654
    t = jnp.tanh(c * (v + 0.044715 * v * v * v))
    value = 0.5 * v * (1.0 + t)
    slope = 0.5 * (1.0 + t) + 0.5 * v * (1.0 - t * t) * (c * (1.0 + 3 * 0.044715 * v * v))
    return value, slope


def ffn_kernel(quarters, x, ct, xt, ctq, wg, wu, wd, act, gg, gu, grads, both, act_t):
    at = pl.program_id(0)
    rows, width = act.shape

    @pl.when(at < 4)
    def _():
        gate = dot(x[...], wg[...])
        up = dot(x[...], wu[...])
        grad_act = dot(ct[...], wd[...], NT)
        value, slope = gelu_parts(gate)
        low = (value * up).astype(BF)
        grad_gate = (grad_act * up * slope).astype(BF)
        grad_up = (grad_act * value).astype(BF)
        act[...] = low
        gg[...] = grad_gate
        gu[...] = grad_up
        here = pl.ds(pl.multiple_of(at * rows, rows), rows)
        both[here, :width] = grad_gate
        both[here, width:] = grad_up
        act_t[:, here] = low.T

    @pl.when(at >= 4)
    def _():
        grads[0, :, : 2 * width] = dot(xt[...], both[...]).astype(BF)
        down = dot(act_t[...], ctq[...]).astype(BF)
        for i in range(width // 128):
            tile = down[i * 128 : (i + 1) * 128]
            grads[0, :128, i * 128 + 2 * width : (i + 1) * 128 + 2 * width] = tile[:, :128]
            grads[0, 128:, i * 128 + 2 * width : (i + 1) * 128 + 2 * width] = tile[:, 128:]


def ffn(quarters, x, ct, xt, wg, wu, wd):
    seq, d = x.shape
    width = wg.shape[1]
    tile = seq // 4
    early = lambda s, q: jnp.minimum(s, 3)
    late = lambda s, q: q[jnp.maximum(s - 4, 0)]
    rows = pl.BlockSpec((tile, d), lambda s, q: (early(s, q), 0))
    low = pl.BlockSpec((tile, width), lambda s, q: (early(s, q), 0))
    return pl.pallas_call(
        ffn_kernel,
        grid_spec=pltpu.PrefetchScalarGridSpec(
            num_scalar_prefetch=1,
            grid=(8,),
            in_specs=[
                rows,
                rows,
                pl.BlockSpec((d // 4, seq), lambda s, q: (late(s, q), 0)),
                pl.BlockSpec((seq, d // 4), lambda s, q: (0, late(s, q))),
                pl.BlockSpec((d, width), lambda s, q: (0, 0)),
                pl.BlockSpec((d, width), lambda s, q: (0, 0)),
                pl.BlockSpec((width, d), lambda s, q: (0, 0)),
            ],
            out_specs=[
                low,
                low,
                low,
                pl.BlockSpec((1, d // 4, 3 * width), lambda s, q: (jnp.maximum(s - 4, 0), 0, 0)),
            ],
            scratch_shapes=[pltpu.VMEM((seq, 2 * width), BF), pltpu.VMEM((width, seq), BF)],
        ),
        out_shape=[shape((seq, width), BF)] * 3 + [shape((4, d // 4, 3 * width), BF)],
        compiler_params=params(),
        cost_estimate=cost(12 * seq * d * width, 8 * seq * d + 12 * d * width),
    )(quarters, x, ct, xt, ct, wg, wu, wd)


def ffn_sums_kernel(*refs, chunks):
    acts, ggs, gus = refs[:chunks], refs[chunks : 2 * chunks], refs[2 * chunks : 3 * chunks]
    wg, wu, wd, own, send, back = refs[3 * chunks :]
    act = jnp.concatenate([a[...] for a in acts], 1)
    out = dot(act, wd[...])
    gg = jnp.concatenate([a[...] for a in ggs], 1)
    gu = jnp.concatenate([a[...] for a in gus], 1)
    back[...] = (dot(gg, wg[...], NT) + dot(gu, wu[...], NT)).astype(BF)
    late = pl.program_id(0) >= pl.num_programs(0) // 2

    @pl.when(late)
    def _():
        own[...] = out

    @pl.when(jnp.logical_not(late))
    def _():
        send[...] = out.astype(BF)


def ffn_sums(acts, ggs, gus, wg, wu, wd, tile=256):
    seq, d = acts[0].shape[0], wd.shape[1]
    n = seq // tile
    row = lambda i: lax.rem(i + n // 2, n)
    whole = lambda a: pl.BlockSpec(a.shape, lambda i: (0, 0))
    return pl.pallas_call(
        functools.partial(ffn_sums_kernel, chunks=len(acts)),
        grid=(n,),
        in_specs=[pl.BlockSpec((tile, a.shape[1]), lambda i: (row(i), 0)) for a in acts + ggs + gus]
        + [whole(wg), whole(wu), whole(wd)],
        out_specs=[
            pl.BlockSpec((tile, d), lambda i: (jnp.maximum(i - n // 2, 0), 0)),
            pl.BlockSpec((tile, d), lambda i: (jnp.minimum(i, n // 2 - 1), 0)),
            pl.BlockSpec((tile, d), lambda i: (row(i), 0)),
        ],
        out_shape=[shape((seq // 2, d), F32), shape((seq // 2, d), BF), shape((seq, d), BF)],
        compiler_params=params(),
        cost_estimate=cost(6 * seq * d * wg.shape[1], 10 * seq * d + 6 * d * wg.shape[1]),
    )(*acts, *ggs, *gus, wg, wu, wd)


def norm_back(value, gain, grad):
    r = lax.rsqrt(jnp.mean(value * value, axis=-1, keepdims=True) + EPSILON)
    u = grad * gain
    inner = jnp.mean(u * value, axis=-1, keepdims=True)
    return r * u - value * (r * r * r * inner), jnp.sum(grad * value * r, axis=0, keepdims=True)


def middle_back_kernel(mine, theirs, hidden, ct, gain, low, keep, gain_grad):
    at = pl.program_id(0)
    grad = mine[...].astype(F32) + theirs[...].astype(F32)
    through, part = norm_back(hidden[...], gain[...], grad)
    total = ct[...].astype(F32) + through
    low[...] = total.astype(BF)

    @pl.when(at == 0)
    def _():
        gain_grad[...] = part

    @pl.when(at > 0)
    def _():
        gain_grad[...] += part

    @pl.when(at < pl.num_programs(0) // 2)
    def _():
        keep[...] = total


def middle_back(mine, theirs, hidden, ct, gain, tile=256):
    seq, d = hidden.shape
    n = seq // tile
    block = lambda f: pl.BlockSpec((tile, d), lambda i: (f(i), 0))
    return pl.pallas_call(
        middle_back_kernel,
        grid=(n,),
        in_specs=[
            block(lambda i: i),
            block(lambda i: lax.rem(i + n // 2, n)),
            block(lambda i: i),
            block(lambda i: i),
            pl.BlockSpec((1, d), lambda i: (0, 0)),
        ],
        out_specs=[
            block(lambda i: i),
            block(lambda i: jnp.minimum(i, n // 2 - 1)),
            pl.BlockSpec((1, d), lambda i: (0, 0)),
        ],
        out_shape=[shape((seq, d), BF), shape((seq // 2, d), F32), shape((1, d), F32)],
        compiler_params=params(),
        cost_estimate=cost(20 * seq * d, 14 * seq * d),
    )(mine, theirs, hidden, ct, gain)


def out_back_kernel(quarters, g, gq, mixed_t, w_out, grad_mixed, grads):
    at = pl.program_id(0)

    @pl.when(at < 4)
    def _():
        grad_mixed[...] = dot(g[...], w_out[...], NT).astype(BF)

    @pl.when(at >= 4)
    def _():
        part = dot(mixed_t[...], gq[...]).astype(BF)
        step = grads.shape[1]
        for i in range(part.shape[0] // step):
            grads[0, :, i * part.shape[1] : (i + 1) * part.shape[1]] = part[i * step : (i + 1) * step]


def out_back(quarters, g, mixed_t, w_out):
    seq, d = g.shape
    width = w_out.shape[0]
    late = lambda s, q: q[jnp.maximum(s - 4, 0)]
    return pl.pallas_call(
        out_back_kernel,
        grid_spec=pltpu.PrefetchScalarGridSpec(
            num_scalar_prefetch=1,
            grid=(8,),
            in_specs=[
                pl.BlockSpec((seq // 4, d), lambda s, q: (jnp.minimum(s, 3), 0)),
                pl.BlockSpec((seq, d // 4), lambda s, q: (0, late(s, q))),
                pl.BlockSpec((width, seq), lambda s, q: (0, 0)),
                pl.BlockSpec((width, d), lambda s, q: (0, 0)),
            ],
            out_specs=[
                pl.BlockSpec((seq // 4, width), lambda s, q: (jnp.minimum(s, 3), 0)),
                pl.BlockSpec((1, d // 4, width), lambda s, q: (jnp.maximum(s - 4, 0), 0, 0)),
            ],
        ),
        out_shape=[shape((seq, width), BF), shape((4, d // 4, width), BF)],
        compiler_params=params(),
        cost_estimate=cost(4 * seq * d * width, 6 * seq * d),
    )(quarters, g, g, mixed_t, w_out)


def qkv_grads_kernel(quarters, normed_t, dq, dk, dv, grads):
    width = dq.shape[1]
    for at, part in enumerate((dq, dk, dv)):
        grads[0, :, at * width : (at + 1) * width] = dot(normed_t[...], part[...]).astype(BF)


def qkv_grads(quarters, normed_t, dq, dk, dv):
    d, seq = normed_t.shape
    width = dq.shape[1]
    whole = pl.BlockSpec((seq, width), lambda s, q: (0, 0))
    return pl.pallas_call(
        qkv_grads_kernel,
        grid_spec=pltpu.PrefetchScalarGridSpec(
            num_scalar_prefetch=1,
            grid=(4,),
            in_specs=[pl.BlockSpec((d // 4, seq), lambda s, q: (q[s], 0)), whole, whole, whole],
            out_specs=pl.BlockSpec((1, d // 4, 3 * width), lambda s, q: (s, 0, 0)),
        ),
        out_shape=shape((4, d // 4, 3 * width), BF),
        compiler_params=params(),
        cost_estimate=cost(6 * seq * d * width, 8 * seq * d),
    )(quarters, normed_t, dq, dk, dv)


def qkv_back_kernel(dq, dk, dv, wq, wk, wv, own, send):
    total = dot(dq[...], wq[...], NT) + dot(dk[...], wk[...], NT) + dot(dv[...], wv[...], NT)
    late = pl.program_id(0) >= pl.num_programs(0) // 2

    @pl.when(late)
    def _():
        own[...] = total

    @pl.when(jnp.logical_not(late))
    def _():
        send[...] = total.astype(BF)


def qkv_back(dq, dk, dv, wq, wk, wv, tile=256):
    seq, width = dq.shape
    d = wq.shape[0]
    n = seq // tile
    rows = pl.BlockSpec((tile, width), lambda i: (lax.rem(i + n // 2, n), 0))
    whole = pl.BlockSpec((d, width), lambda i: (0, 0))
    return pl.pallas_call(
        qkv_back_kernel,
        grid=(n,),
        in_specs=[rows] * 3 + [whole] * 3,
        out_specs=[
            pl.BlockSpec((tile, d), lambda i: (jnp.maximum(i - n // 2, 0), 0)),
            pl.BlockSpec((tile, d), lambda i: (jnp.minimum(i, n // 2 - 1), 0)),
        ],
        out_shape=[shape((seq // 2, d), F32), shape((seq // 2, d), BF)],
        compiler_params=params(),
        cost_estimate=cost(6 * seq * d * width, 12 * seq * d),
    )(dq, dk, dv, wq, wk, wv)


def last_kernel(mine, theirs, tokens, grad_hidden, gain, out, gain_grad):
    at = pl.program_id(0)
    through, part = norm_back(
        tokens[...].astype(F32), gain[...], mine[...] + theirs[...].astype(F32)
    )
    out[...] = (grad_hidden[...] + through).astype(BF)

    @pl.when(at == 0)
    def _():
        gain_grad[...] = part

    @pl.when(at > 0)
    def _():
        gain_grad[...] += part


def last(mine, theirs, tokens, grad_hidden, gain, tile=256):
    rows, d = tokens.shape
    block = pl.BlockSpec((tile, d), lambda i: (i, 0))
    one = pl.BlockSpec((1, d), lambda i: (0, 0))
    return pl.pallas_call(
        last_kernel,
        grid=(rows // tile,),
        in_specs=[block] * 4 + [one],
        out_specs=[block, one],
        out_shape=[shape((rows, d), BF), shape((1, d), F32)],
        compiler_params=params(),
        cost_estimate=cost(20 * rows * d, 16 * rows * d),
    )(mine, theirs, tokens, grad_hidden, gain)


def swap(x):
    return lax.ppermute(x, "mp", [(0, 1), (1, 0)])


def down_layout(part):
    four, rows, width = part.shape
    tiles = part.reshape(four, rows // 128, 128, width // 128, 128)
    return tiles.transpose(3, 2, 0, 1, 4).reshape(width, four * rows)


def shards(
    tokens,
    segment_ids,
    keep_mask,
    w_query,
    w_key,
    w_value,
    w_out,
    w_gate,
    w_up,
    w_down,
    norm_attn,
    norm_ffn,
    cotangent,
):
    half, d = tokens.shape[0], tokens.shape[2]
    seq = segment_ids.shape[1]
    slot = seq // 4
    core = lax.axis_index("mp")
    segs, keep = segment_ids[0], keep_mask[0]
    middle_at = seq // 2
    leads = (segs[0] != segs[middle_at]) | (keep[0] == 0)
    ends = (segs[seq - 1] != segs[middle_at]) | (keep[seq - 1] == 0)
    start = jnp.where(leads, 1, 0)
    padded = jnp.where(jnp.where(leads, keep[0], keep[seq - 1]) == 0, 1, 0)
    logical = (jnp.arange(4, dtype=jnp.int32) + start) % 4
    meta = jnp.concatenate([(logical + 2 * core) % 4, padded[None]]).astype(jnp.int32)
    quarters = jnp.arange(4, dtype=jnp.int32)

    own = tokens[:, 0]
    ct_own = cotangent[:, 0]
    gain_attn, gain_ffn = norm_attn[None], norm_ffn[None]
    other = swap(own)
    ct = jnp.concatenate([ct_own, swap(ct_own)], 0)
    first = project(own, gain_attn, w_query, w_key, w_value, 0)
    qkv, normed_t = project(other, gain_attn, w_query, w_key, w_value, 1, first)
    mixed, mixed_t, lse = attend(meta, qkv)
    attn_part = matmul_rows(mixed, w_out, NN, BF)
    hidden, x, xt = middle(own, other, attn_part, swap(attn_part), gain_ffn)

    acts, ggs, gus, ffn_grads = [], [], [], []
    at = 0
    for width in FFN_CHUNKS:
        a, gg, gu, grads = ffn(
            quarters, x, ct, xt, w_gate[:, at : at + width], w_up[:, at : at + width], w_down[at : at + width]
        )
        acts.append(a)
        ggs.append(gg)
        gus.append(gu)
        ffn_grads.append(lax.psum(grads, "dp"))
        at += width
    out_own, out_send, back_part = ffn_sums(acts, ggs, gus, w_gate, w_up, w_down)
    result = (hidden[:half] + (out_own + swap(out_send).astype(F32))).astype(BF)
    grad_in, grad_hidden, gain_ffn_part = middle_back(back_part, swap(back_part), hidden, ct, gain_ffn)
    grad_mixed, out_grads = out_back(quarters, grad_in, mixed_t, w_out)
    dq, dk, dv = attend_back(meta, qkv, mixed_t, grad_mixed, lse)
    attn_grads = qkv_grads(quarters, normed_t, dq, dk, dv)
    back_own, back_send = qkv_back(dq, dk, dv, w_query, w_key, w_value)
    grad_tokens, gain_attn_part = last(back_own, swap(back_send), own, grad_hidden, gain_attn)

    out_grads, attn_grads = lax.psum((out_grads, attn_grads), "dp")
    gain_attn_grad = lax.psum(gain_attn_part[0], ("dp", "mp"))
    gain_ffn_grad = lax.psum(gain_ffn_part[0], "dp")

    def columns(part):
        return part.reshape(d, -1).astype(F32)

    grad_gate = jnp.concatenate([columns(g[:, :, :w]) for g, w in zip(ffn_grads, FFN_CHUNKS)], 1)
    grad_up = jnp.concatenate([columns(g[:, :, w : 2 * w]) for g, w in zip(ffn_grads, FFN_CHUNKS)], 1)
    grad_down = jnp.concatenate(
        [down_layout(g[:, :, 2 * w :]).astype(F32) for g, w in zip(ffn_grads, FFN_CHUNKS)], 0
    )
    width = w_query.shape[1]
    quarter = d // 4
    grad_out = (
        out_grads.reshape(4, quarter, width // quarter, quarter)
        .transpose(2, 1, 0, 3)
        .reshape(width, d)
        .astype(F32)
    )
    return (
        result[:, None],
        grad_tokens[:, None],
        columns(attn_grads[:, :, :width]),
        columns(attn_grads[:, :, width : 2 * width]),
        columns(attn_grads[:, :, 2 * width :]),
        grad_out,
        grad_gate,
        grad_up,
        grad_down,
        gain_attn_grad,
        gain_ffn_grad,
    )


def solution(mesh):
    return jax.shard_map(
        shards,
        mesh=mesh,
        in_specs=(
            P("mp", "dp", None),
            P("dp", None),
            P("dp", None),
            P(None, "mp"),
            P(None, "mp"),
            P(None, "mp"),
            P("mp", None),
            P(None, "mp"),
            P(None, "mp"),
            P("mp", None),
            P(),
            P(),
            P("mp", "dp", None),
        ),
        out_specs=(
            P("mp", "dp", None),
            P("mp", "dp", None),
            P(None, "mp"),
            P(None, "mp"),
            P(None, "mp"),
            P("mp", None),
            P(None, "mp"),
            P(None, "mp"),
            P("mp", None),
            P(),
            P(),
        ),
        check_vma=False,
    )
```

```python
import functools

import jax
import jax.numpy as jnp
from jax import lax
from jax.experimental import pallas as pl
from jax.experimental.pallas import tpu as pltpu
from jax.sharding import PartitionSpec as P

HDIM = 64
EPSILON = 1e-06
LOG2E = 1.4426950408889634
VMEM_LIMIT = 62 * 1024 * 1024
COST = 1e6
BF = jnp.bfloat16
F32 = jnp.float32
NN = ((1,), (0,))
NT = ((1,), (1,))
TN = ((0,), (0,))
FFN_CHUNKS = (512, 896)


def dot(left, right, dims=NN):
    return lax.dot_general(left, right, (dims, ((), ())), preferred_element_type=F32)


def shape(dims, dtype):
    return jax.ShapeDtypeStruct(dims, dtype)


class Chain:
    def __init__(self):
        self.token = None

    def run(self, kernel, grid, in_specs, out_specs, out_shape, args, prefetch=(), scratch=(), alias=None, us=5):
        before = [] if self.token is None else [self.token]
        some, n_in, n_out = len(prefetch), len(args), len(out_shape)
        skip = len(before)

        def body(*refs):
            kept = refs[: some + n_in] + refs[some + n_in + skip : some + n_in + skip + n_out]
            kernel(*kept, *refs[some + n_in + skip + n_out + 1 :])

        anywhere = pl.BlockSpec(memory_space=pl.ANY)
        *outs, self.token = pl.pallas_call(
            body,
            grid_spec=pltpu.PrefetchScalarGridSpec(
                num_scalar_prefetch=some,
                grid=grid,
                in_specs=list(in_specs) + [anywhere] * skip,
                out_specs=list(out_specs) + [anywhere],
                scratch_shapes=list(scratch),
            ),
            out_shape=list(out_shape) + [shape((8, 128), F32)],
            input_output_aliases=alias or {},
            compiler_params=pltpu.CompilerParams(vmem_limit_bytes=VMEM_LIMIT),
            cost_estimate=pl.CostEstimate(flops=int(us * COST), bytes_accessed=1, transcendentals=0),
        )(*prefetch, *args, *before)
        return outs


ANYWHERE = pl.BlockSpec(memory_space=pl.ANY)


def block(dims, index):
    return pl.BlockSpec(dims, index)


class Copies:
    def __init__(self, sems):
        self.sems, self.started = sems, []

    def start(self, source, target):
        copy = pltpu.make_async_copy(source, target, self.sems.at[len(self.started)])
        copy.start()
        self.started.append(copy)
        return copy


def by_hand(chain, kernel, inputs, outputs, scratch, copies, prefetch=(), alias=None, us=5):
    def body(*refs):
        kernel(*refs[:-1], Copies(refs[-1]))

    return chain.run(
        body,
        (1,),
        [ANYWHERE] * len(inputs),
        [ANYWHERE] * len(outputs),
        outputs,
        inputs,
        prefetch=prefetch,
        scratch=list(scratch) + [pltpu.SemaphoreType.DMA((copies,))],
        alias=alias,
        us=us,
    )


def project(chain, tokens, gain, wq, wk, wv, half, before=()):
    rows, d = tokens.shape
    width = wq.shape[1]
    weights = [wq, wk, wv]

    def kernel(tokens, gain, *refs):
        ws, refs = refs[:3], refs[3 + len(before) :]
        projected, normed, xs, gs, held, out, low, copies = refs
        first = [copies.start(gain, gs), copies.start(tokens, xs)]
        loads = [copies.start(w, held.at[i]) for i, w in enumerate(ws)]
        for c in first:
            c.wait()
        x = xs[...].astype(F32)
        r = lax.rsqrt(jnp.mean(x * x, axis=-1, keepdims=True) + EPSILON)
        low[...] = (x * r * gs[...]).astype(BF)
        here = pl.ds(half * rows, rows)
        stores = [copies.start(low, normed.at[here])]
        for i in range(3):
            loads[i].wait()
            out[i] = dot(low[...], held[i]).astype(BF)
            stores.append(copies.start(out.at[i], projected.at[here, pl.ds(i * width, width)]))
        for c in stores:
            c.wait()

    return by_hand(
        chain,
        kernel,
        [tokens, gain, *weights, *before],
        [shape((2 * rows, 3 * width), BF), shape((2 * rows, d), BF)],
        [
            pltpu.VMEM((rows, d), BF),
            pltpu.VMEM((1, d), F32),
            pltpu.VMEM((3, d, width), BF),
            pltpu.VMEM((3, rows, width), BF),
            pltpu.VMEM((rows, d), BF),
        ],
        9,
        alias={5: 0, 6: 1} if before else None,
    )


def layout(place, segs, keep, slot):
    last, mid = 4 * slot - 1, 2 * slot
    leads = jnp.logical_or(segs[0] != segs[mid], keep[0] == 0)
    start = jnp.where(leads, 1, 0) + 2 * place[0]
    padded = jnp.where(jnp.where(leads, keep[0], keep[last]) == 0, 1, 0)
    return (lambda logical: pl.ds(pl.multiple_of(lax.rem(logical + start, 4) * slot, slot), slot)), padded


def two_heads(columns):
    slot = columns.shape[1]
    zero = jnp.zeros((HDIM, slot), BF)
    first = jnp.concatenate([columns[:HDIM], zero], 0)
    second = jnp.concatenate([zero, columns[HDIM:]], 0)
    return jnp.concatenate([first, second], 1)


def attend(chain, scalars, qkv, w_out, early):
    seq, width = qkv.shape[0], qkv.shape[1] // 3
    d = w_out.shape[1]
    pairs, slot, half = width // 128, seq // 4, seq // 2
    scale = HDIM**-0.5 * LOG2E

    def kernel(place, segs, keep, q_ref, k_ref, v_ref, w_all, early, o_ref, lse_ref, part, mixed, ws, out, sems):
        step = pl.program_id(0)
        rows, padded = layout(place, segs, keep, slot)
        load = pltpu.make_async_copy(w_all, ws, sems.at[0])

        @pl.when(step == 0)
        def _():
            load.start()

        one = jnp.ones((16, slot), BF)
        for at in range(4):
            slots = [j if at < 3 else jnp.where(padded > 0, j, 3) for j in range(3)]
            q2 = two_heads(q_ref[rows(at), :].T)
            scores = [dot(k_ref[rows(j), :], q2) for j in slots]
            top = functools.reduce(jnp.maximum, [jnp.max(s, axis=0, keepdims=True) for s in scores])
            oa = jnp.zeros((HDIM + 16, slot), F32)
            ob = oa
            for j, s in zip(slots, scores):
                p = jnp.exp2((s - top) * scale).astype(BF)
                vt = v_ref[rows(j), :].T
                oa += dot(jnp.concatenate([vt[:HDIM], one], 0), p[:, :slot])
                ob += dot(jnp.concatenate([vt[HDIM:], one], 0), p[:, slot:])
            la, lb = oa[HDIM : HDIM + 1], ob[HDIM : HDIM + 1]
            o = jnp.concatenate([oa[:HDIM] / la, ob[:HDIM] / lb], 0).astype(BF).T
            o_ref[rows(at), :] = o
            mixed[step, rows(at), :] = o
            lse = top * HDIM**-0.5 + jnp.log(jnp.concatenate([la, lb], 1))
            lse_ref[0, 0:1, rows(at)] = lse[:, :slot]
            lse_ref[0, 1:2, rows(at)] = lse[:, slot:]

        @pl.when(step == pairs - 1)
        def _():
            load.wait()
            stores = []
            for k in range(2):
                here = slice(k * half, (k + 1) * half)
                every = jnp.concatenate([mixed[p, here, :] for p in range(pairs)], 1)
                out[here] = dot(every, ws[...]).astype(BF)
                stores.append(pltpu.make_async_copy(out.at[here], part.at[here], sems.at[1 + k]))
                stores[-1].start()
            for c in stores:
                c.wait()

    column = lambda off: block((seq, 128), lambda p, *m: (0, p + off))
    return chain.run(
        kernel,
        (pairs,),
        [column(0), column(pairs), column(2 * pairs), ANYWHERE, ANYWHERE],
        [column(0), block((1, 2, seq), lambda p, *m: (p, 0, 0)), ANYWHERE],
        [shape((seq, width), BF), shape((pairs, 2, seq), F32), shape((seq, d), BF)],
        [qkv, qkv, qkv, w_out, early],
        prefetch=scalars,
        scratch=[
            pltpu.VMEM((pairs, seq, 128), BF),
            pltpu.VMEM((width, d), BF),
            pltpu.VMEM((seq, d), BF),
            pltpu.SemaphoreType.DMA((3,)),
        ],
        us=26,
    )


def attend_back(chain, scalars, order, qkv, mixed, grad_mixed, lse, normed, first, before=None):
    seq, width = qkv.shape[0], qkv.shape[1] // 3
    d = normed.shape[1]
    pairs, slot, quarter = width // 128, seq // 4, d // 4
    scale = HDIM**-0.5 * LOG2E

    def kernel(
        place, segs, keep, order, q_ref, k_ref, v_ref, o_ref, do_ref, lse_ref, *refs
    ):
        rows, padded = layout(place, segs, keep, slot)
        if before is None:
            dq_ref, dk_ref, dv_ref, dk_sum, dv_sum = refs
        else:
            normed_all, *old, dq_ref, dk_ref, dv_ref, kept, sent, dk_sum, dv_sum, every, ns, held, sems = refs
            copies = Copies(sems)
            loads = [copies.start(normed_all, ns)]
            loads += [copies.start(o, every.at[i]) for i, o in enumerate(old)]

        def stacked(x):
            lane = lax.broadcasted_iota(jnp.int32, (slot, 128), 1)
            zero = jnp.zeros_like(x)
            return jnp.concatenate([jnp.where(lane < HDIM, x, zero), jnp.where(lane < HDIM, zero, x)], 0)

        def extended(columns, tail):
            high = tail.astype(BF).astype(F32)
            rest = tail - high
            middle = rest.astype(BF).astype(F32)
            extra = jnp.concatenate([high, middle, rest - middle, jnp.zeros((125, 2 * slot), F32)], 0).astype(BF)
            return jnp.concatenate([two_heads(columns), extra], 0)

        def one_slot(at, slots):
            ones = jnp.ones((slot, 128), BF)
            q, do = q_ref[rows(at), :], do_ref[rows(at), :]
            do_t = do.T
            prod = do_t.astype(F32) * o_ref[rows(at), :].T.astype(F32)
            delta = jnp.concatenate(
                [jnp.sum(prod[:HDIM], 0, keepdims=True), jnp.sum(prod[HDIM:], 0, keepdims=True)], 1
            )
            lse = jnp.concatenate([lse_ref[0, 0:1, rows(at)], lse_ref[0, 1:2, rows(at)]], 1)
            q2 = extended(q.T, lse * -(HDIM**0.5))
            do2 = extended(do_t, -delta)
            qs, dos = stacked(q), stacked(do)
            dqa = jnp.zeros((HDIM, slot), F32)
            dqb = dqa
            for j in slots:
                k, v = k_ref[rows(j), :], v_ref[rows(j), :]
                p = jnp.exp2(dot(jnp.concatenate([k, ones], 1), q2) * scale)
                dp = dot(jnp.concatenate([v, ones], 1), do2)
                ds = (p * dp).astype(BF)
                dv_sum[rows(j), :] += dot(p.astype(BF), dos)
                dk_sum[rows(j), :] += dot(ds, qs)
                kt = k.T
                dqa += dot(kt[:HDIM], ds[:, :slot])
                dqb += dot(kt[HDIM:], ds[:, slot:])
            dq_ref[rows(at), :] = (jnp.concatenate([dqa, dqb], 0) * HDIM**-0.5).astype(BF).T

        dk_sum[...] = jnp.zeros_like(dk_sum)
        dv_sum[...] = jnp.zeros_like(dv_sum)

        def body(at, carry):
            alone = jnp.logical_and(at == 3, padded == 0)
            one_slot(at, [jnp.where(alone, 3, j) for j in range(3)])
            return carry

        lax.fori_loop(0, 4, body, 0)
        dk = (dk_sum[...] * HDIM**-0.5).astype(BF)
        dv = dv_sum[...].astype(BF)
        dk_ref[...] = dk
        dv_ref[...] = dv
        if before is not None:
            for c in loads:
                c.wait()
            right = jnp.concatenate([every[0], dq_ref[...], every[1], dk, every[2], dv], 1)
            stores = []
            for k in range(4):
                held[k] = dot(column_block(ns, order[k], quarter), right, TN).astype(BF)
                stores.append(copies.start(held.at[k], quarters_of([kept, sent])[k]))
            for c in stores:
                c.wait()

    column = lambda off: block((seq, 128), lambda p, *m: (0, off))
    wide = 3 * 2 * 128
    more = before is not None
    return chain.run(
        kernel,
        (1,),
        [
            column(first),
            column(first + pairs),
            column(first + 2 * pairs),
            column(first),
            column(first),
            block((1, 2, seq), lambda p, *m: (first, 0, 0)),
        ]
        + [ANYWHERE] * (4 * more),
        [column(0)] * 3 + [ANYWHERE] * (2 * more),
        [shape((seq, 128), BF)] * 3 + quarter_shapes(2 * more, quarter, wide),
        [qkv, qkv, qkv, mixed, grad_mixed, lse] + ([normed, *before] if more else []),
        prefetch=scalars + [order],
        scratch=[pltpu.VMEM((seq, 128), F32)] * 2
        + [
            pltpu.VMEM((3, seq, 128), BF),
            pltpu.VMEM((seq, d), BF),
            pltpu.VMEM((4, quarter, wide), BF),
            pltpu.SemaphoreType.DMA((8,)),
        ]
        * more,
        us=13,
    )


def middle(chain, own, other, mine, theirs, gain, tile=384):
    half, d = own.shape
    n = 2 * half // tile
    rows = lambda f: block((tile, d), lambda i: (f(i), 0))

    def kernel(own, other, mine, theirs, gain, hidden, normed):
        tokens = jnp.where(pl.program_id(0) < n // 2, own[...], other[...]).astype(F32)
        h = tokens + (mine[...].astype(F32) + theirs[...].astype(F32))
        r = lax.rsqrt(jnp.mean(h * h, axis=-1, keepdims=True) + EPSILON)
        low = (h * r * gain[...]).astype(BF)
        hidden[...] = h
        normed[...] = low

    return chain.run(
        kernel,
        (n,),
        [
            rows(lambda i: jnp.minimum(i, n // 2 - 1)),
            rows(lambda i: jnp.maximum(i - n // 2, 0)),
            rows(lambda i: i),
            rows(lambda i: lax.rem(i + n // 2, n)),
            block((1, d), lambda i: (0, 0)),
        ],
        [rows(lambda i: i), rows(lambda i: i)],
        [shape((2 * half, d), F32), shape((2 * half, d), BF)],
        [own, other, mine, theirs, gain],
        us=5,
    )


def gelu_parts(v):
    c = 0.7978845608028654
    square = v * v
    share = 0.5 + 0.5 * jnp.tanh(v * (c + (c * 0.044715) * square))
    value = v * share
    return value, share + value * (1.0 - share) * (2 * c + (6 * c * 0.044715) * square)


def column_block(ref, number, width):
    return ref[:, pl.ds(pl.multiple_of(number * width, width), width)]


def quarters_of(outs):
    each = 4 // len(outs)
    return [outs[k // each].at[k % each] for k in range(4)]


def quarter_shapes(pieces, rows, width):
    return [shape((4 // pieces, rows, width), BF)] * pieces if pieces else []


def weight_quarters(copies, order, xs, cs, acts, boths, held, targets, quarter, beside=None):
    width = acts.shape[1]
    stores = []
    for k in range(4):
        sides = dot(column_block(xs, order[k], quarter), boths[...], TN)
        down = dot(acts[...], column_block(cs, order[k], quarter), TN).astype(BF)
        held[k, :, : 2 * width] = sides.astype(BF)
        for i in range(width // 128):
            rows = down[i * 128 : (i + 1) * 128]
            place = slice(2 * width + i * 128, 2 * width + (i + 1) * 128)
            held[k, :128, place] = rows[:, :128]
            held[k, 128:, place] = rows[:, 128:]
        if beside is not None:
            beside(k)
        stores.append(copies.start(held.at[k], targets[k]))
    return stores


def ffn(chain, order, x, ct_own, ct_other, w_gate, w_up, w_down, at, width, finish):
    seq, d = x.shape
    half, quarter = seq // 2, d // 4

    def kernel(order, x, ct_own, ct_other, wg_all, wu_all, wd_all, act, both, *refs):
        grads, (xs, cs, wg, wu, wd, acts, boths, *held, copies) = refs[:finish], refs[finish:]
        halves = [slice(0, half), slice(half, seq)]
        x0 = copies.start(x.at[halves[0]], xs.at[halves[0]])
        units = pl.ds(at, width)
        lg = copies.start(wg_all.at[:, units], wg)
        lu = copies.start(wu_all.at[:, units], wu)
        c0 = copies.start(ct_own, cs.at[halves[0]])
        ld = copies.start(wd_all.at[units, :], wd)
        x1 = copies.start(x.at[halves[1]], xs.at[halves[1]])
        c1 = copies.start(ct_other, cs.at[halves[1]])
        waits = [[x0, lg], [lu], [c0, ld]], [[x1], [], [c1]]
        stores = []
        for here, (for_gate, for_up, for_act) in zip(halves, waits):
            for c in for_gate:
                c.wait()
            gate = dot(xs[here], wg[...])
            for c in for_up:
                c.wait()
            up = dot(xs[here], wu[...])
            for c in for_act:
                c.wait()
            grad_act = dot(cs[here], wd[...], NT)
            value, slope = gelu_parts(gate)
            acts[here] = (value * up).astype(BF)
            boths[here, :width] = (grad_act * up * slope).astype(BF)
            boths[here, width:] = (grad_act * value).astype(BF)
            stores.append(copies.start(acts.at[here], act.at[here]))
            stores.append(copies.start(boths.at[here], both.at[here]))
        if finish:
            targets = quarters_of(grads)
            stores += weight_quarters(copies, order, xs, cs, acts, boths, held[0], targets, quarter)
        for c in stores:
            c.wait()

    return by_hand(
        chain,
        kernel,
        [x, ct_own, ct_other, w_gate, w_up, w_down],
        [shape((seq, width), BF), shape((seq, 2 * width), BF)] + quarter_shapes(finish, quarter, 3 * width),
        [
            pltpu.VMEM((seq, d), BF),
            pltpu.VMEM((seq, d), BF),
            pltpu.VMEM((d, width), BF),
            pltpu.VMEM((d, width), BF),
            pltpu.VMEM((width, d), BF),
            pltpu.VMEM((seq, width), BF),
            pltpu.VMEM((seq, 2 * width), BF),
        ]
        + [pltpu.VMEM((4, quarter, 3 * width), BF)] * min(finish, 1),
        15,
        prefetch=[order],
        us=16 if finish else 8,
    )


def ffn_input_grad(chain, boths, wg, wu):
    seq = boths[0].shape[0]
    d, units = wg.shape
    half, chunks = seq // 2, len(boths)
    starts = [sum(b.shape[1] for b in boths[:k]) // 2 for k in range(chunks + 1)]

    def kernel(*refs):
        ins, (wg, wu, back, *held, wgs, wus, out, copies) = refs[:chunks], refs[chunks:]
        loads = []
        for k in range(chunks):
            units = pl.ds(starts[k], starts[k + 1] - starts[k])
            loads.append(
                [
                    copies.start(ins[k].at[pl.ds(0, half)], held[k].at[pl.ds(0, half)]),
                    copies.start(wg.at[:, units], wgs.at[:, units]),
                    copies.start(wu.at[:, units], wus.at[:, units]),
                ]
            )
        later = [copies.start(ins[k].at[pl.ds(half, half)], held[k].at[pl.ds(half, half)]) for k in range(chunks)]
        stores = []
        for h in range(2):
            here = slice(h * half, (h + 1) * half)
            total = None
            for k in range(chunks):
                for c in loads[k] if h == 0 else [later[k]]:
                    c.wait()
                width = starts[k + 1] - starts[k]
                units = slice(starts[k], starts[k + 1])
                part = dot(held[k][here, :width], wgs[:, units], NT) + dot(held[k][here, width:], wus[:, units], NT)
                total = part if total is None else total + part
            out[here] = total.astype(BF)
            stores.append(copies.start(out.at[here], back.at[here]))
        for c in stores:
            c.wait()

    return by_hand(
        chain,
        kernel,
        boths + [wg, wu],
        [shape((seq, d), BF)],
        [pltpu.VMEM(b.shape, BF) for b in boths]
        + [pltpu.VMEM((d, units), BF), pltpu.VMEM((d, units), BF), pltpu.VMEM((seq, d), BF)],
        4 * chunks + 2,
        us=13,
    )[0]


def ffn_output(chain, acts, wd):
    seq, d = acts[0].shape[0], wd.shape[1]
    half, chunks = seq // 2, len(acts)
    starts = [sum(a.shape[1] for a in acts[:k]) for k in range(chunks + 1)]

    def kernel(*refs):
        ins, (wd, own, send, *held, wds, out_own, out_send, copies) = refs[:chunks], refs[chunks:]
        first, second = pl.ds(half, half), pl.ds(0, half)
        loads = []
        for k in range(chunks):
            units = pl.ds(starts[k], starts[k + 1] - starts[k])
            loads.append([copies.start(ins[k].at[first], held[k].at[first]), copies.start(wd.at[units], wds.at[units])])
        later = [copies.start(ins[k].at[second], held[k].at[second]) for k in range(chunks)]
        stores = []
        for h, (here, target, out) in enumerate([(first, out_send, send), (second, out_own, own)]):
            total = None
            for k in range(chunks):
                for c in loads[k] if h == 0 else [later[k]]:
                    c.wait()
                part = dot(held[k][here], wds[starts[k] : starts[k + 1]])
                total = part if total is None else total + part
            target[...] = total.astype(target.dtype)
            stores.append(copies.start(target, out))
        for c in stores:
            c.wait()

    return by_hand(
        chain,
        kernel,
        acts + [wd],
        [shape((half, d), F32), shape((half, d), BF)],
        [pltpu.VMEM(a.shape, BF) for a in acts]
        + [pltpu.VMEM(wd.shape, BF), pltpu.VMEM((half, d), F32), pltpu.VMEM((half, d), BF)],
        3 * chunks + 2,
        us=7,
    )


def norm_back(value, gain, grad):
    r = lax.rsqrt(jnp.mean(value * value, axis=-1, keepdims=True) + EPSILON)
    u = grad * gain
    inner = jnp.mean(u * value, axis=-1, keepdims=True)
    return r * u - value * (r * r * r * inner), jnp.sum(grad * value * r, axis=0, keepdims=True)


def add_up(at, total, part):
    @pl.when(at == 0)
    def _():
        total[...] = part

    @pl.when(at > 0)
    def _():
        total[...] += part


def middle_back(chain, mine, theirs, hidden, ct_own, ct_other, gain, out_own, out_theirs, tile=384):
    seq, d = hidden.shape
    n = seq // tile
    rows = lambda f: block((tile, d), lambda i: (f(i), 0))
    front = rows(lambda i: jnp.minimum(i, n // 2 - 1))

    def kernel(mine, theirs, hidden, ct_own, ct_other, gain, out_own, out_theirs, low, keep, gain_grad, result):
        at = pl.program_id(0)
        h = hidden[...]
        through, part = norm_back(h, gain[...], mine[...].astype(F32) + theirs[...].astype(F32))
        ct = jnp.where(at < n // 2, ct_own[...], ct_other[...])
        total = ct.astype(F32) + through
        low[...] = total.astype(BF)
        add_up(at, gain_grad, part)

        @pl.when(at < n // 2)
        def _():
            keep[...] = total
            result[...] = (h + (out_own[...] + out_theirs[...].astype(F32))).astype(BF)

    return chain.run(
        kernel,
        (n,),
        [
            rows(lambda i: i),
            rows(lambda i: lax.rem(i + n // 2, n)),
            rows(lambda i: i),
            front,
            rows(lambda i: jnp.maximum(i - n // 2, 0)),
            block((1, d), lambda i: (0, 0)),
            front,
            front,
        ],
        [rows(lambda i: i), front, block((1, d), lambda i: (0, 0)), front],
        [shape((seq, d), BF), shape((seq // 2, d), F32), shape((1, d), F32), shape((seq // 2, d), BF)],
        [mine, theirs, hidden, ct_own, ct_other, gain, out_own, out_theirs],
        us=8,
    )


def out_back(chain, order, g, mixed, w_out):
    seq, d = g.shape
    width, quarter, half = w_out.shape[0], d // 4, seq // 2

    def kernel(order, g, mixed, w_out, grad_mixed, *refs):
        *grads, gs, ms, ws, out, held, copies = refs
        halves = [pl.ds(0, half), pl.ds(half, half)]
        loads = [[copies.start(g.at[halves[0]], gs.at[halves[0]]), copies.start(w_out, ws)]]
        loads.append([copies.start(g.at[halves[1]], gs.at[halves[1]])])
        last = copies.start(mixed, ms)
        stores = []
        for here, waits in zip(halves, loads):
            for c in waits:
                c.wait()
            out[here] = dot(gs[here], ws[...], NT).astype(BF)
            stores.append(copies.start(out.at[here], grad_mixed.at[here]))
        last.wait()
        for k in range(4):
            part = dot(ms[...], column_block(gs, order[k], quarter), TN).astype(BF)
            for i in range(width // quarter):
                held[k, :, i * quarter : (i + 1) * quarter] = part[i * quarter : (i + 1) * quarter]
            stores.append(copies.start(held.at[k], quarters_of(grads)[k]))
        for c in stores:
            c.wait()

    return by_hand(
        chain,
        kernel,
        [g, mixed, w_out],
        [shape((seq, width), BF)] + quarter_shapes(2, quarter, width),
        [
            pltpu.VMEM((seq, d), BF),
            pltpu.VMEM((seq, width), BF),
            pltpu.VMEM((width, d), BF),
            pltpu.VMEM((seq, width), BF),
            pltpu.VMEM((4, quarter, width), BF),
        ],
        10,
        prefetch=[order],
        us=8,
    )


def qkv_back(chain, grads, weights, own, other, gain_ffn_grad):
    flat = [g for kind in grads for g in kind]
    count = len(flat)
    pieces = len(grads[0])
    seq = flat[0].shape[0]
    d, width = weights[0].shape
    half = seq // 2

    def kernel(*refs):
        ins, ws, refs = refs[:count], refs[count : count + 3], refs[count + 3 :]
        t_own, t_other, ffn_part, own, send, gains, *held, wh, ts, ffn, sums, out_own, out_send, copies = refs
        first, second = pl.ds(half, half), pl.ds(0, half)
        loads = [[copies.start(ins[i].at[first], held[i].at[first])] for i in range(count)]
        for i in range(3):
            loads[i * pieces].append(copies.start(ws[i], wh.at[i]))
        later = [[copies.start(ins[i].at[second], held[i].at[second])] for i in range(count)]
        tokens = [copies.start(t_other, ts.at[1]), copies.start(t_own, ts.at[0]), copies.start(ffn_part, ffn)]
        stores = []
        gain = 0.0
        for k, (here, waits, target, out) in enumerate([(first, loads, out_send, send), (second, later, out_own, own)]):
            total = 0.0
            for kind in range(3):
                some = range(kind * pieces, (kind + 1) * pieces)
                for i in some:
                    for c in waits[i]:
                        c.wait()
                left = jnp.concatenate([held[i][here] for i in some], 1)
                total += dot(left, wh[kind], NT)
            target[...] = total.astype(target.dtype)
            stores.append(copies.start(target, out))
            tokens[k].wait()
            x = ts[1 - k].astype(F32)
            r = lax.rsqrt(jnp.mean(x * x, axis=-1, keepdims=True) + EPSILON)
            gain += jnp.sum(total * (x * r), axis=0, keepdims=True)
        tokens[2].wait()
        sums[0:1] = gain
        sums[1:2] = 0.5 * ffn[...]
        stores.append(copies.start(sums, gains))
        for c in stores:
            c.wait()

    return by_hand(
        chain,
        kernel,
        flat + list(weights) + [own, other, gain_ffn_grad],
        [shape((half, d), F32), shape((half, d), BF), shape((2, d), F32)],
        [pltpu.VMEM(g.shape, BF) for g in flat]
        + [
            pltpu.VMEM((3, d, width), BF),
            pltpu.VMEM((2, half, d), BF),
            pltpu.VMEM((1, d), F32),
            pltpu.VMEM((2, d), F32),
            pltpu.VMEM((half, d), F32),
            pltpu.VMEM((half, d), BF),
        ],
        2 * count + 9,
        us=8,
    )


def last(chain, mine, theirs, tokens, grad_hidden, gain, tile=384):
    rows, d = tokens.shape
    row = block((tile, d), lambda i: (i, 0))

    def kernel(mine, theirs, tokens, grad_hidden, gain, out):
        grad = mine[...] + theirs[...].astype(F32)
        out[...] = (grad_hidden[...] + norm_back(tokens[...].astype(F32), gain[...], grad)[0]).astype(BF)

    return chain.run(
        kernel,
        (rows // tile,),
        [row] * 4 + [block((1, d), lambda i: (0, 0))],
        [row],
        [shape((rows, d), BF)],
        [mine, theirs, tokens, grad_hidden, gain],
        us=4,
    )[0]


def swap(x):
    return lax.ppermute(x, "mp", [(0, 1), (1, 0)])


def exchange(x, bit):
    return lax.ppermute(x, "dp", [(i, i ^ bit) for i in range(lax.axis_size("dp"))])


def add(terms, pieces=1):
    n, rows, width = terms[0].shape
    tile = rows // 2

    def body(at, z, ins, outs):
        for k, out in enumerate(outs):
            out[0] = sum(t[k].astype(F32) for t in ins).astype(BF)

    spec = block((n, tile, width), lambda i, z: (0, i, 0))
    out = block((1, tile, width), lambda i, z: (0, i, 0))
    return list(terms), [spec] * len(terms), [out] * n, [shape((1, rows, width), BF)] * n, body


def halve(terms, bit):
    _, rows, width = terms[0].shape
    tile = rows // 4

    def body(at, z, ins, outs):
        for k in range(2):
            outs[k][0] = sum(t[0].astype(F32) for t in ins[k::2]).astype(BF)

    mine = block((1, tile, width), lambda i, z: (0, 2 * z[bit] + i, 0))
    others = block((1, tile, width), lambda i, z: (0, 2 * (1 - z[bit]) + i, 0))
    out = block((1, tile, width), lambda i, z: (0, i, 0))
    return (
        [t for t in terms for _ in range(2)],
        [mine, others] * len(terms),
        [out] * 2,
        [shape((1, rows // 2, width), BF)] * 2,
        body,
    )


def join(mine, theirs, bit):
    _, rows, width = mine.shape

    def body(at, z, ins, outs):
        outs[0][0] = jnp.where(at == z[bit], ins[0][0], ins[1][0])

    spec = block((1, rows, width), lambda i, z: (0, 0, 0))
    out = block((1, rows, width), lambda i, z: (0, i, 0))
    return [mine, theirs], [spec] * 2, [out], [shape((1, 2 * rows, width), BF)], body


class Flow:
    def __init__(self, quarters, bits=(1, 2), split=False):
        rest = [1 << b for b in range(2, (lax.axis_size("dp") - 1).bit_length())]
        self.steps = self.walk(quarters, bits, rest, split)
        self.step = next(self.steps)

    def walk(self, quarters, bits, rest, split):
        if len(quarters) == 2:
            keep, send = quarters
            mine, send = yield add([keep, exchange(send, bits[0])])
            terms = [mine, exchange(send, bits[1])]
        else:
            terms = list(quarters)
        if split:
            for k in range(2):
                mine, send = yield halve(terms, k)
                terms = [mine, exchange(send, rest[k])]
            [mine] = yield add(terms)
            for bit in rest[2:]:
                [mine] = yield add([mine, exchange(mine, bit)])
            for k in (1, 0):
                [mine] = yield join(mine, exchange(mine, rest[k]), k)
        else:
            [mine] = yield add(terms)
            for bit in rest:
                [mine] = yield add([mine, exchange(mine, bit)])
        self.mine = mine
        yield None

    def spread(self):
        self.pieces = [self.mine] + [exchange(self.mine, 1 + k) for k in range(3)]


class Total:
    def __init__(self, part):
        self.steps = self.walk(part)
        self.step = next(self.steps)

    def walk(self, mine):
        def body(at, z, ins, outs):
            outs[0][...] = ins[0][...] + ins[1][...]

        spec = block(mine.shape, lambda i, z: (0, 0))
        theirs = swap(mine)
        for bit in [1 << b for b in range((lax.axis_size("dp") - 1).bit_length())] + [None]:
            [mine] = yield [mine, theirs], [spec] * 2, [spec], [shape(mine.shape, F32)], body
            if bit is not None:
                theirs = exchange(mine, bit)
        self.mine = mine
        yield None


def tick(chain, z, *flows):
    args, in_specs, out_specs, shapes = [], [], [], []
    for f in flows:
        args += f.step[0]
        in_specs += f.step[1]
        out_specs += f.step[2]
        shapes += f.step[3]

    def kernel(z, *refs):
        ins, outs = list(refs[: len(args)]), list(refs[len(args) :])
        for some, _, specs, _, body in steps:
            body(pl.program_id(0), z, ins[: len(some)], outs[: len(specs)])
            del ins[: len(some)], outs[: len(specs)]

    steps = [f.step for f in flows]
    outs = chain.run(kernel, (2,), in_specs, out_specs, shapes, args, prefetch=[z], us=2)
    for f in flows:
        count = len(f.step[2])
        f.step = f.steps.send(outs[:count])
        outs = outs[count:]


def finish(chain, z, *flows):
    while left := [f for f in flows if f.step is not None]:
        tick(chain, z, *left)


def unpack(chain, order, pieces, moves, outputs, shapes):
    kept = [o for o in outputs if o is not None]
    whole = len(pieces) == 1
    rows, width = pieces[0].shape[-2:]

    def kernel(order, *refs):
        pieces_in = refs[: len(pieces)]
        outs = refs[len(pieces) + len(kept) : len(pieces) + len(kept) + len(moves)]
        *scratch, sems = refs[len(pieces) + len(kept) + len(moves) :]
        copies = []
        for k in range(4):
            piece = pieces_in[0].at[k] if whole else pieces_in[k].at[0]
            for m, (at, count, tile, place) in enumerate(moves):
                held = scratch[m]
                for i in range(count // tile):
                    columns = piece[:, at + i * tile : at + (i + 1) * tile].astype(F32)
                    if tile == count:
                        held[k] = columns
                    else:
                        for j in range(rows // tile):
                            held[k, i * tile : (i + 1) * tile, j * tile : (j + 1) * tile] = columns[
                                j * tile : (j + 1) * tile
                            ]
                copy = pltpu.make_async_copy(held.at[k], outs[m].at[place(order[k])], sems.at[k, m])
                copy.start()
                copies.append(copy)
        for copy in copies:
            copy.wait()

    return chain.run(
        kernel,
        (1,),
        [block(p.shape, lambda i, q, n=p.ndim: (0,) * n) for p in pieces] + [ANYWHERE] * len(kept),
        [ANYWHERE] * len(moves),
        [shape(s, F32) for s in shapes],
        list(pieces) + kept,
        prefetch=[order],
        scratch=[
            pltpu.VMEM((4, rows, count) if tile == count else (4, count, rows), F32) for _, count, tile, _ in moves
        ]
        + [pltpu.SemaphoreType.DMA((4, len(moves)))],
        alias={1 + len(pieces) + i: i for i in range(len(kept))},
        us=3,
    )


def across(rows, at, count):
    return lambda q: (pl.ds(pl.multiple_of(q * rows, rows), rows), pl.ds(at, count))


def along(rows, at, count):
    return lambda q: (pl.ds(at, count), pl.ds(pl.multiple_of(q * rows, rows), rows))


def shards(
    tokens,
    segment_ids,
    keep_mask,
    w_query,
    w_key,
    w_value,
    w_out,
    w_gate,
    w_up,
    w_down,
    norm_attn,
    norm_ffn,
    cotangent,
):
    d = tokens.shape[2]
    quarter = d // 4
    n = lax.axis_size("dp")
    own_quarter = lax.rem(lax.axis_index("dp"), 4)
    plain = jnp.arange(4, dtype=jnp.int32)
    y_first = own_quarter ^ plain
    x_first = own_quarter ^ ((plain & 1) * 2 + (plain >> 1))
    scalars = [lax.axis_index("mp").astype(jnp.int32)[None], segment_ids[0], keep_mask[0]]
    groups = [[4 * i + j for j in range(4)] for i in range(n // 4)]

    def scatter(grads):
        return lax.psum_scatter(grads, "dp", scatter_dimension=0, axis_index_groups=groups)[None]

    def gather(flow):
        return lax.all_gather(flow.mine[0], "dp", axis=0, axis_index_groups=groups)

    place = lax.axis_index("dp") // 4
    z = jnp.stack([lax.rem(place, 2), lax.rem(place // 2, 2)]).astype(jnp.int32)

    chain = Chain()
    own, ct_own = tokens[:, 0], cotangent[:, 0]
    gain_attn, gain_ffn = norm_attn[None], norm_ffn[None]
    other, ct_other = swap(own), swap(ct_own)
    first = project(chain, own, gain_attn, w_query, w_key, w_value, 0)
    qkv, normed = project(chain, other, gain_attn, w_query, w_key, w_value, 1, first)
    mixed, lse, attn_part = attend(chain, scalars, qkv, w_out, ct_other)
    hidden, x = middle(chain, own, other, attn_part, swap(attn_part), gain_ffn)

    w0, w1 = FFN_CHUNKS
    chunk = lambda at, width: ffn(chain, plain, x, ct_own, ct_other, w_gate, w_up, w_down, at, width, 1)
    act0, both0, grads = chunk(0, w0)
    flow0 = Flow([scatter(grads)])
    act1, both1, grads = chunk(w0, w1)
    flow1 = Flow([scatter(grads)], split=True)
    back_part = ffn_input_grad(chain, [both0, both1], w_gate, w_up)
    back_theirs = swap(back_part)
    out_own, out_send = ffn_output(chain, [act0, act1], w_down)
    tick(chain, z, flow0)
    grad_in, grad_hidden, gain_ffn_part, result = middle_back(
        chain, back_part, back_theirs, hidden, ct_own, ct_other, gain_ffn, out_own, swap(out_send)
    )
    tick(chain, z, flow0)
    grad_mixed, *grads = out_back(chain, y_first, grad_in, mixed, w_out)
    flow_out = Flow(grads, (2, 1))
    back = lambda order, pair, before=None: attend_back(
        chain, scalars, order, qkv, mixed, grad_mixed, lse, normed, pair, before
    )
    pair0 = back(y_first, 0)
    *pair1, kept, sent = back(y_first, 1, pair0)
    flow3 = Flow([kept, sent], (2, 1))
    tick(chain, z, flow0, flow1, flow_out)
    finish(chain, z, flow0)
    gathered0 = gather(flow0)
    pair2 = back(x_first, 2)
    tick(chain, z, flow1, flow_out, flow3)
    *pair3, kept, sent = back(x_first, 3, pair2)
    flow4 = Flow([kept, sent], (1, 2))
    tick(chain, z, flow1, flow_out, flow3)
    back_own, back_send, gain_parts = qkv_back(
        chain, list(zip(pair0, pair1, pair2, pair3)), [w_query, w_key, w_value], own, other, gain_ffn_part
    )
    gains = Total(gain_parts)
    tick(chain, z, flow1, flow_out, flow3, flow4)
    finish(chain, z, flow_out)
    flow_out.spread()

    hidden_units, width = w_gate.shape[1], w_query.shape[1]
    wide_shapes = [(d, hidden_units), (d, hidden_units), (hidden_units, d)]

    def ffn_moves(at, count):
        return [
            (0, count, count, across(quarter, at, count)),
            (count, count, count, across(quarter, at, count)),
            (2 * count, count, 128, along(quarter, at, count)),
        ]

    def unpack_qkv(order, pieces, at, outputs):
        count = 2 * 128
        moves = [(k * count, count, count, across(quarter, at, count)) for k in range(3)]
        return unpack(chain, order, pieces, moves, outputs, [(d, width)] * 3)

    wide = unpack(chain, plain, [gathered0], ffn_moves(0, w0), [None] * 3, wide_shapes)
    tick(chain, z, flow1, flow3, flow4, gains)
    finish(chain, z, flow1)
    gathered1 = gather(flow1)
    grad_tokens = last(chain, back_own, swap(back_send), own, grad_hidden, gain_attn)
    tick(chain, z, flow4, gains)
    finish(chain, z, flow3)
    flow3.spread()
    [grad_out] = unpack(
        chain, y_first, flow_out.pieces, [(0, width, quarter, along(quarter, 0, width))], [None], [(width, d)]
    )
    tick(chain, z, flow4, gains)
    finish(chain, z, flow4)
    flow4.spread()
    tick(chain, z, gains)
    narrow = unpack_qkv(y_first, flow3.pieces, 0, [None] * 3)
    tick(chain, z, gains)
    finish(chain, z, gains)
    narrow = unpack_qkv(y_first, flow4.pieces, 2 * 128, narrow)
    wide = unpack(chain, plain, [gathered1], ffn_moves(w0, w1), wide, wide_shapes)
    return (
        result[:, None],
        grad_tokens[:, None],
        *narrow,
        grad_out,
        *wide,
        gains.mine[0],
        gains.mine[1],
    )


def solution(mesh):
    return jax.shard_map(
        shards,
        mesh=mesh,
        in_specs=(
            P("mp", "dp", None),
            P("dp", None),
            P("dp", None),
            P(None, "mp"),
            P(None, "mp"),
            P(None, "mp"),
            P("mp", None),
            P(None, "mp"),
            P(None, "mp"),
            P("mp", None),
            P(),
            P(),
            P("mp", "dp", None),
        ),
        out_specs=(
            P("mp", "dp", None),
            P("mp", "dp", None),
            P(None, "mp"),
            P(None, "mp"),
            P(None, "mp"),
            P("mp", None),
            P(None, "mp"),
            P(None, "mp"),
            P("mp", None),
            P(),
            P(),
        ),
        check_vma=False,
    )
```

```python
import functools

import jax
import jax.numpy as jnp
from jax import lax
from jax.experimental import pallas as pl
from jax.experimental.pallas import tpu as pltpu
from jax.sharding import PartitionSpec as P

HDIM = 64
EPSILON = 1e-06
LOG2E = 1.4426950408889634
VMEM_LIMIT = 62 * 1024 * 1024
COST = 1e6
BF = jnp.bfloat16
F32 = jnp.float32
NN = ((1,), (0,))
NT = ((1,), (1,))
TN = ((0,), (0,))
FFN_CHUNKS = (512, 896)


def dot(left, right, dims=NN):
    return lax.dot_general(left, right, (dims, ((), ())), preferred_element_type=F32)


def shape(dims, dtype):
    return jax.ShapeDtypeStruct(dims, dtype)


class Chain:
    def __init__(self):
        self.token = None

    def run(self, kernel, grid, in_specs, out_specs, out_shape, args, prefetch=(), scratch=(), alias=None, us=5):
        before = [] if self.token is None else [self.token]
        some, n_in, n_out = len(prefetch), len(args), len(out_shape)
        skip = len(before)

        def body(*refs):
            kept = refs[: some + n_in] + refs[some + n_in + skip : some + n_in + skip + n_out]
            kernel(*kept, *refs[some + n_in + skip + n_out + 1 :])

        anywhere = pl.BlockSpec(memory_space=pl.ANY)
        *outs, self.token = pl.pallas_call(
            body,
            grid_spec=pltpu.PrefetchScalarGridSpec(
                num_scalar_prefetch=some,
                grid=grid,
                in_specs=list(in_specs) + [anywhere] * skip,
                out_specs=list(out_specs) + [anywhere],
                scratch_shapes=list(scratch),
            ),
            out_shape=list(out_shape) + [shape((8, 128), F32)],
            input_output_aliases=alias or {},
            compiler_params=pltpu.CompilerParams(vmem_limit_bytes=VMEM_LIMIT),
            cost_estimate=pl.CostEstimate(flops=int(us * COST), bytes_accessed=1, transcendentals=0),
        )(*prefetch, *args, *before)
        return outs


ANYWHERE = pl.BlockSpec(memory_space=pl.ANY)


def block(dims, index):
    return pl.BlockSpec(dims, index)


class Copies:
    def __init__(self, sems):
        self.sems, self.started = sems, []

    def start(self, source, target):
        copy = pltpu.make_async_copy(source, target, self.sems.at[len(self.started)])
        copy.start()
        self.started.append(copy)
        return copy


def by_hand(chain, kernel, inputs, outputs, scratch, copies, prefetch=(), alias=None, us=5):
    def body(*refs):
        kernel(*refs[:-1], Copies(refs[-1]))

    return chain.run(
        body,
        (1,),
        [ANYWHERE] * len(inputs),
        [ANYWHERE] * len(outputs),
        outputs,
        inputs,
        prefetch=prefetch,
        scratch=list(scratch) + [pltpu.SemaphoreType.DMA((copies,))],
        alias=alias,
        us=us,
    )


def project(chain, tokens, gain, wq, wk, wv, half, before=()):
    rows, d = tokens.shape
    width = wq.shape[1]
    weights = [wq, wk, wv]

    def kernel(tokens, gain, *refs):
        ws, refs = refs[:3], refs[3 + len(before) :]
        projected, normed, xs, gs, held, out, low, copies = refs
        first = [copies.start(gain, gs), copies.start(tokens, xs)]
        loads = [copies.start(w, held.at[i]) for i, w in enumerate(ws)]
        for c in first:
            c.wait()
        x = xs[...].astype(F32)
        r = lax.rsqrt(jnp.mean(x * x, axis=-1, keepdims=True) + EPSILON)
        low[...] = (x * r * gs[...]).astype(BF)
        here = pl.ds(half * rows, rows)
        stores = [copies.start(low, normed.at[here])]
        for i in range(3):
            loads[i].wait()
            out[i] = dot(low[...], held[i]).astype(BF)
            stores.append(copies.start(out.at[i], projected.at[here, pl.ds(i * width, width)]))
        for c in stores:
            c.wait()

    return by_hand(
        chain,
        kernel,
        [tokens, gain, *weights, *before],
        [shape((2 * rows, 3 * width), BF), shape((2 * rows, d), BF)],
        [
            pltpu.VMEM((rows, d), BF),
            pltpu.VMEM((1, d), F32),
            pltpu.VMEM((3, d, width), BF),
            pltpu.VMEM((3, rows, width), BF),
            pltpu.VMEM((rows, d), BF),
        ],
        9,
        alias={5: 0, 6: 1} if before else None,
    )


def layout(place, segs, keep, slot):
    last, mid = 4 * slot - 1, 2 * slot
    leads = jnp.logical_or(segs[0, 0] != segs[0, mid], keep[0, 0] == 0)
    start = jnp.where(leads, 1, 0) + 2 * place[0]
    padded = jnp.where(jnp.where(leads, keep[0, 0], keep[0, last]) == 0, 1, 0)
    return (lambda logical: pl.ds(pl.multiple_of(lax.rem(logical + start, 4) * slot, slot), slot)), padded


def two_heads(columns):
    slot = columns.shape[1]
    zero = jnp.zeros((HDIM, slot), BF)
    first = jnp.concatenate([columns[:HDIM], zero], 0)
    second = jnp.concatenate([zero, columns[HDIM:]], 0)
    return jnp.concatenate([first, second], 1)


def attend(chain, scalars, qkv, w_out, early):
    seq, width = qkv.shape[0], qkv.shape[1] // 3
    d = w_out.shape[1]
    pairs, slot, half = width // 128, seq // 4, seq // 2
    scale = HDIM**-0.5 * LOG2E

    def kernel(place, segs, keep, q_ref, k_ref, v_ref, w_all, early, o_ref, lse_ref, part, mixed, ws, out, sems):
        step = pl.program_id(0)
        rows, padded = layout(place, segs, keep, slot)
        load = pltpu.make_async_copy(w_all, ws, sems.at[0])

        @pl.when(step == 0)
        def _():
            load.start()

        one = jnp.ones((16, slot), BF)
        slots = [[j if at < 3 else jnp.where(padded > 0, j, 3) for j in range(3)] for at in range(4)]

        def scores_of(at):
            q2 = two_heads(q_ref[rows(at), :].T)
            return [dot(k_ref[rows(j), :], q2) for j in slots[at]]

        coming = scores_of(0)
        for at in range(4):
            scores = coming
            if at < 3:
                coming = scores_of(at + 1)
            top = functools.reduce(jnp.maximum, [jnp.max(s, axis=0, keepdims=True) for s in scores])
            oa = jnp.zeros((HDIM + 16, slot), F32)
            ob = oa
            for j, s in zip(slots[at], scores):
                p = jnp.exp2((s - top) * scale).astype(BF)
                vt = v_ref[rows(j), :].T
                oa += dot(jnp.concatenate([vt[:HDIM], one], 0), p[:, :slot])
                ob += dot(jnp.concatenate([vt[HDIM:], one], 0), p[:, slot:])
            la, lb = oa[HDIM : HDIM + 1], ob[HDIM : HDIM + 1]
            o = jnp.concatenate([oa[:HDIM] / la, ob[:HDIM] / lb], 0).astype(BF).T
            o_ref[rows(at), :] = o
            mixed[step, rows(at), :] = o
            lse = top * HDIM**-0.5 + jnp.log(jnp.concatenate([la, lb], 1))
            lse_ref[0, 0:1, rows(at)] = lse[:, :slot]
            lse_ref[0, 1:2, rows(at)] = lse[:, slot:]

        @pl.when(step == pairs - 1)
        def _():
            load.wait()
            stores = []
            for k in range(2):
                here = slice(k * half, (k + 1) * half)
                every = jnp.concatenate([mixed[p, here, :] for p in range(pairs)], 1)
                out[here] = dot(every, ws[...]).astype(BF)
                stores.append(pltpu.make_async_copy(out.at[here], part.at[here], sems.at[1 + k]))
                stores[-1].start()
            for c in stores:
                c.wait()

    column = lambda off: block((seq, 128), lambda p, *m: (0, p + off))
    return chain.run(
        kernel,
        (pairs,),
        [column(0), column(pairs), column(2 * pairs), ANYWHERE, ANYWHERE],
        [column(0), block((1, 2, seq), lambda p, *m: (p, 0, 0)), ANYWHERE],
        [shape((seq, width), BF), shape((pairs, 2, seq), F32), shape((seq, d), BF)],
        [qkv, qkv, qkv, w_out, early],
        prefetch=scalars,
        scratch=[
            pltpu.VMEM((pairs, seq, 128), BF),
            pltpu.VMEM((width, d), BF),
            pltpu.VMEM((seq, d), BF),
            pltpu.SemaphoreType.DMA((3,)),
        ],
        us=26,
    )


def attend_back(chain, scalars, order, qkv, mixed, grad_mixed, lse, normed, first, before=None, g=None):
    seq, width = qkv.shape[0], qkv.shape[1] // 3
    d = normed.shape[1]
    pairs, slot, quarter = width // 128, seq // 4, d // 4
    scale = HDIM**-0.5 * LOG2E

    def kernel(
        place, segs, keep, order, q_ref, k_ref, v_ref, o_ref, do_ref, lse_ref, *refs
    ):
        rows, padded = layout(place, segs, keep, slot)
        if before is None:
            dq_ref, dk_ref, dv_ref, dk_sum, dv_sum = refs
        else:
            normed_all, g_all, mixed_all, *old = refs[:6]
            dq_ref, dk_ref, dv_ref, kept, sent, dk_sum, dv_sum, every, ns, held, gs, ms, sems = refs[6:]
            copies = Copies(sems)
            loads = [copies.start(normed_all, ns), copies.start(g_all, gs), copies.start(mixed_all, ms)]
            loads += [copies.start(o, every.at[i]) for i, o in enumerate(old)]

        def stacked(x):
            lane = lax.broadcasted_iota(jnp.int32, (slot, 128), 1)
            zero = jnp.zeros_like(x)
            return jnp.concatenate([jnp.where(lane < HDIM, x, zero), jnp.where(lane < HDIM, zero, x)], 0)

        def extended(columns, tail):
            high = tail.astype(BF).astype(F32)
            rest = tail - high
            middle = rest.astype(BF).astype(F32)
            extra = jnp.concatenate([high, middle, rest - middle, jnp.zeros((125, 2 * slot), F32)], 0).astype(BF)
            return jnp.concatenate([two_heads(columns), extra], 0)

        def one_slot(at, slots):
            ones = jnp.ones((slot, 128), BF)
            q, do = q_ref[rows(at), :], do_ref[rows(at), :]
            do_t = do.T
            prod = do_t.astype(F32) * o_ref[rows(at), :].T.astype(F32)
            delta = jnp.concatenate(
                [jnp.sum(prod[:HDIM], 0, keepdims=True), jnp.sum(prod[HDIM:], 0, keepdims=True)], 1
            )
            lse = jnp.concatenate([lse_ref[0, 0:1, rows(at)], lse_ref[0, 1:2, rows(at)]], 1)
            q2 = extended(q.T, lse * -(HDIM**0.5))
            do2 = extended(do_t, -delta)
            qs, dos = stacked(q), stacked(do)
            dqa = jnp.zeros((HDIM, slot), F32)
            dqb = dqa
            for j in slots:
                k, v = k_ref[rows(j), :], v_ref[rows(j), :]
                p = jnp.exp2(dot(jnp.concatenate([k, ones], 1), q2) * scale)
                dp = dot(jnp.concatenate([v, ones], 1), do2)
                ds = (p * dp).astype(BF)
                dv_sum[rows(j), :] += dot(p.astype(BF), dos)
                dk_sum[rows(j), :] += dot(ds, qs)
                kt = k.T
                dqa += dot(kt[:HDIM], ds[:, :slot])
                dqb += dot(kt[HDIM:], ds[:, slot:])
            dq_ref[rows(at), :] = (jnp.concatenate([dqa, dqb], 0) * HDIM**-0.5).astype(BF).T

        dk_sum[...] = jnp.zeros_like(dk_sum)
        dv_sum[...] = jnp.zeros_like(dv_sum)

        def body(at, carry):
            alone = jnp.logical_and(at == 3, padded == 0)
            one_slot(at, [jnp.where(alone, 3, j) for j in range(3)])
            return carry

        lax.fori_loop(0, 4, body, 0)
        dk = (dk_sum[...] * HDIM**-0.5).astype(BF)
        dv = dv_sum[...].astype(BF)
        dk_ref[...] = dk
        dv_ref[...] = dv
        if before is not None:
            for c in loads:
                c.wait()
            right = jnp.concatenate([every[0], dq_ref[...], every[1], dk, every[2], dv], 1)
            stores = []
            for k in range(4):
                held[k, :, :wide] = dot(column_block(ns, order[k], quarter), right, TN).astype(BF)
                part = dot(ms[...], column_block(gs, order[k], quarter), TN).astype(BF)
                for i in range(width // quarter):
                    held[k, :, wide + i * quarter : wide + (i + 1) * quarter] = part[i * quarter : (i + 1) * quarter]
                stores.append(copies.start(held.at[k], quarters_of([kept, sent])[k]))
            for c in stores:
                c.wait()

    column = lambda off: block((seq, 128), lambda p, *m: (0, off))
    wide = 3 * 2 * 128
    more = before is not None
    return chain.run(
        kernel,
        (1,),
        [
            column(first),
            column(first + pairs),
            column(first + 2 * pairs),
            column(first),
            column(first),
            block((1, 2, seq), lambda p, *m: (first, 0, 0)),
        ]
        + [ANYWHERE] * (6 * more),
        [column(0)] * 3 + [ANYWHERE] * (2 * more),
        [shape((seq, 128), BF)] * 3 + quarter_shapes(2 * more, quarter, wide + width),
        [qkv, qkv, qkv, mixed, grad_mixed, lse] + ([normed, g, mixed, *before] if more else []),
        prefetch=scalars + [order],
        scratch=[pltpu.VMEM((seq, 128), F32)] * 2
        + [
            pltpu.VMEM((3, seq, 128), BF),
            pltpu.VMEM((seq, d), BF),
            pltpu.VMEM((4, quarter, wide + width), BF),
            pltpu.VMEM((seq, d), BF),
            pltpu.VMEM((seq, width), BF),
            pltpu.SemaphoreType.DMA((10,)),
        ]
        * more,
        us=13,
    )


def middle(chain, own, other, mine, theirs, gain, tile=384):
    half, d = own.shape
    n = 2 * half // tile
    rows = lambda f: block((tile, d), lambda i: (f(i), 0))

    def kernel(own, other, mine, theirs, gain, hidden, normed):
        tokens = jnp.where(pl.program_id(0) < n // 2, own[...], other[...]).astype(F32)
        h = tokens + (mine[...].astype(F32) + theirs[...].astype(F32))
        r = lax.rsqrt(jnp.mean(h * h, axis=-1, keepdims=True) + EPSILON)
        low = (h * r * gain[...]).astype(BF)
        hidden[...] = h
        normed[...] = low

    return chain.run(
        kernel,
        (n,),
        [
            rows(lambda i: jnp.minimum(i, n // 2 - 1)),
            rows(lambda i: jnp.maximum(i - n // 2, 0)),
            rows(lambda i: i),
            rows(lambda i: lax.rem(i + n // 2, n)),
            block((1, d), lambda i: (0, 0)),
        ],
        [rows(lambda i: i), rows(lambda i: i)],
        [shape((2 * half, d), F32), shape((2 * half, d), BF)],
        [own, other, mine, theirs, gain],
        us=5,
    )


def gelu_parts(v):
    c = 0.7978845608028654
    square = v * v
    share = 0.5 + 0.5 * jnp.tanh(v * (c + (c * 0.044715) * square))
    value = v * share
    return value, share + value * (1.0 - share) * (2 * c + (6 * c * 0.044715) * square)


def column_block(ref, number, width):
    return ref[:, pl.ds(pl.multiple_of(number * width, width), width)]


def quarters_of(outs):
    each = 4 // len(outs)
    return [outs[k // each].at[k % each] for k in range(4)]


def quarter_shapes(pieces, rows, width):
    return [shape((4 // pieces, rows, width), BF)] * pieces if pieces else []


def weight_quarters(copies, order, xs, cs, acts, boths, held, targets, quarter, beside=None):
    width = acts.shape[1]
    stores = []
    for k in range(4):
        sides = dot(column_block(xs, order[k], quarter), boths[...], TN)
        down = dot(acts[...], column_block(cs, order[k], quarter), TN).astype(BF)
        held[k, :, : 2 * width] = sides.astype(BF)
        for i in range(width // 128):
            rows = down[i * 128 : (i + 1) * 128]
            place = slice(2 * width + i * 128, 2 * width + (i + 1) * 128)
            held[k, :128, place] = rows[:, :128]
            held[k, 128:, place] = rows[:, 128:]
        if beside is not None:
            beside(k)
        stores.append(copies.start(held.at[k], targets[k]))
    return stores


def ffn(chain, order, x, ct_own, ct_other, w_gate, w_up, w_down, at, width, finish):
    seq, d = x.shape
    half, quarter = seq // 2, d // 4

    def kernel(order, x, ct_own, ct_other, wg_all, wu_all, wd_all, act, both, *refs):
        grads, (xs, cs, wg, wu, wd, acts, boths, *held, copies) = refs[:finish], refs[finish:]
        halves = [slice(0, half), slice(half, seq)]
        x0 = copies.start(x.at[halves[0]], xs.at[halves[0]])
        units = pl.ds(at, width)
        lg = copies.start(wg_all.at[:, units], wg)
        lu = copies.start(wu_all.at[:, units], wu)
        c0 = copies.start(ct_own, cs.at[halves[0]])
        ld = copies.start(wd_all.at[units, :], wd)
        x1 = copies.start(x.at[halves[1]], xs.at[halves[1]])
        c1 = copies.start(ct_other, cs.at[halves[1]])
        waits = [[x0, lg], [lu], [c0, ld]], [[x1], [], [c1]]
        stores = []
        for here, (for_gate, for_up, for_act) in zip(halves, waits):
            for c in for_gate:
                c.wait()
            gate = dot(xs[here], wg[...])
            for c in for_up:
                c.wait()
            up = dot(xs[here], wu[...])
            for c in for_act:
                c.wait()
            grad_act = dot(cs[here], wd[...], NT)
            value, slope = gelu_parts(gate)
            acts[here] = (value * up).astype(BF)
            boths[here, :width] = (grad_act * up * slope).astype(BF)
            boths[here, width:] = (grad_act * value).astype(BF)
            stores.append(copies.start(acts.at[here], act.at[here]))
            stores.append(copies.start(boths.at[here], both.at[here]))
        if finish:
            targets = quarters_of(grads)
            stores += weight_quarters(copies, order, xs, cs, acts, boths, held[0], targets, quarter)
        for c in stores:
            c.wait()

    return by_hand(
        chain,
        kernel,
        [x, ct_own, ct_other, w_gate, w_up, w_down],
        [shape((seq, width), BF), shape((seq, 2 * width), BF)] + quarter_shapes(finish, quarter, 3 * width),
        [
            pltpu.VMEM((seq, d), BF),
            pltpu.VMEM((seq, d), BF),
            pltpu.VMEM((d, width), BF),
            pltpu.VMEM((d, width), BF),
            pltpu.VMEM((width, d), BF),
            pltpu.VMEM((seq, width), BF),
            pltpu.VMEM((seq, 2 * width), BF),
        ]
        + [pltpu.VMEM((4, quarter, 3 * width), BF)] * min(finish, 1),
        15,
        prefetch=[order],
        us=16 if finish else 8,
    )


def ffn_input_grad(chain, boths, wg, wu):
    seq = boths[0].shape[0]
    d, units = wg.shape
    half, chunks = seq // 2, len(boths)
    starts = [sum(b.shape[1] for b in boths[:k]) // 2 for k in range(chunks + 1)]

    def kernel(*refs):
        ins, (wg, wu, back, *held, wgs, wus, out, copies) = refs[:chunks], refs[chunks:]
        loads = []
        for k in range(chunks):
            units = pl.ds(starts[k], starts[k + 1] - starts[k])
            loads.append(
                [
                    copies.start(ins[k].at[pl.ds(0, half)], held[k].at[pl.ds(0, half)]),
                    copies.start(wg.at[:, units], wgs.at[:, units]),
                    copies.start(wu.at[:, units], wus.at[:, units]),
                ]
            )
        later = [copies.start(ins[k].at[pl.ds(half, half)], held[k].at[pl.ds(half, half)]) for k in range(chunks)]
        stores = []
        for h in range(2):
            here = slice(h * half, (h + 1) * half)
            total = None
            for k in range(chunks):
                for c in loads[k] if h == 0 else [later[k]]:
                    c.wait()
                width = starts[k + 1] - starts[k]
                units = slice(starts[k], starts[k + 1])
                part = dot(held[k][here, :width], wgs[:, units], NT) + dot(held[k][here, width:], wus[:, units], NT)
                total = part if total is None else total + part
            out[here] = total.astype(BF)
            stores.append(copies.start(out.at[here], back.at[here]))
        for c in stores:
            c.wait()

    return by_hand(
        chain,
        kernel,
        boths + [wg, wu],
        [shape((seq, d), BF)],
        [pltpu.VMEM(b.shape, BF) for b in boths]
        + [pltpu.VMEM((d, units), BF), pltpu.VMEM((d, units), BF), pltpu.VMEM((seq, d), BF)],
        4 * chunks + 2,
        us=13,
    )[0]


def ffn_output(chain, acts, wd):
    seq, d = acts[0].shape[0], wd.shape[1]
    half, chunks = seq // 2, len(acts)
    starts = [sum(a.shape[1] for a in acts[:k]) for k in range(chunks + 1)]

    def kernel(*refs):
        ins, (wd, own, send, *held, wds, out_own, out_send, copies) = refs[:chunks], refs[chunks:]
        first, second = pl.ds(half, half), pl.ds(0, half)
        loads = []
        for k in range(chunks):
            units = pl.ds(starts[k], starts[k + 1] - starts[k])
            loads.append([copies.start(ins[k].at[first], held[k].at[first]), copies.start(wd.at[units], wds.at[units])])
        later = [copies.start(ins[k].at[second], held[k].at[second]) for k in range(chunks)]
        stores = []
        for h, (here, target, out) in enumerate([(first, out_send, send), (second, out_own, own)]):
            total = None
            for k in range(chunks):
                for c in loads[k] if h == 0 else [later[k]]:
                    c.wait()
                part = dot(held[k][here], wds[starts[k] : starts[k + 1]])
                total = part if total is None else total + part
            target[...] = total.astype(target.dtype)
            stores.append(copies.start(target, out))
        for c in stores:
            c.wait()

    return by_hand(
        chain,
        kernel,
        acts + [wd],
        [shape((half, d), F32), shape((half, d), BF)],
        [pltpu.VMEM(a.shape, BF) for a in acts]
        + [pltpu.VMEM(wd.shape, BF), pltpu.VMEM((half, d), F32), pltpu.VMEM((half, d), BF)],
        3 * chunks + 2,
        us=7,
    )


def norm_back(value, gain, grad):
    r = lax.rsqrt(jnp.mean(value * value, axis=-1, keepdims=True) + EPSILON)
    u = grad * gain
    inner = jnp.mean(u * value, axis=-1, keepdims=True)
    return r * u - value * (r * r * r * inner), jnp.sum(grad * value * r, axis=0, keepdims=True)


def add_up(at, total, part):
    @pl.when(at == 0)
    def _():
        total[...] = part

    @pl.when(at > 0)
    def _():
        total[...] += part


def middle_back(chain, mine, theirs, hidden, ct_own, ct_other, gain, out_own, out_theirs, tile=384):
    seq, d = hidden.shape
    n = seq // tile
    rows = lambda f: block((tile, d), lambda i: (f(i), 0))
    front = rows(lambda i: jnp.minimum(i, n // 2 - 1))

    def kernel(mine, theirs, hidden, ct_own, ct_other, gain, out_own, out_theirs, low, keep, gain_grad, result):
        at = pl.program_id(0)
        h = hidden[...]
        through, part = norm_back(h, gain[...], mine[...].astype(F32) + theirs[...].astype(F32))
        ct = jnp.where(at < n // 2, ct_own[...], ct_other[...])
        total = ct.astype(F32) + through
        low[...] = total.astype(BF)
        add_up(at, gain_grad, part)

        @pl.when(at < n // 2)
        def _():
            keep[...] = total
            result[...] = (h + (out_own[...] + out_theirs[...].astype(F32))).astype(BF)

    return chain.run(
        kernel,
        (n,),
        [
            rows(lambda i: i),
            rows(lambda i: lax.rem(i + n // 2, n)),
            rows(lambda i: i),
            front,
            rows(lambda i: jnp.maximum(i - n // 2, 0)),
            block((1, d), lambda i: (0, 0)),
            front,
            front,
        ],
        [rows(lambda i: i), front, block((1, d), lambda i: (0, 0)), front],
        [shape((seq, d), BF), shape((seq // 2, d), F32), shape((1, d), F32), shape((seq // 2, d), BF)],
        [mine, theirs, hidden, ct_own, ct_other, gain, out_own, out_theirs],
        us=8,
    )


def out_back(chain, g, w_out):
    seq, d = g.shape
    width, half = w_out.shape[0], seq // 2

    def kernel(g, w_out, grad_mixed, gs, ws, out, copies):
        halves = [pl.ds(0, half), pl.ds(half, half)]
        loads = [[copies.start(g.at[halves[0]], gs.at[halves[0]]), copies.start(w_out, ws)]]
        loads.append([copies.start(g.at[halves[1]], gs.at[halves[1]])])
        stores = []
        for here, waits in zip(halves, loads):
            for c in waits:
                c.wait()
            out[here] = dot(gs[here], ws[...], NT).astype(BF)
            stores.append(copies.start(out.at[here], grad_mixed.at[here]))
        for c in stores:
            c.wait()

    return by_hand(
        chain,
        kernel,
        [g, w_out],
        [shape((seq, width), BF)],
        [pltpu.VMEM((seq, d), BF), pltpu.VMEM((width, d), BF), pltpu.VMEM((seq, width), BF)],
        5,
        us=8,
    )[0]


def qkv_back(chain, order, grads, weights, normed, own, other, gain_ffn_grad):
    flat = [g for kind in grads for g in kind]
    count = len(flat)
    pieces = len(grads[0])
    seq = flat[0].shape[0]
    d, width = weights[0].shape
    half, quarter = seq // 2, d // 4
    wide = 3 * sum(g.shape[1] for g in grads[0][-2:])

    def kernel(order, *refs):
        ins, ws, refs = refs[:count], refs[count : count + 3], refs[count + 3 :]
        normed, t_own, t_other, ffn_part, own, send, gains, kept, sent, *held = refs
        *held, wh, ts, ffn, sums, out_own, out_send, ns, out, copies = held
        first, second = pl.ds(half, half), pl.ds(0, half)
        loads = [[copies.start(ins[i].at[first], held[i].at[first])] for i in range(count)]
        for i in range(3):
            loads[i * pieces].append(copies.start(ws[i], wh.at[i]))
        later = [[copies.start(ins[i].at[second], held[i].at[second])] for i in range(count)]
        all_normed = copies.start(normed, ns)
        tokens = [copies.start(t_other, ts.at[1]), copies.start(t_own, ts.at[0]), copies.start(ffn_part, ffn)]
        stores = []
        gain = 0.0
        for k, (here, waits, target, goal) in enumerate([(first, loads, out_send, send), (second, later, out_own, own)]):
            total = 0.0
            for kind in range(3):
                some = range(kind * pieces, (kind + 1) * pieces)
                for i in some:
                    for c in waits[i]:
                        c.wait()
                left = jnp.concatenate([held[i][here] for i in some], 1)
                total += dot(left, wh[kind], NT)
            target[...] = total.astype(target.dtype)
            stores.append(copies.start(target, goal))
            tokens[k].wait()
            x = ts[1 - k].astype(F32)
            r = lax.rsqrt(jnp.mean(x * x, axis=-1, keepdims=True) + EPSILON)
            gain += jnp.sum(total * (x * r), axis=0, keepdims=True)
        all_normed.wait()
        right = jnp.concatenate([held[kind * pieces + p][...] for kind in range(3) for p in (pieces - 2, pieces - 1)], 1)
        for k in range(4):
            out[k] = dot(column_block(ns, order[k], quarter), right, TN).astype(BF)
            stores.append(copies.start(out.at[k], quarters_of([kept, sent])[k]))
        tokens[2].wait()
        sums[0:1] = gain
        sums[1:2] = 0.5 * ffn[...]
        stores.append(copies.start(sums, gains))
        for c in stores:
            c.wait()

    return by_hand(
        chain,
        kernel,
        flat + list(weights) + [normed, own, other, gain_ffn_grad],
        [shape((half, d), F32), shape((half, d), BF), shape((2, d), F32)] + quarter_shapes(2, quarter, wide),
        [pltpu.VMEM(g.shape, BF) for g in flat]
        + [
            pltpu.VMEM((3, d, width), BF),
            pltpu.VMEM((2, half, d), BF),
            pltpu.VMEM((1, d), F32),
            pltpu.VMEM((2, d), F32),
            pltpu.VMEM((half, d), F32),
            pltpu.VMEM((half, d), BF),
            pltpu.VMEM((seq, d), BF),
            pltpu.VMEM((4, quarter, wide), BF),
        ],
        2 * count + 14,
        prefetch=[order],
        us=8,
    )


def last(chain, mine, theirs, tokens, grad_hidden, gain, tile=384):
    rows, d = tokens.shape
    row = block((tile, d), lambda i: (i, 0))

    def kernel(mine, theirs, tokens, grad_hidden, gain, out):
        grad = mine[...] + theirs[...].astype(F32)
        out[...] = (grad_hidden[...] + norm_back(tokens[...].astype(F32), gain[...], grad)[0]).astype(BF)

    return chain.run(
        kernel,
        (rows // tile,),
        [row] * 4 + [block((1, d), lambda i: (0, 0))],
        [row],
        [shape((rows, d), BF)],
        [mine, theirs, tokens, grad_hidden, gain],
        us=4,
    )[0]


def swap(x):
    return lax.ppermute(x, "mp", [(0, 1), (1, 0)])


def exchange(x, bit):
    return lax.ppermute(x, "dp", [(i, i ^ bit) for i in range(lax.axis_size("dp"))])


def add(terms, pieces=1):
    n, rows, width = terms[0].shape
    tile = rows // 2

    def body(at, z, ins, outs):
        for k, out in enumerate(outs):
            out[0] = sum(t[k].astype(F32) for t in ins).astype(BF)

    spec = block((n, tile, width), lambda i, z: (0, i, 0))
    out = block((1, tile, width), lambda i, z: (0, i, 0))
    return list(terms), [spec] * len(terms), [out] * n, [shape((1, rows, width), BF)] * n, body


def halve(terms, bit):
    _, rows, width = terms[0].shape
    tile = rows // 4

    def body(at, z, ins, outs):
        for k in range(2):
            outs[k][0] = sum(t[0].astype(F32) for t in ins[k::2]).astype(BF)

    mine = block((1, tile, width), lambda i, z: (0, 2 * z[bit] + i, 0))
    others = block((1, tile, width), lambda i, z: (0, 2 * (1 - z[bit]) + i, 0))
    out = block((1, tile, width), lambda i, z: (0, i, 0))
    return (
        [t for t in terms for _ in range(2)],
        [mine, others] * len(terms),
        [out] * 2,
        [shape((1, rows // 2, width), BF)] * 2,
        body,
    )


def join(mine, theirs, bit):
    _, rows, width = mine.shape

    def body(at, z, ins, outs):
        outs[0][0] = jnp.where(at == z[bit], ins[0][0], ins[1][0])

    spec = block((1, rows, width), lambda i, z: (0, 0, 0))
    out = block((1, rows, width), lambda i, z: (0, i, 0))
    return [mine, theirs], [spec] * 2, [out], [shape((1, 2 * rows, width), BF)], body


class Flow:
    def __init__(self, quarters, bits=(1, 2), split=False):
        rest = [1 << b for b in range(2, (lax.axis_size("dp") - 1).bit_length())]
        self.steps = self.walk(quarters, bits, rest, split)
        self.step = next(self.steps)

    def walk(self, quarters, bits, rest, split):
        if len(quarters) == 2:
            keep, send = quarters
            mine, send = yield add([keep, exchange(send, bits[0])])
            terms = [mine, exchange(send, bits[1])]
        else:
            terms = list(quarters)
        if split:
            for k in range(2):
                mine, send = yield halve(terms, k)
                terms = [mine, exchange(send, rest[k])]
            [mine] = yield add(terms)
            for bit in rest[2:]:
                [mine] = yield add([mine, exchange(mine, bit)])
            for k in (1, 0):
                [mine] = yield join(mine, exchange(mine, rest[k]), k)
        else:
            [mine] = yield add(terms)
            for bit in rest:
                [mine] = yield add([mine, exchange(mine, bit)])
        self.mine = mine
        yield None

    def spread(self):
        self.pieces = [self.mine] + [exchange(self.mine, 1 + k) for k in range(3)]


class Total:
    def __init__(self, part):
        self.steps = self.walk(part)
        self.step = next(self.steps)

    def walk(self, mine):
        def body(at, z, ins, outs):
            outs[0][...] = ins[0][...] + ins[1][...]

        spec = block(mine.shape, lambda i, z: (0, 0))
        theirs = swap(mine)
        for bit in [1 << b for b in range((lax.axis_size("dp") - 1).bit_length())] + [None]:
            [mine] = yield [mine, theirs], [spec] * 2, [spec], [shape(mine.shape, F32)], body
            if bit is not None:
                theirs = exchange(mine, bit)
        self.mine = mine
        yield None


def tick(chain, z, *flows):
    args, in_specs, out_specs, shapes = [], [], [], []
    for f in flows:
        args += f.step[0]
        in_specs += f.step[1]
        out_specs += f.step[2]
        shapes += f.step[3]

    def kernel(z, *refs):
        ins, outs = list(refs[: len(args)]), list(refs[len(args) :])
        for some, _, specs, _, body in steps:
            body(pl.program_id(0), z, ins[: len(some)], outs[: len(specs)])
            del ins[: len(some)], outs[: len(specs)]

    steps = [f.step for f in flows]
    outs = chain.run(kernel, (2,), in_specs, out_specs, shapes, args, prefetch=[z], us=2)
    for f in flows:
        count = len(f.step[2])
        f.step = f.steps.send(outs[:count])
        outs = outs[count:]


def finish(chain, z, *flows):
    while left := [f for f in flows if f.step is not None]:
        tick(chain, z, *left)


def unpack(chain, order, pieces, moves, outputs, shapes):
    kept = [o for o in outputs if o is not None]
    whole = len(pieces) == 1
    rows, width = pieces[0].shape[-2:]

    def kernel(order, *refs):
        pieces_in = refs[: len(pieces)]
        outs = refs[len(pieces) + len(kept) : len(pieces) + len(kept) + len(shapes)]
        *scratch, sems = refs[len(pieces) + len(kept) + len(shapes) :]
        copies = []
        for k in range(4):
            piece = pieces_in[0].at[k] if whole else pieces_in[k].at[0]
            for m, (goal, at, count, tile, place) in enumerate(moves):
                held = scratch[m]
                for i in range(count // tile):
                    columns = piece[:, at + i * tile : at + (i + 1) * tile].astype(F32)
                    if tile == count:
                        held[k] = columns
                    else:
                        for j in range(rows // tile):
                            held[k, i * tile : (i + 1) * tile, j * tile : (j + 1) * tile] = columns[
                                j * tile : (j + 1) * tile
                            ]
                copy = pltpu.make_async_copy(held.at[k], outs[goal].at[place(order[k])], sems.at[k, m])
                copy.start()
                copies.append(copy)
        for copy in copies:
            copy.wait()

    return chain.run(
        kernel,
        (1,),
        [block(p.shape, lambda i, q, n=p.ndim: (0,) * n) for p in pieces] + [ANYWHERE] * len(kept),
        [ANYWHERE] * len(shapes),
        [shape(s, F32) for s in shapes],
        list(pieces) + kept,
        prefetch=[order],
        scratch=[
            pltpu.VMEM((4, rows, count) if tile == count else (4, count, rows), F32) for _, _, count, tile, _ in moves
        ]
        + [pltpu.SemaphoreType.DMA((4, len(moves)))],
        alias={1 + len(pieces) + i: i for i in range(len(kept))},
        us=3,
    )


def across(rows, at, count):
    return lambda q: (pl.ds(pl.multiple_of(q * rows, rows), rows), pl.ds(at, count))


def along(rows, at, count):
    return lambda q: (pl.ds(at, count), pl.ds(pl.multiple_of(q * rows, rows), rows))


def shards(
    tokens,
    segment_ids,
    keep_mask,
    w_query,
    w_key,
    w_value,
    w_out,
    w_gate,
    w_up,
    w_down,
    norm_attn,
    norm_ffn,
    cotangent,
):
    d = tokens.shape[2]
    quarter = d // 4
    n = lax.axis_size("dp")
    own_quarter = lax.rem(lax.axis_index("dp"), 4)
    plain = jnp.arange(4, dtype=jnp.int32)
    y_first = own_quarter ^ plain
    x_first = own_quarter ^ ((plain & 1) * 2 + (plain >> 1))
    scalars = [lax.axis_index("mp").astype(jnp.int32)[None], segment_ids, keep_mask]
    groups = [[4 * i + j for j in range(4)] for i in range(n // 4)]

    def scatter(grads):
        return lax.psum_scatter(grads, "dp", scatter_dimension=0, axis_index_groups=groups)[None]

    def gather(flow):
        return lax.all_gather(flow.mine[0], "dp", axis=0, axis_index_groups=groups)

    place = lax.axis_index("dp") // 4
    z = jnp.stack([lax.rem(place, 2), lax.rem(place // 2, 2)]).astype(jnp.int32)

    chain = Chain()
    own, ct_own = tokens[:, 0], cotangent[:, 0]
    gain_attn, gain_ffn = norm_attn[None], norm_ffn[None]
    other, ct_other = swap(own), swap(ct_own)
    first = project(chain, own, gain_attn, w_query, w_key, w_value, 0)
    qkv, normed = project(chain, other, gain_attn, w_query, w_key, w_value, 1, first)
    mixed, lse, attn_part = attend(chain, scalars, qkv, w_out, ct_other)
    hidden, x = middle(chain, own, other, attn_part, swap(attn_part), gain_ffn)

    w0, w1 = FFN_CHUNKS
    chunk = lambda at, width: ffn(chain, plain, x, ct_own, ct_other, w_gate, w_up, w_down, at, width, 1)
    act0, both0, grads = chunk(0, w0)
    flow0 = Flow([scatter(grads)])
    act1, both1, grads = chunk(w0, w1)
    flow1 = Flow([scatter(grads)], split=True)
    back_part = ffn_input_grad(chain, [both0, both1], w_gate, w_up)
    back_theirs = swap(back_part)
    out_own, out_send = ffn_output(chain, [act0, act1], w_down)
    tick(chain, z, flow0)
    grad_in, grad_hidden, gain_ffn_part, result = middle_back(
        chain, back_part, back_theirs, hidden, ct_own, ct_other, gain_ffn, out_own, swap(out_send)
    )
    tick(chain, z, flow0)
    grad_mixed = out_back(chain, grad_in, w_out)
    back = lambda order, pair, *more: attend_back(
        chain, scalars, order, qkv, mixed, grad_mixed, lse, normed, pair, *more
    )
    pair0 = back(y_first, 0)
    *pair1, kept, sent = back(y_first, 1, pair0, grad_in)
    flow3 = Flow([kept, sent], (2, 1))
    tick(chain, z, flow0, flow1)
    finish(chain, z, flow0)
    gathered0 = gather(flow0)
    pair2 = back(x_first, 2)
    tick(chain, z, flow1)
    pair3 = back(x_first, 3)
    tick(chain, z, flow1, flow3)
    back_own, back_send, gain_parts, kept, sent = qkv_back(
        chain,
        x_first,
        list(zip(pair0, pair1, pair2, pair3)),
        [w_query, w_key, w_value],
        normed,
        own,
        other,
        gain_ffn_part,
    )
    flow4 = Flow([kept, sent], (1, 2))
    gains = Total(gain_parts)
    tick(chain, z, flow1, flow3, gains)

    hidden_units, width = w_gate.shape[1], w_query.shape[1]
    wide_shapes = [(d, hidden_units), (d, hidden_units), (hidden_units, d)]

    def ffn_moves(at, count):
        return [
            (0, 0, count, count, across(quarter, at, count)),
            (1, count, count, count, across(quarter, at, count)),
            (2, 2 * count, count, 128, along(quarter, at, count)),
        ]

    wide = unpack(chain, plain, [gathered0], ffn_moves(0, w0), [None] * 3, wide_shapes)
    tick(chain, z, flow1, flow4, gains)
    finish(chain, z, flow1)
    gathered1 = gather(flow1)
    tick(chain, z, flow3, flow4, gains)
    grad_tokens = last(chain, back_own, swap(back_send), own, grad_hidden, gain_attn)
    tick(chain, z, flow3, flow4, gains)
    finish(chain, z, flow3)
    flow3.spread()
    tick(chain, z, flow4, gains)
    finish(chain, z, flow4, gains)
    flow4.spread()
    count = 2 * 128
    moves = lambda h: [(k, k * count, count, count, across(quarter, h * count, count)) for k in range(3)]
    *narrow, grad_out = unpack(
        chain,
        y_first,
        flow3.pieces,
        moves(0) + [(3, 3 * count, width, quarter, along(quarter, 0, width))],
        [None] * 4,
        [(d, width)] * 3 + [(width, d)],
    )
    wide = unpack(chain, plain, [gathered1], ffn_moves(w0, w1), wide, wide_shapes)
    narrow = unpack(chain, y_first, flow4.pieces, moves(1), narrow, [(d, width)] * 3)
    return (
        result[:, None],
        grad_tokens[:, None],
        *narrow,
        grad_out,
        *wide,
        gains.mine[0],
        gains.mine[1],
    )


def solution(mesh):
    return jax.shard_map(
        shards,
        mesh=mesh,
        in_specs=(
            P("mp", "dp", None),
            P("dp", None),
            P("dp", None),
            P(None, "mp"),
            P(None, "mp"),
            P(None, "mp"),
            P("mp", None),
            P(None, "mp"),
            P(None, "mp"),
            P("mp", None),
            P(),
            P(),
            P("mp", "dp", None),
        ),
        out_specs=(
            P("mp", "dp", None),
            P("mp", "dp", None),
            P(None, "mp"),
            P(None, "mp"),
            P(None, "mp"),
            P("mp", None),
            P(None, "mp"),
            P(None, "mp"),
            P("mp", None),
            P(),
            P(),
        ),
        check_vma=False,
    )
```

```python
import functools

import jax
import jax.numpy as jnp
from jax import lax
from jax.experimental import pallas as pl
from jax.experimental.pallas import tpu as pltpu
from jax.sharding import PartitionSpec as P

HDIM = 64
EPSILON = 1e-06
LOG2E = 1.4426950408889634
VMEM_LIMIT = 62 * 1024 * 1024
COST = 1e6
BF = jnp.bfloat16
F32 = jnp.float32
NN = ((1,), (0,))
NT = ((1,), (1,))
TN = ((0,), (0,))
FFN_CHUNKS = (512, 896)


def dot(left, right, dims=NN):
    return lax.dot_general(left, right, (dims, ((), ())), preferred_element_type=F32)


def shape(dims, dtype):
    return jax.ShapeDtypeStruct(dims, dtype)


class Chain:
    def __init__(self):
        self.token = None

    def run(self, kernel, grid, in_specs, out_specs, out_shape, args, prefetch=(), scratch=(), alias=None, us=5):
        before = [] if self.token is None else [self.token]
        some, n_in, n_out = len(prefetch), len(args), len(out_shape)
        skip = len(before)

        def body(*refs):
            kept = refs[: some + n_in] + refs[some + n_in + skip : some + n_in + skip + n_out]
            kernel(*kept, *refs[some + n_in + skip + n_out + 1 :])

        anywhere = pl.BlockSpec(memory_space=pl.ANY)
        *outs, self.token = pl.pallas_call(
            body,
            grid_spec=pltpu.PrefetchScalarGridSpec(
                num_scalar_prefetch=some,
                grid=grid,
                in_specs=list(in_specs) + [anywhere] * skip,
                out_specs=list(out_specs) + [anywhere],
                scratch_shapes=list(scratch),
            ),
            out_shape=list(out_shape) + [shape((8, 128), F32)],
            input_output_aliases=alias or {},
            compiler_params=pltpu.CompilerParams(vmem_limit_bytes=VMEM_LIMIT),
            cost_estimate=pl.CostEstimate(flops=int(us * COST), bytes_accessed=1, transcendentals=0),
        )(*prefetch, *args, *before)
        return outs


ANYWHERE = pl.BlockSpec(memory_space=pl.ANY)


def block(dims, index):
    return pl.BlockSpec(dims, index)


class Copies:
    def __init__(self, sems):
        self.sems, self.started = sems, []

    def start(self, source, target):
        copy = pltpu.make_async_copy(source, target, self.sems.at[len(self.started)])
        copy.start()
        self.started.append(copy)
        return copy


def by_hand(chain, kernel, inputs, outputs, scratch, copies, prefetch=(), alias=None, us=5):
    def body(*refs):
        kernel(*refs[:-1], Copies(refs[-1]))

    return chain.run(
        body,
        (1,),
        [ANYWHERE] * len(inputs),
        [ANYWHERE] * len(outputs),
        outputs,
        inputs,
        prefetch=prefetch,
        scratch=list(scratch) + [pltpu.SemaphoreType.DMA((copies,))],
        alias=alias,
        us=us,
    )


def project(chain, tokens, gain, wq, wk, wv, half, before=()):
    rows, d = tokens.shape
    width = wq.shape[1]
    weights = [wq, wk, wv]

    def kernel(tokens, gain, *refs):
        ws, refs = refs[:3], refs[3 + len(before) :]
        projected, normed, xs, gs, held, out, low, copies = refs
        first = [copies.start(gain, gs), copies.start(tokens, xs)]
        loads = [copies.start(w, held.at[i]) for i, w in enumerate(ws)]
        for c in first:
            c.wait()
        x = xs[...].astype(F32)
        r = lax.rsqrt(jnp.mean(x * x, axis=-1, keepdims=True) + EPSILON)
        low[...] = (x * r * gs[...]).astype(BF)
        here = pl.ds(half * rows, rows)
        stores = [copies.start(low, normed.at[here])]
        for i in range(3):
            loads[i].wait()
            out[i] = dot(low[...], held[i]).astype(BF)
            stores.append(copies.start(out.at[i], projected.at[here, pl.ds(i * width, width)]))
        for c in stores:
            c.wait()

    return by_hand(
        chain,
        kernel,
        [tokens, gain, *weights, *before],
        [shape((2 * rows, 3 * width), BF), shape((2 * rows, d), BF)],
        [
            pltpu.VMEM((rows, d), BF),
            pltpu.VMEM((1, d), F32),
            pltpu.VMEM((3, d, width), BF),
            pltpu.VMEM((3, rows, width), BF),
            pltpu.VMEM((rows, d), BF),
        ],
        9,
        alias={5: 0, 6: 1} if before else None,
    )


def layout(place, segs, keep, slot):
    last, mid = 4 * slot - 1, 2 * slot
    leads = jnp.logical_or(segs[0, 0] != segs[0, mid], keep[0, 0] == 0)
    start = jnp.where(leads, 1, 0) + 2 * place[0]
    padded = jnp.where(jnp.where(leads, keep[0, 0], keep[0, last]) == 0, 1, 0)
    return (lambda logical: pl.ds(pl.multiple_of(lax.rem(logical + start, 4) * slot, slot), slot)), padded


def two_heads(columns):
    slot = columns.shape[1]
    zero = jnp.zeros((HDIM, slot), BF)
    first = jnp.concatenate([columns[:HDIM], zero], 0)
    second = jnp.concatenate([zero, columns[HDIM:]], 0)
    return jnp.concatenate([first, second], 1)


def attend(chain, scalars, qkv, w_out, early):
    seq, width = qkv.shape[0], qkv.shape[1] // 3
    d = w_out.shape[1]
    pairs, slot, half = width // 128, seq // 4, seq // 2
    scale = HDIM**-0.5 * LOG2E

    def kernel(place, segs, keep, q_ref, k_ref, v_ref, w_all, early, o_ref, lse_ref, part, mixed, ws, out, sems):
        step = pl.program_id(0)
        rows, padded = layout(place, segs, keep, slot)
        load = pltpu.make_async_copy(w_all, ws, sems.at[0])

        @pl.when(step == 0)
        def _():
            load.start()

        one = jnp.ones((16, slot), BF)
        slots = [[j if at < 3 else jnp.where(padded > 0, j, 3) for j in range(3)] for at in range(4)]

        def scores_of(at):
            q2 = two_heads(q_ref[rows(at), :].T)
            return [dot(k_ref[rows(j), :], q2) for j in slots[at]]

        coming = scores_of(0)
        for at in range(4):
            scores = coming
            if at < 3:
                coming = scores_of(at + 1)
            top = functools.reduce(jnp.maximum, [jnp.max(s, axis=0, keepdims=True) for s in scores])
            oa = jnp.zeros((HDIM + 16, slot), F32)
            ob = oa
            for j, s in zip(slots[at], scores):
                p = jnp.exp2((s - top) * scale).astype(BF)
                vt = v_ref[rows(j), :].T
                oa += dot(jnp.concatenate([vt[:HDIM], one], 0), p[:, :slot])
                ob += dot(jnp.concatenate([vt[HDIM:], one], 0), p[:, slot:])
            la, lb = oa[HDIM : HDIM + 1], ob[HDIM : HDIM + 1]
            o = jnp.concatenate([oa[:HDIM] / la, ob[:HDIM] / lb], 0).astype(BF).T
            o_ref[rows(at), :] = o
            mixed[step, rows(at), :] = o
            lse = top * HDIM**-0.5 + jnp.log(jnp.concatenate([la, lb], 1))
            lse_ref[0, 0:1, rows(at)] = lse[:, :slot]
            lse_ref[0, 1:2, rows(at)] = lse[:, slot:]

        @pl.when(step == pairs - 1)
        def _():
            load.wait()
            stores = []
            for k in range(2):
                here = slice(k * half, (k + 1) * half)
                every = jnp.concatenate([mixed[p, here, :] for p in range(pairs)], 1)
                out[here] = dot(every, ws[...]).astype(BF)
                stores.append(pltpu.make_async_copy(out.at[here], part.at[here], sems.at[1 + k]))
                stores[-1].start()
            for c in stores:
                c.wait()

    column = lambda off: block((seq, 128), lambda p, *m: (0, p + off))
    return chain.run(
        kernel,
        (pairs,),
        [column(0), column(pairs), column(2 * pairs), ANYWHERE, ANYWHERE],
        [column(0), block((1, 2, seq), lambda p, *m: (p, 0, 0)), ANYWHERE],
        [shape((seq, width), BF), shape((pairs, 2, seq), F32), shape((seq, d), BF)],
        [qkv, qkv, qkv, w_out, early],
        prefetch=scalars,
        scratch=[
            pltpu.VMEM((pairs, seq, 128), BF),
            pltpu.VMEM((width, d), BF),
            pltpu.VMEM((seq, d), BF),
            pltpu.SemaphoreType.DMA((3,)),
        ],
        us=26,
    )


def attend_back(chain, scalars, order, qkv, mixed, grad_mixed, lse, normed, first, before=None, g=None):
    seq, width = qkv.shape[0], qkv.shape[1] // 3
    d = normed.shape[1]
    pairs, slot, quarter = width // 128, seq // 4, d // 4
    scale = HDIM**-0.5 * LOG2E

    def kernel(
        place, segs, keep, order, q_ref, k_ref, v_ref, o_ref, do_ref, lse_ref, *refs
    ):
        rows, padded = layout(place, segs, keep, slot)
        if before is None:
            dq_ref, dk_ref, dv_ref, dk_sum, dv_sum = refs
        else:
            normed_all, g_all, mixed_all, *old = refs[:6]
            dq_ref, dk_ref, dv_ref, kept, sent, dk_sum, dv_sum, every, ns, held, gs, ms, sems = refs[6:]
            copies = Copies(sems)
            loads = [copies.start(normed_all, ns), copies.start(g_all, gs), copies.start(mixed_all, ms)]
            loads += [copies.start(o, every.at[i]) for i, o in enumerate(old)]

        def stacked(x):
            lane = lax.broadcasted_iota(jnp.int32, (slot, 128), 1)
            zero = jnp.zeros_like(x)
            return jnp.concatenate([jnp.where(lane < HDIM, x, zero), jnp.where(lane < HDIM, zero, x)], 0)

        def extended(columns, tail):
            high = tail.astype(BF).astype(F32)
            rest = tail - high
            middle = rest.astype(BF).astype(F32)
            extra = jnp.concatenate([high, middle, rest - middle, jnp.zeros((125, 2 * slot), F32)], 0).astype(BF)
            return jnp.concatenate([two_heads(columns), extra], 0)

        def one_slot(at, slots):
            ones = jnp.ones((slot, 128), BF)
            q, do = q_ref[rows(at), :], do_ref[rows(at), :]
            do_t = do.T
            prod = do_t.astype(F32) * o_ref[rows(at), :].T.astype(F32)
            delta = jnp.concatenate(
                [jnp.sum(prod[:HDIM], 0, keepdims=True), jnp.sum(prod[HDIM:], 0, keepdims=True)], 1
            )
            lse = jnp.concatenate([lse_ref[0, 0:1, rows(at)], lse_ref[0, 1:2, rows(at)]], 1)
            q2 = extended(q.T, lse * -(HDIM**0.5))
            do2 = extended(do_t, -delta)
            qs, dos = stacked(q), stacked(do)
            dqa = jnp.zeros((HDIM, slot), F32)
            dqb = dqa
            for j in slots:
                k, v = k_ref[rows(j), :], v_ref[rows(j), :]
                p = jnp.exp2(dot(jnp.concatenate([k, ones], 1), q2) * scale)
                dp = dot(jnp.concatenate([v, ones], 1), do2)
                ds = (p * dp).astype(BF)
                dv_sum[rows(j), :] += dot(p.astype(BF), dos)
                dk_sum[rows(j), :] += dot(ds, qs)
                kt = k.T
                dqa += dot(kt[:HDIM], ds[:, :slot])
                dqb += dot(kt[HDIM:], ds[:, slot:])
            dq_ref[rows(at), :] = (jnp.concatenate([dqa, dqb], 0) * HDIM**-0.5).astype(BF).T

        dk_sum[...] = jnp.zeros_like(dk_sum)
        dv_sum[...] = jnp.zeros_like(dv_sum)

        def body(at, carry):
            alone = jnp.logical_and(at == 3, padded == 0)
            one_slot(at, [jnp.where(alone, 3, j) for j in range(3)])
            return carry

        lax.fori_loop(0, 4, body, 0)
        dk = (dk_sum[...] * HDIM**-0.5).astype(BF)
        dv = dv_sum[...].astype(BF)
        dk_ref[...] = dk
        dv_ref[...] = dv
        if before is not None:
            for c in loads:
                c.wait()
            right = jnp.concatenate([every[0], dq_ref[...], every[1], dk, every[2], dv], 1)
            stores = []
            for k in range(4):
                held[k, :, :wide] = dot(column_block(ns, order[k], quarter), right, TN).astype(BF)
                part = dot(ms[...], column_block(gs, order[k], quarter), TN).astype(BF)
                for i in range(width // quarter):
                    held[k, :, wide + i * quarter : wide + (i + 1) * quarter] = part[i * quarter : (i + 1) * quarter]
                stores.append(copies.start(held.at[k], quarters_of([kept, sent])[k]))
            for c in stores:
                c.wait()

    column = lambda off: block((seq, 128), lambda p, *m: (0, off))
    wide = 3 * 2 * 128
    more = before is not None
    return chain.run(
        kernel,
        (1,),
        [
            column(first),
            column(first + pairs),
            column(first + 2 * pairs),
            column(first),
            column(first),
            block((1, 2, seq), lambda p, *m: (first, 0, 0)),
        ]
        + [ANYWHERE] * (6 * more),
        [column(0)] * 3 + [ANYWHERE] * (2 * more),
        [shape((seq, 128), BF)] * 3 + quarter_shapes(2 * more, quarter, wide + width),
        [qkv, qkv, qkv, mixed, grad_mixed, lse] + ([normed, g, mixed, *before] if more else []),
        prefetch=scalars + [order],
        scratch=[pltpu.VMEM((seq, 128), F32)] * 2
        + [
            pltpu.VMEM((3, seq, 128), BF),
            pltpu.VMEM((seq, d), BF),
            pltpu.VMEM((4, quarter, wide + width), BF),
            pltpu.VMEM((seq, d), BF),
            pltpu.VMEM((seq, width), BF),
            pltpu.SemaphoreType.DMA((10,)),
        ]
        * more,
        us=13,
    )


def gelu_parts(v):
    c = 0.7978845608028654
    square = v * v
    share = 0.5 + 0.5 * jnp.tanh(v * (c + (c * 0.044715) * square))
    value = v * share
    return value, share + value * (1.0 - share) * (2 * c + (6 * c * 0.044715) * square)


def column_block(ref, number, width):
    return ref[:, pl.ds(pl.multiple_of(number * width, width), width)]


def quarters_of(outs):
    each = 4 // len(outs)
    return [outs[k // each].at[k % each] for k in range(4)]


def quarter_shapes(pieces, rows, width):
    return [shape((4 // pieces, rows, width), BF)] * pieces if pieces else []


def weight_quarters(copies, order, xs, cs, acts, boths, held, targets, quarter, beside=None):
    width = acts.shape[1]
    stores = []
    for k in range(4):
        sides = dot(column_block(xs, order[k], quarter), boths[...], TN)
        down = dot(acts[...], column_block(cs, order[k], quarter), TN).astype(BF)
        held[k, :, : 2 * width] = sides.astype(BF)
        for i in range(width // 128):
            rows = down[i * 128 : (i + 1) * 128]
            place = slice(2 * width + i * 128, 2 * width + (i + 1) * 128)
            held[k, :128, place] = rows[:, :128]
            held[k, 128:, place] = rows[:, 128:]
        if beside is not None:
            beside(k)
        stores.append(copies.start(held.at[k], targets[k]))
    return stores


def ffn(chain, order, begin, ct_own, ct_other, w_gate, w_up, w_down, at, width, finish):
    seq, d = begin[-1].shape
    half, quarter = seq // 2, d // 4
    early = len(begin) > 1

    def kernel(order, *refs):
        before, (ct_own, ct_other, wg_all, wu_all, wd_all, act, both, *refs) = refs[: len(begin)], refs[len(begin) :]
        grads, refs = refs[:finish], refs[finish:]
        if early:
            (hidden, x), refs = refs[:2], refs[2:]
            *refs, ts, ms, others, gs, hs, copies = refs
        else:
            *refs, copies = refs
        xs, cs, wg, wu, wd, acts, boths, *held = refs
        halves = [slice(0, half), slice(half, seq)]
        stores = []
        if early:
            gain_in, own, other, theirs, mine = before
            tokens = [own, other]
            gain_load = copies.start(gain_in, gs)

            def load(k):
                return [
                    copies.start(tokens[k], ts.at[k]),
                    copies.start(mine.at[halves[k]], ms.at[halves[k]]),
                    copies.start(theirs.at[halves[1 - k]], others.at[halves[1 - k]]),
                ]

            def normed(k, loads):
                for c in loads + [gain_load] * (k == 0):
                    c.wait()
                here = halves[k]
                h = ts[k].astype(F32) + (ms[here].astype(F32) + others[halves[1 - k]].astype(F32))
                r = lax.rsqrt(jnp.mean(h * h, axis=-1, keepdims=True) + EPSILON)
                hs[here] = h
                xs[here] = (h * r * gs[...]).astype(BF)
                stores.append(copies.start(hs.at[here], hidden.at[here]))
                stores.append(copies.start(xs.at[here], x.at[here]))

        else:

            def load(k):
                return [copies.start(before[0].at[halves[k]], xs.at[halves[k]])]

            def normed(k, loads):
                for c in loads:
                    c.wait()

        x0 = load(0)
        units = pl.ds(at, width)
        lg = copies.start(wg_all.at[:, units], wg)
        lu = copies.start(wu_all.at[:, units], wu)
        c0 = copies.start(ct_own, cs.at[halves[0]])
        ld = copies.start(wd_all.at[units, :], wd)
        x1 = load(1)
        c1 = copies.start(ct_other, cs.at[halves[1]])
        waits = [[lg], [lu], [c0, ld]], [[], [], [c1]]
        normed(0, x0)
        for here, (for_gate, for_up, for_act) in zip(halves, waits):
            for c in for_gate:
                c.wait()
            gate = dot(xs[here], wg[...])
            for c in for_up:
                c.wait()
            up = dot(xs[here], wu[...])
            for c in for_act:
                c.wait()
            if here.start == 0:
                normed(1, x1)
            grad_act = dot(cs[here], wd[...], NT)
            value, slope = gelu_parts(gate)
            acts[here] = (value * up).astype(BF)
            boths[here, :width] = (grad_act * up * slope).astype(BF)
            boths[here, width:] = (grad_act * value).astype(BF)
            stores.append(copies.start(acts.at[here], act.at[here]))
            stores.append(copies.start(boths.at[here], both.at[here]))
        if finish:
            targets = quarters_of(grads)
            stores += weight_quarters(copies, order, xs, cs, acts, boths, held[0], targets, quarter)
        for c in stores:
            c.wait()

    return by_hand(
        chain,
        kernel,
        [*begin, ct_own, ct_other, w_gate, w_up, w_down],
        [shape((seq, width), BF), shape((seq, 2 * width), BF)]
        + quarter_shapes(finish, quarter, 3 * width)
        + [shape((seq, d), F32), shape((seq, d), BF)] * early,
        [
            pltpu.VMEM((seq, d), BF),
            pltpu.VMEM((seq, d), BF),
            pltpu.VMEM((d, width), BF),
            pltpu.VMEM((d, width), BF),
            pltpu.VMEM((width, d), BF),
            pltpu.VMEM((seq, width), BF),
            pltpu.VMEM((seq, 2 * width), BF),
        ]
        + [pltpu.VMEM((4, quarter, 3 * width), BF)] * min(finish, 1)
        + [
            pltpu.VMEM((2, half, d), BF),
            pltpu.VMEM((seq, d), BF),
            pltpu.VMEM((seq, d), BF),
            pltpu.VMEM((1, d), F32),
            pltpu.VMEM((seq, d), F32),
        ]
        * early,
        15 + 9 * early,
        prefetch=[order],
        us=16 if finish else 8,
    )


def ffn_input_grad(chain, boths, wg, wu):
    seq = boths[0].shape[0]
    d, units = wg.shape
    half, chunks = seq // 2, len(boths)
    starts = [sum(b.shape[1] for b in boths[:k]) // 2 for k in range(chunks + 1)]

    def kernel(*refs):
        ins, (wg, wu, back, *held, wgs, wus, out, copies) = refs[:chunks], refs[chunks:]
        loads = []
        for k in range(chunks):
            units = pl.ds(starts[k], starts[k + 1] - starts[k])
            loads.append(
                [
                    copies.start(ins[k].at[pl.ds(0, half)], held[k].at[pl.ds(0, half)]),
                    copies.start(wg.at[:, units], wgs.at[:, units]),
                    copies.start(wu.at[:, units], wus.at[:, units]),
                ]
            )
        later = [copies.start(ins[k].at[pl.ds(half, half)], held[k].at[pl.ds(half, half)]) for k in range(chunks)]
        stores = []
        for h in range(2):
            here = slice(h * half, (h + 1) * half)
            total = None
            for k in range(chunks):
                for c in loads[k] if h == 0 else [later[k]]:
                    c.wait()
                width = starts[k + 1] - starts[k]
                units = slice(starts[k], starts[k + 1])
                part = dot(held[k][here, :width], wgs[:, units], NT) + dot(held[k][here, width:], wus[:, units], NT)
                total = part if total is None else total + part
            out[here] = total.astype(BF)
            stores.append(copies.start(out.at[here], back.at[here]))
        for c in stores:
            c.wait()

    return by_hand(
        chain,
        kernel,
        boths + [wg, wu],
        [shape((seq, d), BF)],
        [pltpu.VMEM(b.shape, BF) for b in boths]
        + [pltpu.VMEM((d, units), BF), pltpu.VMEM((d, units), BF), pltpu.VMEM((seq, d), BF)],
        4 * chunks + 2,
        us=13,
    )[0]


def ffn_output(chain, acts, wd):
    seq, d = acts[0].shape[0], wd.shape[1]
    half, chunks = seq // 2, len(acts)
    starts = [sum(a.shape[1] for a in acts[:k]) for k in range(chunks + 1)]

    def kernel(*refs):
        ins, (wd, own, send, *held, wds, out_own, out_send, copies) = refs[:chunks], refs[chunks:]
        first, second = pl.ds(half, half), pl.ds(0, half)
        loads = []
        for k in range(chunks):
            units = pl.ds(starts[k], starts[k + 1] - starts[k])
            loads.append([copies.start(ins[k].at[first], held[k].at[first]), copies.start(wd.at[units], wds.at[units])])
        later = [copies.start(ins[k].at[second], held[k].at[second]) for k in range(chunks)]
        stores = []
        for h, (here, target, out) in enumerate([(first, out_send, send), (second, out_own, own)]):
            total = None
            for k in range(chunks):
                for c in loads[k] if h == 0 else [later[k]]:
                    c.wait()
                part = dot(held[k][here], wds[starts[k] : starts[k + 1]])
                total = part if total is None else total + part
            target[...] = total.astype(target.dtype)
            stores.append(copies.start(target, out))
        for c in stores:
            c.wait()

    return by_hand(
        chain,
        kernel,
        acts + [wd],
        [shape((half, d), F32), shape((half, d), BF)],
        [pltpu.VMEM(a.shape, BF) for a in acts]
        + [pltpu.VMEM(wd.shape, BF), pltpu.VMEM((half, d), F32), pltpu.VMEM((half, d), BF)],
        3 * chunks + 2,
        us=7,
    )


def norm_back(value, gain, grad):
    r = lax.rsqrt(jnp.mean(value * value, axis=-1, keepdims=True) + EPSILON)
    u = grad * gain
    inner = jnp.mean(u * value, axis=-1, keepdims=True)
    return r * u - value * (r * r * r * inner), jnp.sum(grad * value * r, axis=0, keepdims=True)


def add_up(at, total, part):
    @pl.when(at == 0)
    def _():
        total[...] = part

    @pl.when(at > 0)
    def _():
        total[...] += part


def middle_back(chain, mine, theirs, hidden, ct_own, ct_other, gain, tile=384):
    seq, d = hidden.shape
    n = seq // tile
    rows = lambda f: block((tile, d), lambda i: (f(i), 0))
    front = rows(lambda i: jnp.minimum(i, n // 2 - 1))

    def kernel(mine, theirs, hidden, ct_own, ct_other, gain, low, keep, gain_grad):
        at = pl.program_id(0)
        h = hidden[...]
        through, part = norm_back(h, gain[...], mine[...].astype(F32) + theirs[...].astype(F32))
        ct = jnp.where(at < n // 2, ct_own[...], ct_other[...])
        total = ct.astype(F32) + through
        low[...] = total.astype(BF)
        add_up(at, gain_grad, part)

        @pl.when(at < n // 2)
        def _():
            keep[...] = total

    return chain.run(
        kernel,
        (n,),
        [
            rows(lambda i: i),
            rows(lambda i: lax.rem(i + n // 2, n)),
            rows(lambda i: i),
            front,
            rows(lambda i: jnp.maximum(i - n // 2, 0)),
            block((1, d), lambda i: (0, 0)),
        ],
        [rows(lambda i: i), front, block((1, d), lambda i: (0, 0))],
        [shape((seq, d), BF), shape((seq // 2, d), F32), shape((1, d), F32)],
        [mine, theirs, hidden, ct_own, ct_other, gain],
        us=8,
    )


def add_output(chain, hidden, own, theirs, tile=384):
    rows, d = own.shape
    row = block((tile, d), lambda i: (i, 0))

    def kernel(hidden, own, theirs, result):
        result[...] = (hidden[...] + (own[...] + theirs[...].astype(F32))).astype(BF)

    return chain.run(kernel, (rows // tile,), [row] * 3, [row], [shape((rows, d), BF)], [hidden, own, theirs], us=4)[0]


def out_back(chain, g, w_out):
    seq, d = g.shape
    width, half = w_out.shape[0], seq // 2

    def kernel(g, w_out, grad_mixed, gs, ws, out, copies):
        halves = [pl.ds(0, half), pl.ds(half, half)]
        loads = [[copies.start(g.at[halves[0]], gs.at[halves[0]]), copies.start(w_out, ws)]]
        loads.append([copies.start(g.at[halves[1]], gs.at[halves[1]])])
        stores = []
        for here, waits in zip(halves, loads):
            for c in waits:
                c.wait()
            out[here] = dot(gs[here], ws[...], NT).astype(BF)
            stores.append(copies.start(out.at[here], grad_mixed.at[here]))
        for c in stores:
            c.wait()

    return by_hand(
        chain,
        kernel,
        [g, w_out],
        [shape((seq, width), BF)],
        [pltpu.VMEM((seq, d), BF), pltpu.VMEM((width, d), BF), pltpu.VMEM((seq, width), BF)],
        5,
        us=8,
    )[0]


def qkv_back(chain, order, grads, weights, normed, own, other, gain_ffn_grad):
    flat = [g for kind in grads for g in kind]
    count = len(flat)
    pieces = len(grads[0])
    seq = flat[0].shape[0]
    d, width = weights[0].shape
    half, quarter = seq // 2, d // 4
    wide = 3 * sum(g.shape[1] for g in grads[0][-2:])

    def kernel(order, *refs):
        ins, ws, refs = refs[:count], refs[count : count + 3], refs[count + 3 :]
        normed, t_own, t_other, ffn_part, own, send, gains, kept, sent, *held = refs
        *held, wh, ts, ffn, sums, out_own, out_send, ns, out, copies = held
        first, second = pl.ds(half, half), pl.ds(0, half)
        loads = [[copies.start(ins[i].at[first], held[i].at[first])] for i in range(count)]
        for i in range(3):
            loads[i * pieces].append(copies.start(ws[i], wh.at[i]))
        later = [[copies.start(ins[i].at[second], held[i].at[second])] for i in range(count)]
        all_normed = copies.start(normed, ns)
        tokens = [copies.start(t_other, ts.at[1]), copies.start(t_own, ts.at[0]), copies.start(ffn_part, ffn)]
        stores = []
        gain = 0.0
        for k, (here, waits, target, goal) in enumerate([(first, loads, out_send, send), (second, later, out_own, own)]):
            total = 0.0
            for kind in range(3):
                some = range(kind * pieces, (kind + 1) * pieces)
                for i in some:
                    for c in waits[i]:
                        c.wait()
                left = jnp.concatenate([held[i][here] for i in some], 1)
                total += dot(left, wh[kind], NT)
            target[...] = total.astype(target.dtype)
            stores.append(copies.start(target, goal))
            tokens[k].wait()
            x = ts[1 - k].astype(F32)
            r = lax.rsqrt(jnp.mean(x * x, axis=-1, keepdims=True) + EPSILON)
            gain += jnp.sum(total * (x * r), axis=0, keepdims=True)
        all_normed.wait()
        right = jnp.concatenate([held[kind * pieces + p][...] for kind in range(3) for p in (pieces - 2, pieces - 1)], 1)
        for k in range(4):
            out[k] = dot(column_block(ns, order[k], quarter), right, TN).astype(BF)
            stores.append(copies.start(out.at[k], quarters_of([kept, sent])[k]))
        tokens[2].wait()
        sums[0:1] = gain
        sums[1:2] = 0.5 * ffn[...]
        stores.append(copies.start(sums, gains))
        for c in stores:
            c.wait()

    return by_hand(
        chain,
        kernel,
        flat + list(weights) + [normed, own, other, gain_ffn_grad],
        [shape((half, d), F32), shape((half, d), BF), shape((2, d), F32)] + quarter_shapes(2, quarter, wide),
        [pltpu.VMEM(g.shape, BF) for g in flat]
        + [
            pltpu.VMEM((3, d, width), BF),
            pltpu.VMEM((2, half, d), BF),
            pltpu.VMEM((1, d), F32),
            pltpu.VMEM((2, d), F32),
            pltpu.VMEM((half, d), F32),
            pltpu.VMEM((half, d), BF),
            pltpu.VMEM((seq, d), BF),
            pltpu.VMEM((4, quarter, wide), BF),
        ],
        2 * count + 14,
        prefetch=[order],
        us=8,
    )


def last(chain, mine, theirs, tokens, grad_hidden, gain, tile=384):
    rows, d = tokens.shape
    row = block((tile, d), lambda i: (i, 0))

    def kernel(mine, theirs, tokens, grad_hidden, gain, out):
        grad = mine[...] + theirs[...].astype(F32)
        out[...] = (grad_hidden[...] + norm_back(tokens[...].astype(F32), gain[...], grad)[0]).astype(BF)

    return chain.run(
        kernel,
        (rows // tile,),
        [row] * 4 + [block((1, d), lambda i: (0, 0))],
        [row],
        [shape((rows, d), BF)],
        [mine, theirs, tokens, grad_hidden, gain],
        us=4,
    )[0]


def swap(x):
    return lax.ppermute(x, "mp", [(0, 1), (1, 0)])


def exchange(x, bit):
    return lax.ppermute(x, "dp", [(i, i ^ bit) for i in range(lax.axis_size("dp"))])


def add(terms, pieces=1):
    n, rows, width = terms[0].shape
    tile = rows // 2

    def body(at, z, ins, outs):
        for k, out in enumerate(outs):
            out[0] = sum(t[k].astype(F32) for t in ins).astype(BF)

    spec = block((n, tile, width), lambda i, z: (0, i, 0))
    out = block((1, tile, width), lambda i, z: (0, i, 0))
    return list(terms), [spec] * len(terms), [out] * n, [shape((1, rows, width), BF)] * n, body


def halve(terms, bit):
    _, rows, width = terms[0].shape
    tile = rows // 4

    def body(at, z, ins, outs):
        for k in range(2):
            outs[k][0] = sum(t[0].astype(F32) for t in ins[k::2]).astype(BF)

    mine = block((1, tile, width), lambda i, z: (0, 2 * z[bit] + i, 0))
    others = block((1, tile, width), lambda i, z: (0, 2 * (1 - z[bit]) + i, 0))
    out = block((1, tile, width), lambda i, z: (0, i, 0))
    return (
        [t for t in terms for _ in range(2)],
        [mine, others] * len(terms),
        [out] * 2,
        [shape((1, rows // 2, width), BF)] * 2,
        body,
    )


def join(mine, theirs, bit):
    _, rows, width = mine.shape

    def body(at, z, ins, outs):
        outs[0][0] = jnp.where(at == z[bit], ins[0][0], ins[1][0])

    spec = block((1, rows, width), lambda i, z: (0, 0, 0))
    out = block((1, rows, width), lambda i, z: (0, i, 0))
    return [mine, theirs], [spec] * 2, [out], [shape((1, 2 * rows, width), BF)], body


class Flow:
    def __init__(self, quarters, bits=(1, 2), split=False):
        rest = [1 << b for b in range(2, (lax.axis_size("dp") - 1).bit_length())]
        self.steps = self.walk(quarters, bits, rest, split)
        self.step = next(self.steps)

    def walk(self, quarters, bits, rest, split):
        if len(quarters) == 2:
            keep, send = quarters
            mine, send = yield add([keep, exchange(send, bits[0])])
            terms = [mine, exchange(send, bits[1])]
        else:
            terms = list(quarters)
        if split:
            for k in range(2):
                mine, send = yield halve(terms, k)
                terms = [mine, exchange(send, rest[k])]
            [mine] = yield add(terms)
            for bit in rest[2:]:
                [mine] = yield add([mine, exchange(mine, bit)])
            for k in (1, 0):
                [mine] = yield join(mine, exchange(mine, rest[k]), k)
        else:
            [mine] = yield add(terms)
            for bit in rest:
                [mine] = yield add([mine, exchange(mine, bit)])
        self.mine = mine
        yield None

    def spread(self):
        self.pieces = [self.mine] + [exchange(self.mine, 1 + k) for k in range(3)]


class Total:
    def __init__(self, part):
        self.steps = self.walk(part)
        self.step = next(self.steps)

    def walk(self, mine):
        def body(at, z, ins, outs):
            outs[0][...] = ins[0][...] + ins[1][...]

        spec = block(mine.shape, lambda i, z: (0, 0))
        theirs = swap(mine)
        for bit in [1 << b for b in range((lax.axis_size("dp") - 1).bit_length())] + [None]:
            [mine] = yield [mine, theirs], [spec] * 2, [spec], [shape(mine.shape, F32)], body
            if bit is not None:
                theirs = exchange(mine, bit)
        self.mine = mine
        yield None


def tick(chain, z, *flows):
    args, in_specs, out_specs, shapes = [], [], [], []
    for f in flows:
        args += f.step[0]
        in_specs += f.step[1]
        out_specs += f.step[2]
        shapes += f.step[3]

    def kernel(z, *refs):
        ins, outs = list(refs[: len(args)]), list(refs[len(args) :])
        for some, _, specs, _, body in steps:
            body(pl.program_id(0), z, ins[: len(some)], outs[: len(specs)])
            del ins[: len(some)], outs[: len(specs)]

    steps = [f.step for f in flows]
    outs = chain.run(kernel, (2,), in_specs, out_specs, shapes, args, prefetch=[z], us=2)
    for f in flows:
        count = len(f.step[2])
        f.step = f.steps.send(outs[:count])
        outs = outs[count:]


def finish(chain, z, *flows):
    while left := [f for f in flows if f.step is not None]:
        tick(chain, z, *left)


def unpack(chain, order, pieces, moves, outputs, shapes):
    kept = [o for o in outputs if o is not None]
    whole = len(pieces) == 1
    rows, width = pieces[0].shape[-2:]

    def kernel(order, *refs):
        pieces_in = refs[: len(pieces)]
        outs = refs[len(pieces) + len(kept) : len(pieces) + len(kept) + len(shapes)]
        *scratch, sems = refs[len(pieces) + len(kept) + len(shapes) :]
        copies = []
        for k in range(4):
            piece = pieces_in[0].at[k] if whole else pieces_in[k].at[0]
            for m, (goal, at, count, tile, place) in enumerate(moves):
                held = scratch[m]
                for i in range(count // tile):
                    columns = piece[:, at + i * tile : at + (i + 1) * tile].astype(F32)
                    if tile == count:
                        held[k] = columns
                    else:
                        for j in range(rows // tile):
                            held[k, i * tile : (i + 1) * tile, j * tile : (j + 1) * tile] = columns[
                                j * tile : (j + 1) * tile
                            ]
                copy = pltpu.make_async_copy(held.at[k], outs[goal].at[place(order[k])], sems.at[k, m])
                copy.start()
                copies.append(copy)
        for copy in copies:
            copy.wait()

    return chain.run(
        kernel,
        (1,),
        [block(p.shape, lambda i, q, n=p.ndim: (0,) * n) for p in pieces] + [ANYWHERE] * len(kept),
        [ANYWHERE] * len(shapes),
        [shape(s, F32) for s in shapes],
        list(pieces) + kept,
        prefetch=[order],
        scratch=[
            pltpu.VMEM((4, rows, count) if tile == count else (4, count, rows), F32) for _, _, count, tile, _ in moves
        ]
        + [pltpu.SemaphoreType.DMA((4, len(moves)))],
        alias={1 + len(pieces) + i: i for i in range(len(kept))},
        us=3,
    )


def across(rows, at, count):
    return lambda q: (pl.ds(pl.multiple_of(q * rows, rows), rows), pl.ds(at, count))


def along(rows, at, count):
    return lambda q: (pl.ds(at, count), pl.ds(pl.multiple_of(q * rows, rows), rows))


def shards(
    tokens,
    segment_ids,
    keep_mask,
    w_query,
    w_key,
    w_value,
    w_out,
    w_gate,
    w_up,
    w_down,
    norm_attn,
    norm_ffn,
    cotangent,
):
    d = tokens.shape[2]
    quarter = d // 4
    n = lax.axis_size("dp")
    own_quarter = lax.rem(lax.axis_index("dp"), 4)
    plain = jnp.arange(4, dtype=jnp.int32)
    y_first = own_quarter ^ plain
    x_first = own_quarter ^ ((plain & 1) * 2 + (plain >> 1))
    scalars = [lax.axis_index("mp").astype(jnp.int32)[None], segment_ids, keep_mask]
    groups = [[4 * i + j for j in range(4)] for i in range(n // 4)]

    def scatter(grads):
        return lax.psum_scatter(grads, "dp", scatter_dimension=0, axis_index_groups=groups)[None]

    def gather(flow):
        return lax.all_gather(flow.mine[0], "dp", axis=0, axis_index_groups=groups)

    place = lax.axis_index("dp") // 4
    z = jnp.stack([lax.rem(place, 2), lax.rem(place // 2, 2)]).astype(jnp.int32)

    chain = Chain()
    own, ct_own = tokens[:, 0], cotangent[:, 0]
    gain_attn, gain_ffn = norm_attn[None], norm_ffn[None]
    other, ct_other = swap(own), swap(ct_own)
    first = project(chain, own, gain_attn, w_query, w_key, w_value, 0)
    qkv, normed = project(chain, other, gain_attn, w_query, w_key, w_value, 1, first)
    mixed, lse, attn_part = attend(chain, scalars, qkv, w_out, ct_other)

    w0, w1 = FFN_CHUNKS
    chunk = lambda begin, at, width: ffn(chain, plain, begin, ct_own, ct_other, w_gate, w_up, w_down, at, width, 1)
    act0, both0, grads, hidden, x = chunk([gain_ffn, own, other, swap(attn_part), attn_part], 0, w0)
    flow0 = Flow([scatter(grads)])
    act1, both1, grads = chunk([x], w0, w1)
    flow1 = Flow([scatter(grads)], split=True)
    back_part = ffn_input_grad(chain, [both0, both1], w_gate, w_up)
    back_theirs = swap(back_part)
    tick(chain, z, flow0)
    grad_in, grad_hidden, gain_ffn_part = middle_back(
        chain, back_part, back_theirs, hidden, ct_own, ct_other, gain_ffn
    )
    grad_mixed = out_back(chain, grad_in, w_out)
    tick(chain, z, flow0)
    back = lambda order, pair, *more: attend_back(
        chain, scalars, order, qkv, mixed, grad_mixed, lse, normed, pair, *more
    )
    pair0 = back(x_first, 0)
    *pair1, kept, sent = back(x_first, 1, pair0, grad_in)
    flow3 = Flow([kept, sent], (1, 2))
    pair2 = back(x_first, 2)
    tick(chain, z, flow0, flow1)
    finish(chain, z, flow0)
    gathered0 = gather(flow0)
    pair3 = back(x_first, 3)
    tick(chain, z, flow1)
    back_own, back_send, gain_parts, kept, sent = qkv_back(
        chain,
        x_first,
        list(zip(pair0, pair1, pair2, pair3)),
        [w_query, w_key, w_value],
        normed,
        own,
        other,
        gain_ffn_part,
    )
    flow4 = Flow([kept, sent], (1, 2))
    tick(chain, z, flow1)
    gains = Total(gain_parts)
    out_own, out_send = ffn_output(chain, [act0, act1], w_down)
    tick(chain, z, flow1, flow3, gains)
    tick(chain, z, flow1, flow3, flow4, gains)
    finish(chain, z, flow1)
    gathered1 = gather(flow1)
    grad_tokens = last(chain, back_own, swap(back_send), own, grad_hidden, gain_attn)
    tick(chain, z, flow3, flow4, gains)
    result = add_output(chain, hidden, out_own, swap(out_send))

    hidden_units, width = w_gate.shape[1], w_query.shape[1]
    wide_shapes = [(d, hidden_units), (d, hidden_units), (hidden_units, d)]

    def ffn_moves(at, count):
        return [
            (0, 0, count, count, across(quarter, at, count)),
            (1, count, count, count, across(quarter, at, count)),
            (2, 2 * count, count, 128, along(quarter, at, count)),
        ]

    wide = unpack(chain, plain, [gathered0], ffn_moves(0, w0), [None] * 3, wide_shapes)
    tick(chain, z, flow3, flow4, gains)
    finish(chain, z, flow3)
    flow3.spread()
    tick(chain, z, flow4, gains)
    finish(chain, z, flow4, gains)
    flow4.spread()
    count = 2 * 128
    moves = lambda h: [(k, k * count, count, count, across(quarter, h * count, count)) for k in range(3)]
    wide = unpack(chain, plain, [gathered1], ffn_moves(w0, w1), wide, wide_shapes)
    *narrow, grad_out = unpack(
        chain,
        y_first,
        flow3.pieces,
        moves(0) + [(3, 3 * count, width, quarter, along(quarter, 0, width))],
        [None] * 4,
        [(d, width)] * 3 + [(width, d)],
    )
    narrow = unpack(chain, y_first, flow4.pieces, moves(1), narrow, [(d, width)] * 3)
    return (
        result[:, None],
        grad_tokens[:, None],
        *narrow,
        grad_out,
        *wide,
        gains.mine[0],
        gains.mine[1],
    )


def solution(mesh):
    return jax.shard_map(
        shards,
        mesh=mesh,
        in_specs=(
            P("mp", "dp", None),
            P("dp", None),
            P("dp", None),
            P(None, "mp"),
            P(None, "mp"),
            P(None, "mp"),
            P("mp", None),
            P(None, "mp"),
            P(None, "mp"),
            P("mp", None),
            P(),
            P(),
            P("mp", "dp", None),
        ),
        out_specs=(
            P("mp", "dp", None),
            P("mp", "dp", None),
            P(None, "mp"),
            P(None, "mp"),
            P(None, "mp"),
            P("mp", None),
            P(None, "mp"),
            P(None, "mp"),
            P("mp", None),
            P(),
            P(),
        ),
        check_vma=False,
    )
```

```python
import functools

import jax
import jax.numpy as jnp
from jax import lax
from jax.experimental import pallas as pl
from jax.experimental.pallas import tpu as pltpu
from jax.sharding import PartitionSpec as P

HDIM = 64
EPSILON = 1e-06
LOG2E = 1.4426950408889634
VMEM_LIMIT = 62 * 1024 * 1024
COST = 1e6
BF = jnp.bfloat16
F32 = jnp.float32
NN = ((1,), (0,))
NT = ((1,), (1,))
TN = ((0,), (0,))
FFN_CHUNKS = (512, 896)


def dot(left, right, dims=NN):
    return lax.dot_general(left, right, (dims, ((), ())), preferred_element_type=F32)


def shape(dims, dtype):
    return jax.ShapeDtypeStruct(dims, dtype)


class Chain:
    def __init__(self):
        self.token = None

    def run(self, kernel, grid, in_specs, out_specs, out_shape, args, prefetch=(), scratch=(), alias=None, us=5):
        before = [] if self.token is None else [self.token]
        some, n_in, n_out = len(prefetch), len(args), len(out_shape)
        skip = len(before)

        def body(*refs):
            kept = refs[: some + n_in] + refs[some + n_in + skip : some + n_in + skip + n_out]
            kernel(*kept, *refs[some + n_in + skip + n_out + 1 :])

        anywhere = pl.BlockSpec(memory_space=pl.ANY)
        *outs, self.token = pl.pallas_call(
            body,
            grid_spec=pltpu.PrefetchScalarGridSpec(
                num_scalar_prefetch=some,
                grid=grid,
                in_specs=list(in_specs) + [anywhere] * skip,
                out_specs=list(out_specs) + [anywhere],
                scratch_shapes=list(scratch),
            ),
            out_shape=list(out_shape) + [shape((8, 128), F32)],
            input_output_aliases=alias or {},
            compiler_params=pltpu.CompilerParams(vmem_limit_bytes=VMEM_LIMIT),
            cost_estimate=pl.CostEstimate(flops=int(us * COST), bytes_accessed=1, transcendentals=0),
        )(*prefetch, *args, *before)
        return outs


ANYWHERE = pl.BlockSpec(memory_space=pl.ANY)


def block(dims, index):
    return pl.BlockSpec(dims, index)


class Copies:
    def __init__(self, sems):
        self.sems, self.started = sems, []

    def start(self, source, target):
        copy = pltpu.make_async_copy(source, target, self.sems.at[len(self.started)])
        copy.start()
        self.started.append(copy)
        return copy


def by_hand(chain, kernel, inputs, outputs, scratch, copies, prefetch=(), alias=None, us=5):
    def body(*refs):
        kernel(*refs[:-1], Copies(refs[-1]))

    return chain.run(
        body,
        (1,),
        [ANYWHERE] * len(inputs),
        [ANYWHERE] * len(outputs),
        outputs,
        inputs,
        prefetch=prefetch,
        scratch=list(scratch) + [pltpu.SemaphoreType.DMA((copies,))],
        alias=alias,
        us=us,
    )


def project(chain, tokens, gain, wq, wk, wv, half, before=()):
    rows, d = tokens.shape
    width = wq.shape[1]
    weights = [wq, wk, wv]

    def kernel(tokens, gain, *refs):
        ws, refs = refs[:3], refs[3 + len(before) :]
        projected, normed, xs, gs, held, out, low, copies = refs
        first = [copies.start(gain, gs), copies.start(tokens, xs)]
        loads = [copies.start(w, held.at[i]) for i, w in enumerate(ws)]
        for c in first:
            c.wait()
        x = xs[...].astype(F32)
        r = lax.rsqrt(jnp.mean(x * x, axis=-1, keepdims=True) + EPSILON)
        low[...] = (x * r * gs[...]).astype(BF)
        here = pl.ds(half * rows, rows)
        stores = [copies.start(low, normed.at[here])]
        for i in range(3):
            loads[i].wait()
            out[i] = dot(low[...], held[i]).astype(BF)
            stores.append(copies.start(out.at[i], projected.at[here, pl.ds(i * width, width)]))
        for c in stores:
            c.wait()

    return by_hand(
        chain,
        kernel,
        [tokens, gain, *weights, *before],
        [shape((2 * rows, 3 * width), BF), shape((2 * rows, d), BF)],
        [
            pltpu.VMEM((rows, d), BF),
            pltpu.VMEM((1, d), F32),
            pltpu.VMEM((3, d, width), BF),
            pltpu.VMEM((3, rows, width), BF),
            pltpu.VMEM((rows, d), BF),
        ],
        9,
        alias={5: 0, 6: 1} if before else None,
    )


def layout(place, segs, keep, slot):
    last, mid = 4 * slot - 1, 2 * slot
    leads = jnp.logical_or(segs[0, 0] != segs[0, mid], keep[0, 0] == 0)
    start = jnp.where(leads, 1, 0) + 2 * place[0]
    padded = jnp.where(jnp.where(leads, keep[0, 0], keep[0, last]) == 0, 1, 0)
    return (lambda logical: pl.ds(pl.multiple_of(lax.rem(logical + start, 4) * slot, slot), slot)), padded


def two_heads(columns):
    slot = columns.shape[1]
    zero = jnp.zeros((HDIM, slot), BF)
    first = jnp.concatenate([columns[:HDIM], zero], 0)
    second = jnp.concatenate([zero, columns[HDIM:]], 0)
    return jnp.concatenate([first, second], 1)


def attend(chain, scalars, qkv, w_out, early):
    seq, width = qkv.shape[0], qkv.shape[1] // 3
    d = w_out.shape[1]
    pairs, slot, half = width // 128, seq // 4, seq // 2
    scale = HDIM**-0.5 * LOG2E

    def kernel(place, segs, keep, q_ref, k_ref, v_ref, w_all, early, o_ref, lse_ref, part, mixed, ws, out, sems):
        step = pl.program_id(0)
        rows, padded = layout(place, segs, keep, slot)
        load = pltpu.make_async_copy(w_all, ws, sems.at[0])

        @pl.when(step == 0)
        def _():
            load.start()

        one = jnp.ones((16, slot), BF)
        slots = [[j if at < 3 else jnp.where(padded > 0, j, 3) for j in range(3)] for at in range(4)]

        def scores_of(at):
            q2 = two_heads(q_ref[rows(at), :].T)
            return [dot(k_ref[rows(j), :], q2) for j in slots[at]]

        coming = scores_of(0)
        for at in range(4):
            scores = coming
            if at < 3:
                coming = scores_of(at + 1)
            top = functools.reduce(jnp.maximum, [jnp.max(s, axis=0, keepdims=True) for s in scores])
            oa = jnp.zeros((HDIM + 16, slot), F32)
            ob = oa
            for j, s in zip(slots[at], scores):
                p = jnp.exp2((s - top) * scale).astype(BF)
                vt = v_ref[rows(j), :].T
                oa += dot(jnp.concatenate([vt[:HDIM], one], 0), p[:, :slot])
                ob += dot(jnp.concatenate([vt[HDIM:], one], 0), p[:, slot:])
            la, lb = oa[HDIM : HDIM + 1], ob[HDIM : HDIM + 1]
            o = jnp.concatenate([oa[:HDIM] / la, ob[:HDIM] / lb], 0).astype(BF).T
            o_ref[rows(at), :] = o
            mixed[step, rows(at), :] = o
            lse = top * HDIM**-0.5 + jnp.log(jnp.concatenate([la, lb], 1))
            lse_ref[0, 0:1, rows(at)] = lse[:, :slot]
            lse_ref[0, 1:2, rows(at)] = lse[:, slot:]

        @pl.when(step == pairs - 1)
        def _():
            load.wait()
            stores = []
            for k in range(2):
                here = slice(k * half, (k + 1) * half)
                every = jnp.concatenate([mixed[p, here, :] for p in range(pairs)], 1)
                out[here] = dot(every, ws[...]).astype(BF)
                stores.append(pltpu.make_async_copy(out.at[here], part.at[here], sems.at[1 + k]))
                stores[-1].start()
            for c in stores:
                c.wait()

    column = lambda off: block((seq, 128), lambda p, *m: (0, p + off))
    return chain.run(
        kernel,
        (pairs,),
        [column(0), column(pairs), column(2 * pairs), ANYWHERE, ANYWHERE],
        [column(0), block((1, 2, seq), lambda p, *m: (p, 0, 0)), ANYWHERE],
        [shape((seq, width), BF), shape((pairs, 2, seq), F32), shape((seq, d), BF)],
        [qkv, qkv, qkv, w_out, early],
        prefetch=scalars,
        scratch=[
            pltpu.VMEM((pairs, seq, 128), BF),
            pltpu.VMEM((width, d), BF),
            pltpu.VMEM((seq, d), BF),
            pltpu.SemaphoreType.DMA((3,)),
        ],
        us=26,
    )


def attend_back(chain, scalars, order, qkv, mixed, grad_mixed, lse, normed, first, before=None, g=None):
    seq, width = qkv.shape[0], qkv.shape[1] // 3
    d = normed.shape[1]
    pairs, slot, quarter = width // 128, seq // 4, d // 4
    scale = HDIM**-0.5 * LOG2E

    def kernel(
        place, segs, keep, order, q_ref, k_ref, v_ref, o_ref, do_ref, lse_ref, *refs
    ):
        rows, padded = layout(place, segs, keep, slot)
        if before is None:
            dq_ref, dk_ref, dv_ref, dk_sum, dv_sum = refs
        else:
            normed_all, g_all, mixed_all, *old = refs[:6]
            dq_ref, dk_ref, dv_ref, kept, sent, dk_sum, dv_sum, every, ns, held, gs, ms, sems = refs[6:]
            copies = Copies(sems)
            loads = [copies.start(normed_all, ns), copies.start(g_all, gs), copies.start(mixed_all, ms)]
            loads += [copies.start(o, every.at[i]) for i, o in enumerate(old)]

        def stacked(x):
            lane = lax.broadcasted_iota(jnp.int32, (slot, 128), 1)
            zero = jnp.zeros_like(x)
            return jnp.concatenate([jnp.where(lane < HDIM, x, zero), jnp.where(lane < HDIM, zero, x)], 0)

        def extended(columns, tail):
            high = tail.astype(BF).astype(F32)
            rest = tail - high
            middle = rest.astype(BF).astype(F32)
            extra = jnp.concatenate([high, middle, rest - middle, jnp.zeros((125, 2 * slot), F32)], 0).astype(BF)
            return jnp.concatenate([two_heads(columns), extra], 0)

        def one_slot(at, slots):
            ones = jnp.ones((slot, 128), BF)
            q, do = q_ref[rows(at), :], do_ref[rows(at), :]
            do_t = do.T
            prod = do_t.astype(F32) * o_ref[rows(at), :].T.astype(F32)
            delta = jnp.concatenate(
                [jnp.sum(prod[:HDIM], 0, keepdims=True), jnp.sum(prod[HDIM:], 0, keepdims=True)], 1
            )
            lse = jnp.concatenate([lse_ref[0, 0:1, rows(at)], lse_ref[0, 1:2, rows(at)]], 1)
            q2 = extended(q.T, lse * -(HDIM**0.5))
            do2 = extended(do_t, -delta)
            qs, dos = stacked(q), stacked(do)
            dqa = jnp.zeros((HDIM, slot), F32)
            dqb = dqa
            for j in slots:
                k, v = k_ref[rows(j), :], v_ref[rows(j), :]
                p = jnp.exp2(dot(jnp.concatenate([k, ones], 1), q2) * scale)
                dp = dot(jnp.concatenate([v, ones], 1), do2)
                ds = (p * dp).astype(BF)
                dv_sum[rows(j), :] += dot(p.astype(BF), dos)
                dk_sum[rows(j), :] += dot(ds, qs)
                kt = k.T
                dqa += dot(kt[:HDIM], ds[:, :slot])
                dqb += dot(kt[HDIM:], ds[:, slot:])
            dq_ref[rows(at), :] = (jnp.concatenate([dqa, dqb], 0) * HDIM**-0.5).astype(BF).T

        dk_sum[...] = jnp.zeros_like(dk_sum)
        dv_sum[...] = jnp.zeros_like(dv_sum)

        def body(at, carry):
            alone = jnp.logical_and(at == 3, padded == 0)
            one_slot(at, [jnp.where(alone, 3, j) for j in range(3)])
            return carry

        lax.fori_loop(0, 4, body, 0)
        dk = (dk_sum[...] * HDIM**-0.5).astype(BF)
        dv = dv_sum[...].astype(BF)
        dk_ref[...] = dk
        dv_ref[...] = dv
        if before is not None:
            for c in loads:
                c.wait()
            right = jnp.concatenate([every[0], dq_ref[...], every[1], dk, every[2], dv], 1)
            stores = []
            for k in range(4):
                held[k, :, :wide] = dot(column_block(ns, order[k], quarter), right, TN).astype(BF)
                part = dot(ms[...], column_block(gs, order[k], quarter), TN).astype(BF)
                for i in range(width // quarter):
                    held[k, :, wide + i * quarter : wide + (i + 1) * quarter] = part[i * quarter : (i + 1) * quarter]
                stores.append(copies.start(held.at[k], quarters_of([kept, sent])[k]))
            for c in stores:
                c.wait()

    column = lambda off: block((seq, 128), lambda p, *m: (0, off))
    wide = 3 * 2 * 128
    more = before is not None
    return chain.run(
        kernel,
        (1,),
        [
            column(first),
            column(first + pairs),
            column(first + 2 * pairs),
            column(first),
            column(first),
            block((1, 2, seq), lambda p, *m: (first, 0, 0)),
        ]
        + [ANYWHERE] * (6 * more),
        [column(0)] * 3 + [ANYWHERE] * (2 * more),
        [shape((seq, 128), BF)] * 3 + quarter_shapes(2 * more, quarter, wide + width),
        [qkv, qkv, qkv, mixed, grad_mixed, lse] + ([normed, g, mixed, *before] if more else []),
        prefetch=scalars + [order],
        scratch=[pltpu.VMEM((seq, 128), F32)] * 2
        + [
            pltpu.VMEM((3, seq, 128), BF),
            pltpu.VMEM((seq, d), BF),
            pltpu.VMEM((4, quarter, wide + width), BF),
            pltpu.VMEM((seq, d), BF),
            pltpu.VMEM((seq, width), BF),
            pltpu.SemaphoreType.DMA((10,)),
        ]
        * more,
        us=13,
    )


def gelu_parts(v):
    c = 0.7978845608028654
    square = v * v
    share = 0.5 + 0.5 * jnp.tanh(v * (c + (c * 0.044715) * square))
    value = v * share
    return value, share + value * (1.0 - share) * (2 * c + (6 * c * 0.044715) * square)


def column_block(ref, number, width):
    if isinstance(number, int):
        return ref[:, number * width : (number + 1) * width]
    return ref[:, pl.ds(pl.multiple_of(number * width, width), width)]


def quarters_of(outs):
    each = 4 // len(outs)
    return [outs[k // each].at[k % each] for k in range(4)]


def quarter_shapes(pieces, rows, width):
    return [shape((4 // pieces, rows, width), BF)] * pieces if pieces else []


def weight_quarters(copies, order, xs, cs, acts, boths, held, targets, quarter, beside=None):
    width = acts.shape[1]
    stores = []
    for k in range(4):
        sides = dot(column_block(xs, order[k], quarter), boths[...], TN)
        down = dot(acts[...], column_block(cs, order[k], quarter), TN).astype(BF)
        held[k, :, : 2 * width] = sides.astype(BF)
        for i in range(width // 128):
            rows = down[i * 128 : (i + 1) * 128]
            place = slice(2 * width + i * 128, 2 * width + (i + 1) * 128)
            held[k, :128, place] = rows[:, :128]
            held[k, 128:, place] = rows[:, 128:]
        if beside is not None:
            beside(k)
        stores.append(copies.start(held.at[k], targets[k]))
    return stores


def ffn(chain, begin, ct_own, ct_other, w_gate, w_up, w_down, at, width, finish):
    seq, d = begin[-1].shape
    half, quarter = seq // 2, d // 4
    early = len(begin) > 1

    order = range(4)

    def kernel(*refs):
        before, (ct_own, ct_other, wg_all, wu_all, wd_all, act, both, *refs) = refs[: len(begin)], refs[len(begin) :]
        grads, refs = refs[:finish], refs[finish:]
        if early:
            (hidden, x), refs = refs[:2], refs[2:]
            *refs, ts, ms, others, gs, hs, copies = refs
        else:
            *refs, copies = refs
        xs, cs, wg, wu, wd, acts, boths, *held = refs
        halves = [slice(0, half), slice(half, seq)]
        stores = []
        if early:
            gain_in, own, other, theirs, mine = before
            tokens = [own, other]
            gain_load = copies.start(gain_in, gs)

            def load(k):
                return [
                    copies.start(tokens[k], ts.at[k]),
                    copies.start(mine.at[halves[k]], ms.at[halves[k]]),
                    copies.start(theirs.at[halves[1 - k]], others.at[halves[1 - k]]),
                ]

            def normed(k, loads):
                for c in loads + [gain_load] * (k == 0):
                    c.wait()
                here = halves[k]
                h = ts[k].astype(F32) + (ms[here].astype(F32) + others[halves[1 - k]].astype(F32))
                r = lax.rsqrt(jnp.mean(h * h, axis=-1, keepdims=True) + EPSILON)
                hs[here] = h
                xs[here] = (h * r * gs[...]).astype(BF)
                stores.append(copies.start(hs.at[here], hidden.at[here]))
                stores.append(copies.start(xs.at[here], x.at[here]))

        else:

            def load(k):
                return [copies.start(before[0].at[halves[k]], xs.at[halves[k]])]

            def normed(k, loads):
                for c in loads:
                    c.wait()

        x0 = load(0)
        units = pl.ds(at, width)
        lg = copies.start(wg_all.at[:, units], wg)
        lu = copies.start(wu_all.at[:, units], wu)
        c0 = copies.start(ct_own, cs.at[halves[0]])
        ld = copies.start(wd_all.at[units, :], wd)
        x1 = load(1)
        c1 = copies.start(ct_other, cs.at[halves[1]])
        waits = [[lg], [lu], [c0, ld]], [[], [], [c1]]
        normed(0, x0)
        for here, (for_gate, for_up, for_act) in zip(halves, waits):
            for c in for_gate:
                c.wait()
            gate = dot(xs[here], wg[...])
            for c in for_up:
                c.wait()
            up = dot(xs[here], wu[...])
            for c in for_act:
                c.wait()
            if here.start == 0:
                normed(1, x1)
            grad_act = dot(cs[here], wd[...], NT)
            value, slope = gelu_parts(gate)
            acts[here] = (value * up).astype(BF)
            boths[here, :width] = (grad_act * up * slope).astype(BF)
            boths[here, width:] = (grad_act * value).astype(BF)
            stores.append(copies.start(acts.at[here], act.at[here]))
            stores.append(copies.start(boths.at[here], both.at[here]))
        if finish:
            targets = quarters_of(grads)
            stores += weight_quarters(copies, order, xs, cs, acts, boths, held[0], targets, quarter)
        for c in stores:
            c.wait()

    return by_hand(
        chain,
        kernel,
        [*begin, ct_own, ct_other, w_gate, w_up, w_down],
        [shape((seq, width), BF), shape((seq, 2 * width), BF)]
        + quarter_shapes(finish, quarter, 3 * width)
        + [shape((seq, d), F32), shape((seq, d), BF)] * early,
        [
            pltpu.VMEM((seq, d), BF),
            pltpu.VMEM((seq, d), BF),
            pltpu.VMEM((d, width), BF),
            pltpu.VMEM((d, width), BF),
            pltpu.VMEM((width, d), BF),
            pltpu.VMEM((seq, width), BF),
            pltpu.VMEM((seq, 2 * width), BF),
        ]
        + [pltpu.VMEM((4, quarter, 3 * width), BF)] * min(finish, 1)
        + [
            pltpu.VMEM((2, half, d), BF),
            pltpu.VMEM((seq, d), BF),
            pltpu.VMEM((seq, d), BF),
            pltpu.VMEM((1, d), F32),
            pltpu.VMEM((seq, d), F32),
        ]
        * early,
        15 + 9 * early,
        us=16 if finish else 8,
    )


def ffn_input_grad(chain, boths, wg, wu):
    seq = boths[0].shape[0]
    d, units = wg.shape
    half, chunks = seq // 2, len(boths)
    starts = [sum(b.shape[1] for b in boths[:k]) // 2 for k in range(chunks + 1)]

    def kernel(*refs):
        ins, (wg, wu, back, *held, wgs, wus, out, copies) = refs[:chunks], refs[chunks:]
        loads = []
        for k in range(chunks):
            units = pl.ds(starts[k], starts[k + 1] - starts[k])
            loads.append(
                [
                    copies.start(ins[k].at[pl.ds(0, half)], held[k].at[pl.ds(0, half)]),
                    copies.start(wg.at[:, units], wgs.at[:, units]),
                    copies.start(wu.at[:, units], wus.at[:, units]),
                ]
            )
        later = [copies.start(ins[k].at[pl.ds(half, half)], held[k].at[pl.ds(half, half)]) for k in range(chunks)]
        stores = []
        for h in range(2):
            here = slice(h * half, (h + 1) * half)
            total = None
            for k in range(chunks):
                for c in loads[k] if h == 0 else [later[k]]:
                    c.wait()
                width = starts[k + 1] - starts[k]
                units = slice(starts[k], starts[k + 1])
                part = dot(held[k][here, :width], wgs[:, units], NT) + dot(held[k][here, width:], wus[:, units], NT)
                total = part if total is None else total + part
            out[here] = total.astype(BF)
            stores.append(copies.start(out.at[here], back.at[here]))
        for c in stores:
            c.wait()

    return by_hand(
        chain,
        kernel,
        boths + [wg, wu],
        [shape((seq, d), BF)],
        [pltpu.VMEM(b.shape, BF) for b in boths]
        + [pltpu.VMEM((d, units), BF), pltpu.VMEM((d, units), BF), pltpu.VMEM((seq, d), BF)],
        4 * chunks + 2,
        us=13,
    )[0]


def ffn_output(chain, acts, wd):
    seq, d = acts[0].shape[0], wd.shape[1]
    half, chunks = seq // 2, len(acts)
    starts = [sum(a.shape[1] for a in acts[:k]) for k in range(chunks + 1)]

    def kernel(*refs):
        ins, (wd, own, send, *held, wds, out_own, out_send, copies) = refs[:chunks], refs[chunks:]
        first, second = pl.ds(half, half), pl.ds(0, half)
        loads = []
        for k in range(chunks):
            units = pl.ds(starts[k], starts[k + 1] - starts[k])
            loads.append([copies.start(ins[k].at[first], held[k].at[first]), copies.start(wd.at[units], wds.at[units])])
        later = [copies.start(ins[k].at[second], held[k].at[second]) for k in range(chunks)]
        stores = []
        for h, (here, target, out) in enumerate([(first, out_send, send), (second, out_own, own)]):
            total = None
            for k in range(chunks):
                for c in loads[k] if h == 0 else [later[k]]:
                    c.wait()
                part = dot(held[k][here], wds[starts[k] : starts[k + 1]])
                total = part if total is None else total + part
            target[...] = total.astype(target.dtype)
            stores.append(copies.start(target, out))
        for c in stores:
            c.wait()

    return by_hand(
        chain,
        kernel,
        acts + [wd],
        [shape((half, d), F32), shape((half, d), BF)],
        [pltpu.VMEM(a.shape, BF) for a in acts]
        + [pltpu.VMEM(wd.shape, BF), pltpu.VMEM((half, d), F32), pltpu.VMEM((half, d), BF)],
        3 * chunks + 2,
        us=7,
    )


def norm_back(value, gain, grad):
    r = lax.rsqrt(jnp.mean(value * value, axis=-1, keepdims=True) + EPSILON)
    u = grad * gain
    inner = jnp.mean(u * value, axis=-1, keepdims=True)
    return r * u - value * (r * r * r * inner), jnp.sum(grad * value * r, axis=0, keepdims=True)


def add_up(at, total, part):
    @pl.when(at == 0)
    def _():
        total[...] = part

    @pl.when(at > 0)
    def _():
        total[...] += part


def middle_back(chain, mine, theirs, hidden, ct_own, ct_other, gain, tile=384):
    seq, d = hidden.shape
    n = seq // tile
    rows = lambda f: block((tile, d), lambda i: (f(i), 0))
    front = rows(lambda i: jnp.minimum(i, n // 2 - 1))

    def kernel(mine, theirs, hidden, ct_own, ct_other, gain, low, keep, gain_grad):
        at = pl.program_id(0)
        h = hidden[...]
        through, part = norm_back(h, gain[...], mine[...].astype(F32) + theirs[...].astype(F32))
        ct = jnp.where(at < n // 2, ct_own[...], ct_other[...])
        total = ct.astype(F32) + through
        low[...] = total.astype(BF)
        add_up(at, gain_grad, part)

        @pl.when(at < n // 2)
        def _():
            keep[...] = total

    return chain.run(
        kernel,
        (n,),
        [
            rows(lambda i: i),
            rows(lambda i: lax.rem(i + n // 2, n)),
            rows(lambda i: i),
            front,
            rows(lambda i: jnp.maximum(i - n // 2, 0)),
            block((1, d), lambda i: (0, 0)),
        ],
        [rows(lambda i: i), front, block((1, d), lambda i: (0, 0))],
        [shape((seq, d), BF), shape((seq // 2, d), F32), shape((1, d), F32)],
        [mine, theirs, hidden, ct_own, ct_other, gain],
        us=8,
    )


def add_output(chain, hidden, own, theirs, tile=384):
    rows, d = own.shape
    row = block((tile, d), lambda i: (i, 0))

    def kernel(hidden, own, theirs, result):
        result[...] = (hidden[...] + (own[...] + theirs[...].astype(F32))).astype(BF)

    return chain.run(kernel, (rows // tile,), [row] * 3, [row], [shape((rows, d), BF)], [hidden, own, theirs], us=4)[0]


def out_back(chain, g, w_out):
    seq, d = g.shape
    width, half = w_out.shape[0], seq // 2

    def kernel(g, w_out, grad_mixed, gs, ws, out, copies):
        halves = [pl.ds(0, half), pl.ds(half, half)]
        loads = [[copies.start(g.at[halves[0]], gs.at[halves[0]]), copies.start(w_out, ws)]]
        loads.append([copies.start(g.at[halves[1]], gs.at[halves[1]])])
        stores = []
        for here, waits in zip(halves, loads):
            for c in waits:
                c.wait()
            out[here] = dot(gs[here], ws[...], NT).astype(BF)
            stores.append(copies.start(out.at[here], grad_mixed.at[here]))
        for c in stores:
            c.wait()

    return by_hand(
        chain,
        kernel,
        [g, w_out],
        [shape((seq, width), BF)],
        [pltpu.VMEM((seq, d), BF), pltpu.VMEM((width, d), BF), pltpu.VMEM((seq, width), BF)],
        5,
        us=8,
    )[0]


def qkv_back(chain, order, grads, weights, normed, own, other, gain_ffn_grad):
    flat = [g for kind in grads for g in kind]
    count = len(flat)
    pieces = len(grads[0])
    seq = flat[0].shape[0]
    d, width = weights[0].shape
    half, quarter = seq // 2, d // 4
    wide = 3 * sum(g.shape[1] for g in grads[0][-2:])

    def kernel(order, *refs):
        ins, ws, refs = refs[:count], refs[count : count + 3], refs[count + 3 :]
        normed, t_own, t_other, ffn_part, own, send, gains, kept, sent, *held = refs
        *held, wh, ts, ffn, sums, out_own, out_send, ns, out, copies = held
        first, second = pl.ds(half, half), pl.ds(0, half)
        loads = [[copies.start(ins[i].at[first], held[i].at[first])] for i in range(count)]
        for i in range(3):
            loads[i * pieces].append(copies.start(ws[i], wh.at[i]))
        later = [[copies.start(ins[i].at[second], held[i].at[second])] for i in range(count)]
        all_normed = copies.start(normed, ns)
        tokens = [copies.start(t_other, ts.at[1]), copies.start(t_own, ts.at[0]), copies.start(ffn_part, ffn)]
        stores = []
        gain = 0.0
        for k, (here, waits, target, goal) in enumerate([(first, loads, out_send, send), (second, later, out_own, own)]):
            total = 0.0
            for kind in range(3):
                some = range(kind * pieces, (kind + 1) * pieces)
                for i in some:
                    for c in waits[i]:
                        c.wait()
                left = jnp.concatenate([held[i][here] for i in some], 1)
                total += dot(left, wh[kind], NT)
            target[...] = total.astype(target.dtype)
            stores.append(copies.start(target, goal))
            tokens[k].wait()
            x = ts[1 - k].astype(F32)
            r = lax.rsqrt(jnp.mean(x * x, axis=-1, keepdims=True) + EPSILON)
            gain += jnp.sum(total * (x * r), axis=0, keepdims=True)
        all_normed.wait()
        right = jnp.concatenate([held[kind * pieces + p][...] for kind in range(3) for p in (pieces - 2, pieces - 1)], 1)
        for k in range(4):
            out[k] = dot(column_block(ns, order[k], quarter), right, TN).astype(BF)
            stores.append(copies.start(out.at[k], quarters_of([kept, sent])[k]))
        tokens[2].wait()
        sums[0:1] = gain
        sums[1:2] = 0.5 * ffn[...]
        stores.append(copies.start(sums, gains))
        for c in stores:
            c.wait()

    return by_hand(
        chain,
        kernel,
        flat + list(weights) + [normed, own, other, gain_ffn_grad],
        [shape((half, d), F32), shape((half, d), BF), shape((2, d), F32)] + quarter_shapes(2, quarter, wide),
        [pltpu.VMEM(g.shape, BF) for g in flat]
        + [
            pltpu.VMEM((3, d, width), BF),
            pltpu.VMEM((2, half, d), BF),
            pltpu.VMEM((1, d), F32),
            pltpu.VMEM((2, d), F32),
            pltpu.VMEM((half, d), F32),
            pltpu.VMEM((half, d), BF),
            pltpu.VMEM((seq, d), BF),
            pltpu.VMEM((4, quarter, wide), BF),
        ],
        2 * count + 14,
        prefetch=[order],
        us=8,
    )


def last(chain, mine, theirs, tokens, grad_hidden, gain, tile=384):
    rows, d = tokens.shape
    row = block((tile, d), lambda i: (i, 0))

    def kernel(mine, theirs, tokens, grad_hidden, gain, out):
        grad = mine[...] + theirs[...].astype(F32)
        out[...] = (grad_hidden[...] + norm_back(tokens[...].astype(F32), gain[...], grad)[0]).astype(BF)

    return chain.run(
        kernel,
        (rows // tile,),
        [row] * 4 + [block((1, d), lambda i: (0, 0))],
        [row],
        [shape((rows, d), BF)],
        [mine, theirs, tokens, grad_hidden, gain],
        us=4,
    )[0]


def swap(x):
    return lax.ppermute(x, "mp", [(0, 1), (1, 0)])


def exchange(x, bit):
    return lax.ppermute(x, "dp", [(i, i ^ bit) for i in range(lax.axis_size("dp"))])


def add(terms, pieces=1):
    n, rows, width = terms[0].shape
    tile = rows // 2

    def body(at, z, ins, outs):
        for k, out in enumerate(outs):
            out[0] = sum(t[k].astype(F32) for t in ins).astype(BF)

    spec = block((n, tile, width), lambda i, z: (0, i, 0))
    out = block((1, tile, width), lambda i, z: (0, i, 0))
    return list(terms), [spec] * len(terms), [out] * n, [shape((1, rows, width), BF)] * n, body


def halve(terms, bit):
    _, rows, width = terms[0].shape
    tile = rows // 4

    def body(at, z, ins, outs):
        for k in range(2):
            outs[k][0] = sum(t[0].astype(F32) for t in ins[k::2]).astype(BF)

    mine = block((1, tile, width), lambda i, z: (0, 2 * z[bit] + i, 0))
    others = block((1, tile, width), lambda i, z: (0, 2 * (1 - z[bit]) + i, 0))
    out = block((1, tile, width), lambda i, z: (0, i, 0))
    return (
        [t for t in terms for _ in range(2)],
        [mine, others] * len(terms),
        [out] * 2,
        [shape((1, rows // 2, width), BF)] * 2,
        body,
    )


def join(mine, theirs, bit):
    _, rows, width = mine.shape

    def body(at, z, ins, outs):
        outs[0][0] = jnp.where(at == z[bit], ins[0][0], ins[1][0])

    spec = block((1, rows, width), lambda i, z: (0, 0, 0))
    out = block((1, rows, width), lambda i, z: (0, i, 0))
    return [mine, theirs], [spec] * 2, [out], [shape((1, 2 * rows, width), BF)], body


class Flow:
    def __init__(self, quarters, bits=(1, 2), split=False):
        rest = [1 << b for b in range(2, (lax.axis_size("dp") - 1).bit_length())]
        self.steps = self.walk(quarters, bits, rest, split)
        self.step = next(self.steps)

    def walk(self, quarters, bits, rest, split):
        if len(quarters) == 2:
            keep, send = quarters
            mine, send = yield add([keep, exchange(send, bits[0])])
            terms = [mine, exchange(send, bits[1])]
        else:
            terms = list(quarters)
        if split:
            for k in range(2):
                mine, send = yield halve(terms, k)
                terms = [mine, exchange(send, rest[k])]
            [mine] = yield add(terms)
            for bit in rest[2:]:
                [mine] = yield add([mine, exchange(mine, bit)])
            for k in (1, 0):
                [mine] = yield join(mine, exchange(mine, rest[k]), k)
        else:
            [mine] = yield add(terms)
            for bit in rest:
                [mine] = yield add([mine, exchange(mine, bit)])
        self.mine = mine
        yield None

    def spread(self):
        self.pieces = [self.mine] + [exchange(self.mine, 1 + k) for k in range(3)]


class Total:
    def __init__(self, part):
        self.steps = self.walk(part)
        self.step = next(self.steps)

    def walk(self, mine):
        def body(at, z, ins, outs):
            outs[0][...] = ins[0][...] + ins[1][...]

        spec = block(mine.shape, lambda i, z: (0, 0))
        theirs = swap(mine)
        for bit in [1 << b for b in range((lax.axis_size("dp") - 1).bit_length())] + [None]:
            [mine] = yield [mine, theirs], [spec] * 2, [spec], [shape(mine.shape, F32)], body
            if bit is not None:
                theirs = exchange(mine, bit)
        self.mine = mine
        yield None


def tick(chain, z, *flows):
    args, in_specs, out_specs, shapes = [], [], [], []
    for f in flows:
        args += f.step[0]
        in_specs += f.step[1]
        out_specs += f.step[2]
        shapes += f.step[3]

    def kernel(z, *refs):
        ins, outs = list(refs[: len(args)]), list(refs[len(args) :])
        for some, _, specs, _, body in steps:
            body(pl.program_id(0), z, ins[: len(some)], outs[: len(specs)])
            del ins[: len(some)], outs[: len(specs)]

    steps = [f.step for f in flows]
    outs = chain.run(kernel, (2,), in_specs, out_specs, shapes, args, prefetch=[z], us=2)
    for f in flows:
        count = len(f.step[2])
        f.step = f.steps.send(outs[:count])
        outs = outs[count:]


def finish(chain, z, *flows):
    while left := [f for f in flows if f.step is not None]:
        tick(chain, z, *left)


def unpack(chain, order, pieces, moves, outputs, shapes):
    kept = [o for o in outputs if o is not None]
    whole = len(pieces) == 1
    rows, width = pieces[0].shape[-2:]

    def kernel(order, *refs):
        pieces_in = refs[: len(pieces)]
        outs = refs[len(pieces) + len(kept) : len(pieces) + len(kept) + len(shapes)]
        *scratch, sems = refs[len(pieces) + len(kept) + len(shapes) :]
        copies = []
        for k in range(4):
            piece = pieces_in[0].at[k] if whole else pieces_in[k].at[0]
            for m, (goal, at, count, tile, place) in enumerate(moves):
                held = scratch[m]
                for i in range(count // tile):
                    columns = piece[:, at + i * tile : at + (i + 1) * tile].astype(F32)
                    if tile == count:
                        held[k] = columns
                    else:
                        for j in range(rows // tile):
                            held[k, i * tile : (i + 1) * tile, j * tile : (j + 1) * tile] = columns[
                                j * tile : (j + 1) * tile
                            ]
                copy = pltpu.make_async_copy(held.at[k], outs[goal].at[place(order[k])], sems.at[k, m])
                copy.start()
                copies.append(copy)
        for copy in copies:
            copy.wait()

    return chain.run(
        kernel,
        (1,),
        [block(p.shape, lambda i, q, n=p.ndim: (0,) * n) for p in pieces] + [ANYWHERE] * len(kept),
        [ANYWHERE] * len(shapes),
        [shape(s, F32) for s in shapes],
        list(pieces) + kept,
        prefetch=[order],
        scratch=[
            pltpu.VMEM((4, rows, count) if tile == count else (4, count, rows), F32) for _, _, count, tile, _ in moves
        ]
        + [pltpu.SemaphoreType.DMA((4, len(moves)))],
        alias={1 + len(pieces) + i: i for i in range(len(kept))},
        us=3,
    )


def across(rows, at, count):
    return lambda q: (pl.ds(pl.multiple_of(q * rows, rows), rows), pl.ds(at, count))


def along(rows, at, count):
    return lambda q: (pl.ds(at, count), pl.ds(pl.multiple_of(q * rows, rows), rows))


def shards(
    tokens,
    segment_ids,
    keep_mask,
    w_query,
    w_key,
    w_value,
    w_out,
    w_gate,
    w_up,
    w_down,
    norm_attn,
    norm_ffn,
    cotangent,
):
    d = tokens.shape[2]
    quarter = d // 4
    n = lax.axis_size("dp")
    own_quarter = lax.rem(lax.axis_index("dp"), 4)
    plain = jnp.arange(4, dtype=jnp.int32)
    y_first = own_quarter ^ plain
    x_first = own_quarter ^ ((plain & 1) * 2 + (plain >> 1))
    scalars = [lax.axis_index("mp").astype(jnp.int32)[None], segment_ids, keep_mask]
    groups = [[4 * i + j for j in range(4)] for i in range(n // 4)]

    def scatter(grads):
        return lax.psum_scatter(grads, "dp", scatter_dimension=0, axis_index_groups=groups)[None]

    def gather(flow):
        return lax.all_gather(flow.mine[0], "dp", axis=0, axis_index_groups=groups)

    place = lax.axis_index("dp") // 4
    z = jnp.stack([lax.rem(place, 2), lax.rem(place // 2, 2)]).astype(jnp.int32)

    chain = Chain()
    own, ct_own = tokens[:, 0], cotangent[:, 0]
    gain_attn, gain_ffn = norm_attn[None], norm_ffn[None]
    other, ct_other = swap(own), swap(ct_own)
    first = project(chain, own, gain_attn, w_query, w_key, w_value, 0)
    qkv, normed = project(chain, other, gain_attn, w_query, w_key, w_value, 1, first)
    mixed, lse, attn_part = attend(chain, scalars, qkv, w_out, ct_other)

    w0, w1 = FFN_CHUNKS
    chunk = lambda begin, at, width: ffn(chain, begin, ct_own, ct_other, w_gate, w_up, w_down, at, width, 1)
    act0, both0, grads, hidden, x = chunk([gain_ffn, own, other, swap(attn_part), attn_part], 0, w0)
    flow0 = Flow([scatter(grads)])
    act1, both1, grads = chunk([x], w0, w1)
    flow1 = Flow([scatter(grads)], split=True)
    back_part = ffn_input_grad(chain, [both0, both1], w_gate, w_up)
    back_theirs = swap(back_part)
    tick(chain, z, flow0)
    grad_in, grad_hidden, gain_ffn_part = middle_back(
        chain, back_part, back_theirs, hidden, ct_own, ct_other, gain_ffn
    )
    grad_mixed = out_back(chain, grad_in, w_out)
    tick(chain, z, flow0)
    back = lambda order, pair, *more: attend_back(
        chain, scalars, order, qkv, mixed, grad_mixed, lse, normed, pair, *more
    )
    pair0 = back(x_first, 0)
    *pair1, kept, sent = back(x_first, 1, pair0, grad_in)
    flow3 = Flow([kept, sent], (1, 2))
    pair2 = back(x_first, 2)
    tick(chain, z, flow0, flow1)
    finish(chain, z, flow0)
    gathered0 = gather(flow0)
    pair3 = back(x_first, 3)
    tick(chain, z, flow1)
    back_own, back_send, gain_parts, kept, sent = qkv_back(
        chain,
        x_first,
        list(zip(pair0, pair1, pair2, pair3)),
        [w_query, w_key, w_value],
        normed,
        own,
        other,
        gain_ffn_part,
    )
    flow4 = Flow([kept, sent], (1, 2))
    tick(chain, z, flow1)
    gains = Total(gain_parts)
    out_own, out_send = ffn_output(chain, [act0, act1], w_down)
    tick(chain, z, flow1, flow3, gains)
    tick(chain, z, flow1, flow3, flow4, gains)
    finish(chain, z, flow1)
    gathered1 = gather(flow1)
    grad_tokens = last(chain, back_own, swap(back_send), own, grad_hidden, gain_attn)
    tick(chain, z, flow3, flow4, gains)
    result = add_output(chain, hidden, out_own, swap(out_send))

    hidden_units, width = w_gate.shape[1], w_query.shape[1]
    wide_shapes = [(d, hidden_units), (d, hidden_units), (hidden_units, d)]

    def ffn_moves(at, count):
        return [
            (0, 0, count, count, across(quarter, at, count)),
            (1, count, count, count, across(quarter, at, count)),
            (2, 2 * count, count, 128, along(quarter, at, count)),
        ]

    wide = unpack(chain, plain, [gathered0], ffn_moves(0, w0), [None] * 3, wide_shapes)
    tick(chain, z, flow3, flow4, gains)
    finish(chain, z, flow3)
    flow3.spread()
    tick(chain, z, flow4, gains)
    finish(chain, z, flow4, gains)
    flow4.spread()
    count = 2 * 128
    moves = lambda h: [(k, k * count, count, count, across(quarter, h * count, count)) for k in range(3)]
    wide = unpack(chain, plain, [gathered1], ffn_moves(w0, w1), wide, wide_shapes)
    *narrow, grad_out = unpack(
        chain,
        y_first,
        flow3.pieces,
        moves(0) + [(3, 3 * count, width, quarter, along(quarter, 0, width))],
        [None] * 4,
        [(d, width)] * 3 + [(width, d)],
    )
    narrow = unpack(chain, y_first, flow4.pieces, moves(1), narrow, [(d, width)] * 3)
    return (
        result[:, None],
        grad_tokens[:, None],
        *narrow,
        grad_out,
        *wide,
        gains.mine[0],
        gains.mine[1],
    )


def solution(mesh):
    return jax.shard_map(
        shards,
        mesh=mesh,
        in_specs=(
            P("mp", "dp", None),
            P("dp", None),
            P("dp", None),
            P(None, "mp"),
            P(None, "mp"),
            P(None, "mp"),
            P("mp", None),
            P(None, "mp"),
            P(None, "mp"),
            P("mp", None),
            P(),
            P(),
            P("mp", "dp", None),
        ),
        out_specs=(
            P("mp", "dp", None),
            P("mp", "dp", None),
            P(None, "mp"),
            P(None, "mp"),
            P(None, "mp"),
            P("mp", None),
            P(None, "mp"),
            P(None, "mp"),
            P("mp", None),
            P(),
            P(),
        ),
        check_vma=False,
    )
```
